32 devices in a mesh: dp: 4 (over x, core), seq: 8 (over z, y).
Axes of the slice: x: 2, y: 2, z: 4, core: 2. Of those that a mesh axis runs over, the one named last changes fastest.
Arguments:
- tokens: bfloat16 [2, 4, 1024, 2048], P(None, 'dp', 'seq'), may hold values from -6 to 6
- segments: int32 [2, 4, 1024], P(None, 'dp'), may hold values from 0 to 3, as said below
- attn_gain: bfloat16 [2048], P(('dp', 'seq')), may hold values from 0.099609375 to 1.8984375
- query_weight: bfloat16 [2048, 2048], P(('dp', 'seq')), may hold values from -0.125 to 0.125
- key_weight: bfloat16 [2048, 1024], P(('dp', 'seq')), may hold values from -0.125 to 0.125
- value_weight: bfloat16 [2048, 1024], P(('dp', 'seq')), may hold values from -0.125 to 0.125
- out_weight: bfloat16 [2048, 2048], P(('dp', 'seq')), may hold values from -1 to 1
- ffn_gain: bfloat16 [2048], P(('dp', 'seq')), may hold values from 0.099609375 to 1.8984375
- gate_weight: bfloat16 [2048, 8192], P(('dp', 'seq')), may hold values from -0.125 to 0.125
- up_weight: bfloat16 [2048, 8192], P(('dp', 'seq')), may hold values from -0.125 to 0.125
- down_weight: bfloat16 [2048, 8192], P(('dp', 'seq')), may hold values from -0.0625 to 0.0625
- cotangent: bfloat16 [2, 4, 1024, 2048], P(None, 'dp', 'seq'), may hold values from -6 to 6
Outputs:
- output: bfloat16 [2, 4, 1024, 2048], P(None, 'dp', 'seq')
- input_grad: float32 [2, 4, 1024, 2048], P(None, 'dp', 'seq')
- attn_gain_grad: float32 [2048], P(('dp', 'seq'))
- query_grad: float32 [2048, 2048], P(('dp', 'seq'))
- key_grad: float32 [2048, 1024], P(('dp', 'seq'))
- value_grad: float32 [2048, 1024], P(('dp', 'seq'))
- proj_grad: float32 [2048, 2048], P(('dp', 'seq'))
- ffn_gain_grad: float32 [2048], P(('dp', 'seq'))
- gate_grad: float32 [2048, 8192], P(('dp', 'seq'))
- up_grad: float32 [2048, 8192], P(('dp', 'seq'))
- down_grad: float32 [2048, 8192], P(('dp', 'seq'))
The draws below stay inside these ranges and needn't reach their ends.
Inputs may be any that keep to these rules, and one draw needn't show every extreme that they name: `segments`: along each sequence the document number starts at 0 and never falls.
All inputs are finite; a program needn't handle non-finite values.
Results may differ from the reference program's by a relative error of at most 0.015.
Values may be sent and summed in bfloat16 or wider, within the bound.
A program may use at most 704 MiB of HBM per device.

```python
import jax
import jax.numpy as jnp
from jax import lax

D = 2048
HEADS = 8
KV_HEADS = 4
HEAD_DIM = 256
FF = 8192
MICRO = 2
WINDOW = 1024
PIECE = 128
LEN = 1024
SEQ_G = 1
SEQS = 4


def draw_segments(key, part):
    key = jax.random.fold_in(key, 7)
    key_spread, key_front, key_back, key_pick = jax.random.split(key, 4)
    spread_breaks = jax.random.randint(key_spread, (MICRO, SEQS, 3), 1, LEN)
    front_breaks = jax.random.randint(key_front, (MICRO, SEQS, 1), 1, PIECE)
    back_breaks = jax.random.randint(key_back, (MICRO, SEQS, 2), LEN - PIECE + 1, LEN)
    chosen = jnp.concatenate([front_breaks, back_breaks], -1)
    picked = jax.random.randint(key_pick, (MICRO, SEQS // SEQ_G, 1), 0, SEQ_G)
    is_chosen = (jnp.arange(SEQ_G, dtype=jnp.int32)[None, None, :] == picked).reshape(MICRO, SEQS, 1)
    breaks = jnp.where(is_chosen, chosen, spread_breaks)
    positions = jnp.arange(LEN, dtype=jnp.int32)
    return jnp.sum((positions[None, None, :, None] >= breaks[:, :, None, :]).astype(jnp.int32), -1).astype(jnp.int32)


def level_of(rng, dims, cuts, low, largest):
    loudness = 1.0
    for position, parts in cuts:
        steps = jax.random.uniform(jax.random.fold_in(jax.random.fold_in(rng, 6), position), (parts,), jnp.float32, low / len(cuts), largest / len(cuts))
        loudness = loudness * jnp.repeat(jnp.exp(steps), dims[position] // parts).reshape((-1,) + (1,) * (len(dims) - 1 - position))
    return loudness


def noise(rng, shape, width, most, cuts=(), kind=jnp.bfloat16):
    values = jax.random.normal(rng, shape, jnp.float32) * width
    if len(cuts) > 0:
        values = level_of(rng, shape, cuts, -0.22, 0.18) * values
    return jnp.clip(values, min=-most, max=most).astype(kind)


def setup_inputs(seed: int = 0) -> dict:
    streams_of = jax.random.split(jax.random.key(seed), 13)
    tokens = noise(streams_of[0], (MICRO, SEQS, LEN, D), 1.0, 6.0, ((1, 4), (2, 8)))
    segments = draw_segments(jax.random.fold_in(streams_of[12], 71), 0)
    attn_gain = jnp.clip(1.0 + 0.18 * jax.random.normal(streams_of[2], (D,), jnp.float32), 0.099609375, 1.8984375).astype(jnp.bfloat16)
    query_weight = noise(streams_of[3], (D, HEADS * HEAD_DIM), D ** -0.5, 0.125, ((0, 32),))
    key_weight = noise(streams_of[4], (D, KV_HEADS * HEAD_DIM), D ** -0.5, 0.125, ((0, 32),))
    value_weight = noise(streams_of[5], (D, KV_HEADS * HEAD_DIM), D ** -0.5, 0.125, ((0, 32),))
    out_weight = noise(streams_of[6], (HEADS * HEAD_DIM, D), (HEADS * HEAD_DIM // 64) ** -0.5, 1.0, ((0, 32),))
    ffn_gain = jnp.clip(1.0 + 0.18 * jax.random.normal(streams_of[7], (D,), jnp.float32), 0.099609375, 1.8984375).astype(jnp.bfloat16)
    gate_weight = noise(streams_of[8], (D, FF), D ** -0.5, 0.125, ((0, 32),))
    up_weight = noise(streams_of[9], (D, FF), D ** -0.5, 0.125, ((0, 32),))
    down_weight = noise(streams_of[10], (D, FF), FF ** -0.5, 0.0625, ((0, 32),))
    cotangent = noise(streams_of[11], (MICRO, SEQS, LEN, D), 1.0, 6.0, ((1, 4), (2, 8)))
    return {"tokens": tokens, "segments": segments, "attn_gain": attn_gain, "query_weight": query_weight, "key_weight": key_weight, "value_weight": value_weight, "out_weight": out_weight, "ffn_gain": ffn_gain, "gate_weight": gate_weight, "up_weight": up_weight, "down_weight": down_weight, "cotangent": cotangent}


NORM_EPS = 1e-06
ROPE_BASE = 1000042.0

@jax.custom_vjp
def low(v):
    return lax.optimization_barrier(v.astype(jnp.bfloat16)).astype(jnp.float32)

@jax.custom_vjp
def low_back(v):
    return v

def low_keep(v):
    return (low(v), None)

def low_pass(kept, grad):
    return (grad,)

def back_keep(v):
    return (v, None)

def back_low(kept, grad):
    return (low(grad),)
low.defvjp(low_keep, low_pass)
low_back.defvjp(back_keep, back_low)

def rms_norm(values, gain_vec):
    return values * lax.rsqrt(lax.optimization_barrier(jnp.mean(values * values, -1, keepdims=True)) + NORM_EPS) * gain_vec

def rope_tables(positions):
    inv_freq = 1.0 / ROPE_BASE ** (jnp.arange(0, HEAD_DIM, 2, dtype=jnp.float32) / HEAD_DIM)
    angles = positions.astype(jnp.float32)[:, None] * inv_freq[None, :]
    return (jnp.cos(angles), jnp.sin(angles))

def rotate(values, cosine, sine_table):
    half_dim = values.shape[-1] // 2
    front_half = values[..., :half_dim]
    back_half = values[..., half_dim:]
    return jnp.concatenate([front_half * cosine - back_half * sine_table, back_half * cosine + front_half * sine_table], -1)

def block_forward(inputs, segment_ids, weights):
    attn_gain, query_weight, key_weight, value_weight, out_weight, ffn_gain, gate_weight, up_weight, down_weight = weights
    highest = lax.Precision.HIGHEST
    seq_len = inputs.shape[0]
    group_size = HEADS // KV_HEADS
    positions = jnp.arange(seq_len, dtype=jnp.int32)
    cosine, sine_table = rope_tables(positions)
    cosine = cosine[:, None, :]
    sine_table = sine_table[:, None, :]
    normed = low(rms_norm(inputs, attn_gain))
    queries = low_back(jnp.dot(normed, query_weight, precision=highest)).reshape(seq_len, HEADS, HEAD_DIM)
    key_heads = low_back(jnp.dot(normed, key_weight, precision=highest)).reshape(seq_len, KV_HEADS, HEAD_DIM)
    value_heads = low(low_back(jnp.dot(normed, value_weight, precision=highest))).reshape(seq_len, KV_HEADS, HEAD_DIM)
    queries = low(rotate(queries, cosine, sine_table)).reshape(seq_len, KV_HEADS, group_size, HEAD_DIM)
    key_heads = low(rotate(key_heads, cosine, sine_table))
    score_scale = HEAD_DIM ** (-0.5)
    scores = low_back(jnp.einsum('qgjd,kgd->gjqk', queries, key_heads, precision=highest) * score_scale)
    allowed = (positions[None, :] <= positions[:, None]) & (positions[:, None] - positions[None, :] < WINDOW)
    allowed = allowed & (segment_ids[:, None] == segment_ids[None, :])
    masked = jnp.where(allowed, scores, -1e+30)
    row_max = lax.optimization_barrier(jnp.max(masked, -1, keepdims=True))
    exp_scores = jnp.exp(masked - row_max)
    prob_low = low(exp_scores / lax.optimization_barrier(jnp.sum(exp_scores, -1, keepdims=True)))
    mixed_heads = jnp.einsum('gjqk,kgd->qgjd', prob_low, value_heads, precision=highest).reshape(seq_len, HEADS * HEAD_DIM)
    mixed_heads = low(low_back(mixed_heads))
    hidden = inputs + low_back(jnp.dot(mixed_heads, out_weight, precision=highest))
    normed_two = low(rms_norm(hidden, ffn_gain))
    gate_act = low_back(jnp.dot(normed_two, gate_weight, precision=highest))
    up_act = low_back(jnp.dot(normed_two, up_weight, precision=highest))
    middle = low(jax.nn.silu(gate_act) * up_act)
    return hidden + low_back(jnp.dot(middle, down_weight.T, precision=highest))

def reference(tokens, segments, attn_gain, query_weight, key_weight, value_weight, out_weight, ffn_gain, gate_weight, up_weight, down_weight, cotangent):
    weights = tuple((weight_arg.astype(jnp.float32) for weight_arg in (attn_gain, query_weight, key_weight, value_weight, out_weight, ffn_gain, gate_weight, up_weight, down_weight)))
    seq_count = MICRO * SEQS
    full_shape = tokens.shape
    inputs = tokens.astype(jnp.float32).reshape(seq_count, LEN, D)
    segment_ids = segments.reshape(seq_count, LEN).astype(jnp.int32)
    checked = jax.checkpoint(block_forward)

    def forward(weight_set, layer_inputs):

        def scan_step(carried, seq_pair):
            return (carried, checked(seq_pair[0], seq_pair[1], weight_set))
        return lax.scan(scan_step, jnp.float32(0.0), (layer_inputs, segment_ids))[1]
    outputs, pullback = jax.vjp(forward, weights, inputs)
    weight_grads, input_grads = pullback(cotangent.astype(jnp.float32).reshape(seq_count, LEN, D))
    return (outputs.astype(jnp.bfloat16).reshape(full_shape), input_grads.reshape(full_shape), weight_grads[0], weight_grads[1], weight_grads[2], weight_grads[3], weight_grads[4], weight_grads[5], weight_grads[6], weight_grads[7], weight_grads[8])
```

```python
import functools

import jax
import jax.numpy as jnp
from jax import lax
from jax.experimental import pallas as pl
from jax.experimental.pallas import tpu as pltpu
from jax.sharding import Mesh
from jax.sharding import PartitionSpec as P

HEADS = 8
KV_HEADS = 4
HEAD_DIM = 256
WINDOW = 1024
NORM_EPS = 1e-06
ROPE_BASE = 1000042.0
NEG_LARGE = -1e30
SCALE = HEAD_DIM**-0.5
PLANE = ("x", "core", "y")
EVERY = ("x", "core", "z", "y")
BF16 = jnp.bfloat16
F32 = jnp.float32


def dot_nn(a, b):
    return lax.dot_general(a, b, (((1,), (0,)), ((), ())), preferred_element_type=F32)


def dot_nt(a, b):
    return lax.dot_general(a, b, (((1,), (1,)), ((), ())), preferred_element_type=F32)


def dot_tn(a, b):
    return lax.dot_general(a, b, (((0,), (0,)), ((), ())), preferred_element_type=F32)


def rotate(values, cosine, sine):
    half = values.shape[-1] // 2
    a, b = values[:, :half], values[:, half:]
    return jnp.concatenate([a * cosine - b * sine, b * cosine + a * sine], -1)


def masked_prob(q, k, qinfo, kseg):
    scores = dot_nt(q, k) * SCALE
    qpos, qseg = qinfo[:, 0:1], qinfo[:, 1:2]
    kpos = lax.broadcasted_iota(jnp.int32, scores.shape, 1)
    allowed = (kpos <= qpos) & (qpos - kpos < WINDOW) & (qseg == kseg)
    masked = jnp.where(allowed, scores, NEG_LARGE)
    e = jnp.exp(masked - jnp.max(masked, -1, keepdims=True))
    return e / jnp.sum(e, -1, keepdims=True)


def attn_fwd_kernel(q_ref, k_ref, v_ref, qinfo_ref, kseg_ref, o_ref):
    hd = q_ref.shape[-1]
    q = q_ref[...].reshape(-1, hd)
    k = k_ref[...].reshape(-1, hd)
    v = v_ref[...].reshape(-1, hd)
    prob = masked_prob(q, k, qinfo_ref[0], kseg_ref[0])
    o_ref[...] = dot_nn(prob.astype(BF16), v).astype(BF16).reshape(o_ref.shape)


def attn_bwd_kernel(
    q_ref, k_ref, v_ref, do_ref, qinfo_ref, kseg_ref, dq_ref, dk_ref, dv_ref
):
    hd = q_ref.shape[-1]
    q = q_ref[...].reshape(-1, hd)
    k = k_ref[...].reshape(-1, hd)
    v = v_ref[...].reshape(-1, hd)
    do = do_ref[...].reshape(-1, hd)
    prob = masked_prob(q, k, qinfo_ref[0], kseg_ref[0])
    dprob = dot_nt(do, v)
    ds = prob * (dprob - jnp.sum(prob * dprob, -1, keepdims=True))
    dsb = ds.astype(BF16)
    dq_ref[...] = (dot_nn(dsb, k) * SCALE).reshape(dq_ref.shape)
    dk_ref[...] = (dot_tn(dsb, q) * SCALE).astype(BF16).reshape(dk_ref.shape)
    dv_ref[...] = dot_tn(prob.astype(BF16), do).astype(BF16).reshape(dv_ref.shape)


def attention_specs(dims):
    dp, ny, ms, pl_len, nz, hd = dims
    qspec = pl.BlockSpec((1, ny, 1, pl_len, hd), lambda d, m: (d, 0, m, 0, 0))
    kspec = pl.BlockSpec((nz, 1, ny, 1, pl_len, hd), lambda d, m: (0, d, 0, m, 0, 0))
    qi = pl.BlockSpec((1, ny * pl_len, 2), lambda d, m: (d * ms + m, 0, 0))
    ks = pl.BlockSpec((1, 1, nz * ny * pl_len), lambda d, m: (d * ms + m, 0, 0))
    return qspec, kspec, qi, ks


def attn_forward(q, k, v, qinfo, kseg, dims):
    dp, ny, ms, pl_len, nz, hd = dims
    qspec, kspec, qi, ks = attention_specs(dims)
    return pl.pallas_call(
        attn_fwd_kernel,
        grid=(dp, ms),
        in_specs=[qspec, kspec, kspec, qi, ks],
        out_specs=qspec,
        out_shape=jax.ShapeDtypeStruct((dp, ny, ms, pl_len, hd), BF16),
        compiler_params=pltpu.CompilerParams(vmem_limit_bytes=48 << 20),
        cost_estimate=pl.CostEstimate(
            flops=dp * ms * ny * pl_len * nz * ny * pl_len * hd * 4,
            bytes_accessed=4 * dp * ms * nz * ny * pl_len * hd,
            transcendentals=dp * ms * ny * pl_len * nz * ny * pl_len,
        ),
        name="attention_forward",
    )(q, k, v, qinfo, kseg)


def attn_backward(q, k, v, do, qinfo, kseg, dims):
    dp, ny, ms, pl_len, nz, hd = dims
    qspec, kspec, qi, ks = attention_specs(dims)
    kshape = (nz, dp, ny, ms, pl_len, hd)
    return pl.pallas_call(
        attn_bwd_kernel,
        grid=(dp, ms),
        in_specs=[qspec, kspec, kspec, qspec, qi, ks],
        out_specs=[qspec, kspec, kspec],
        out_shape=[
            jax.ShapeDtypeStruct((dp, ny, ms, pl_len, hd), F32),
            jax.ShapeDtypeStruct(kshape, BF16),
            jax.ShapeDtypeStruct(kshape, BF16),
        ],
        compiler_params=pltpu.CompilerParams(vmem_limit_bytes=48 << 20),
        cost_estimate=pl.CostEstimate(
            flops=dp * ms * ny * pl_len * nz * ny * pl_len * hd * 10,
            bytes_accessed=8 * dp * ms * nz * ny * pl_len * hd,
            transcendentals=dp * ms * ny * pl_len * nz * ny * pl_len,
        ),
        name="attention_backward",
    )(q, k, v, do, qinfo, kseg)


def plane_gather(a):
    return lax.all_gather(a, PLANE, axis=0, tiled=True)


def plane_scatter(a):
    return lax.psum_scatter(a, PLANE, scatter_dimension=0, tiled=True)


def weight_columns(w):
    part = lax.all_to_all(w, PLANE, split_axis=1, concat_axis=0, tiled=True)
    part = part.reshape(-1, w.shape[2])
    return lax.all_gather(part, "z", axis=0, tiled=True)


def weight_rows_back(g, rows):
    part = lax.psum_scatter(g, "z", scatter_dimension=0, tiled=True)
    part = part.reshape(8 * rows, 1, g.shape[1])
    return lax.all_to_all(part, PLANE, split_axis=0, concat_axis=1, tiled=True)


def shards(
    tokens,
    segments,
    attn_gain,
    query_weight,
    key_weight,
    value_weight,
    out_weight,
    ffn_gain,
    gate_weight,
    up_weight,
    down_weight,
    cotangent,
):
    micro, seq_local, pl_len, width = tokens.shape
    seq_len = segments.shape[2]
    ms = micro * seq_local
    rows_w = gate_weight.shape[0]
    ffn_width = gate_weight.shape[1]
    nx, nc, nz, ny = (lax.axis_size(a) for a in EVERY)
    dp = nx * nc
    n_own = ms * pl_len
    n_plane = 8 * n_own
    col_block = width // (dp * nz)
    dims = (dp, ny, ms, pl_len, nz, HEAD_DIM)
    z_index = lax.axis_index("z")
    core = lax.axis_index("core")

    def perm(a):
        lead = a.shape[:-1]
        return a.reshape(*lead, dp, nz, col_block).swapaxes(-3, -2).reshape(*lead, width)

    def unperm(a):
        lead = a.shape[:-1]
        return a.reshape(*lead, nz, dp, col_block).swapaxes(-3, -2).reshape(*lead, width)

    def by_head(a):
        return a.reshape(a.shape[0], 2, 2, 2, -1).swapaxes(2, 3).reshape(a.shape[0], 8, -1)

    def from_head(a):
        return a.reshape(a.shape[0], 2, 2, 2, -1).swapaxes(2, 3).reshape(a.shape[0], -1)

    heads_of = [(x * 2 + y) * 2 + c for x in range(2) for c in range(2) for y in range(2)]

    def place(x, c, z, y):
        return ((x * 2 + c) * nz + z) * 2 + y

    to_head, to_owner = [], []
    for x in range(2):
        for c in range(2):
            for y in range(2):
                head = (x * 2 + y) * 2 + c
                for k in range(nz):
                    to_head.append((head * nz + k, place(x, c, k, y)))
                    to_owner.append((place(x, c, k, y), head * nz + k))

    g1 = attn_gain.astype(F32)[:, None]
    g2 = ffn_gain.astype(F32)[:, None]

    def fold(w, g):
        return (w.astype(F32) * g).astype(BF16)

    wq_own = by_head(query_weight)
    wkv_own = jnp.stack(
        [key_weight.reshape(rows_w, KV_HEADS, HEAD_DIM), value_weight.reshape(rows_w, KV_HEADS, HEAD_DIM)], 2
    ).reshape(rows_w, 8 * HEAD_DIM)
    wkv_own = by_head(wkv_own)
    wqkv_own = jnp.concatenate([wq_own, wkv_own], 2)
    w_qkv = weight_columns((wqkv_own.astype(F32) * g1[:, :, None]).astype(BF16))
    w_out = lax.all_gather(
        lax.ppermute(perm(out_weight), EVERY, to_head), "z", axis=0, tiled=True
    )
    w_gate = weight_columns(fold(gate_weight, g2).reshape(rows_w, 8, -1))
    w_up = weight_columns(fold(up_weight, g2).reshape(rows_w, 8, -1))
    w_down = weight_columns(down_weight.reshape(rows_w, 8, -1))

    x = perm(tokens).reshape(n_own, width).astype(F32)
    r1 = lax.rsqrt(jnp.mean(x * x, -1, keepdims=True) + NORM_EPS)
    xhat = x * r1
    xa = plane_gather(xhat.astype(BF16))

    inv_freq = 1.0 / ROPE_BASE ** (jnp.arange(0, HEAD_DIM, 2, dtype=F32) / HEAD_DIM)
    pos = z_index * (ny * pl_len) + jnp.arange(ny * pl_len, dtype=jnp.int32)
    angles = pos.astype(F32)[:, None] * inv_freq[None, :]

    def spread(t):
        t = t.reshape(1, ny, 1, pl_len, HEAD_DIM // 2)
        return jnp.broadcast_to(t, (dp, ny, ms, pl_len, HEAD_DIM // 2)).reshape(n_plane, -1)

    cos_q, sin_q = spread(jnp.cos(angles)), spread(jnp.sin(angles))
    cos_k = jnp.where(core == 0, cos_q, 1.0)
    sin_k = jnp.where(core == 0, sin_q, 0.0)

    seg_all = lax.all_gather(segments, ("x", "core"), axis=0, tiled=False)
    seg_all = seg_all.reshape(dp * ms, seq_len)
    qseg = lax.dynamic_slice_in_dim(seg_all, z_index * (ny * pl_len), ny * pl_len, 1)
    qinfo = jnp.stack([jnp.broadcast_to(pos[None], qseg.shape), qseg], -1)
    kseg = seg_all[:, None, :]

    qkv = dot_nn(xa, w_qkv)
    qb = rotate(qkv[:, :HEAD_DIM], cos_q, sin_q).astype(BF16)
    kvb = rotate(qkv[:, HEAD_DIM:], cos_k, sin_k).astype(BF16)
    kv_all = lax.all_gather(lax.all_gather(kvb, "z", axis=0), "core", axis=0)
    k_all = kv_all[0].reshape(nz, dp, ny, ms, pl_len, HEAD_DIM)
    v_all = kv_all[1].reshape(nz, dp, ny, ms, pl_len, HEAD_DIM)
    q5 = qb.reshape(dp, ny, ms, pl_len, HEAD_DIM)
    ob = attn_forward(q5, k_all, v_all, qinfo, kseg, dims).reshape(n_plane, HEAD_DIM)
    h = x + plane_scatter(dot_nn(ob, w_out).astype(BF16)).astype(F32)

    r2 = lax.rsqrt(jnp.mean(h * h, -1, keepdims=True) + NORM_EPS)
    hhat = h * r2
    ha = plane_gather(hhat.astype(BF16))
    gate = dot_nn(ha, w_gate)
    up = dot_nn(ha, w_up)
    sig = jax.nn.sigmoid(gate)
    silu = gate * sig
    mid = (silu * up).astype(BF16)
    result = h + plane_scatter(dot_nt(mid, w_down).astype(BF16)).astype(F32)
    output = unperm(result.astype(BF16)).reshape(tokens.shape)

    cot = perm(cotangent).reshape(n_own, width)
    ca = plane_gather(cot)
    d_mid = dot_nn(ca, w_down)
    dgb = (d_mid * up * sig * (1.0 + gate * (1.0 - sig))).astype(BF16)
    dub = (d_mid * silu).astype(BF16)
    d_hhat = plane_scatter((dot_nt(dgb, w_gate) + dot_nt(dub, w_up)).astype(BF16)).astype(F32)
    dh = cot.astype(F32) + r2 * (d_hhat - hhat * jnp.mean(d_hhat * hhat, -1, keepdims=True))
    da = plane_gather(dh.astype(BF16))
    dob = dot_nt(da, w_out).astype(BF16)

    dq, dk_h, dv_h = attn_backward(
        q5, k_all, v_all, dob.reshape(q5.shape), qinfo, kseg, dims
    )
    dkv = lax.psum_scatter(jnp.stack([dk_h, dv_h]), "core", scatter_dimension=0)
    dkv = lax.psum_scatter(dkv, "z", scatter_dimension=0).reshape(n_plane, HEAD_DIM)
    dqb = rotate(dq.reshape(n_plane, HEAD_DIM), cos_q, -sin_q).astype(BF16)
    dkvb = rotate(dkv.astype(F32), cos_k, -sin_k).astype(BF16)
    dqkv = jnp.concatenate([dqb, dkvb], 1)
    d_xhat = plane_scatter(dot_nt(dqkv, w_qkv).astype(BF16)).astype(F32)
    input_grad = dh + r1 * (d_xhat - xhat * jnp.mean(d_xhat * xhat, -1, keepdims=True))
    input_grad = unperm(input_grad).reshape(tokens.shape)

    gate_back = weight_rows_back(dot_tn(ha, dgb).astype(BF16), rows_w).reshape(rows_w, -1).astype(F32)
    up_back = weight_rows_back(dot_tn(ha, dub).astype(BF16), rows_w).reshape(rows_w, -1).astype(F32)
    down_back = weight_rows_back(dot_tn(ca, mid).astype(BF16), rows_w).reshape(rows_w, -1).astype(F32)
    out_back = lax.psum_scatter(
        dot_tn(ob, da).astype(BF16), "z", scatter_dimension=0, tiled=True
    )
    out_back = unperm(lax.ppermute(out_back, EVERY, to_owner).astype(F32))
    qkv_back = weight_rows_back(dot_tn(xa, dqkv).astype(BF16), rows_w).astype(F32)
    q_back = from_head(qkv_back[:, :, :HEAD_DIM])
    kv_back = from_head(qkv_back[:, :, HEAD_DIM:]).reshape(rows_w, KV_HEADS, 2, HEAD_DIM)
    k_back = kv_back[:, :, 0].reshape(rows_w, -1)
    v_back = kv_back[:, :, 1].reshape(rows_w, -1)

    def gain_term(pairs):
        return sum(jnp.sum(w.astype(F32) * g, -1) for w, g in pairs)

    return (
        output,
        input_grad,
        gain_term([(query_weight, q_back), (key_weight, k_back), (value_weight, v_back)]),
        q_back * g1,
        k_back * g1,
        v_back * g1,
        out_back,
        gain_term([(gate_weight, gate_back), (up_weight, up_back)]),
        gate_back * g2,
        up_back * g2,
        down_back,
    )


def solution(mesh):
    dp, seq = mesh.shape["dp"], mesh.shape["seq"]
    fine = Mesh(mesh.devices.reshape(dp // 2, 2, seq // 2, 2), EVERY)
    dp_axes, seq_axes = ("x", "core"), ("z", "y")
    tok = P(None, dp_axes, seq_axes, None)
    vec, mat = P(EVERY), P(EVERY, None)
    return jax.shard_map(
        shards,
        mesh=fine,
        in_specs=(tok, P(None, dp_axes, None), vec, mat, mat, mat, mat, vec, mat, mat, mat, tok),
        out_specs=(tok, tok, vec, mat, mat, mat, mat, vec, mat, mat, mat),
        check_vma=False,
    )
```

```python
import functools

import jax
import jax.numpy as jnp
from jax import lax
from jax.experimental import pallas as pl
from jax.experimental.pallas import tpu as pltpu
from jax.sharding import Mesh
from jax.sharding import PartitionSpec as P

HEADS = 8
KV_HEADS = 4
HEAD_DIM = 256
WINDOW = 1024
NORM_EPS = 1e-06
ROPE_BASE = 1000042.0
NEG_LARGE = -1e30
SCALE = HEAD_DIM**-0.5
PLANE = ("x", "core", "y")
EVERY = ("x", "core", "z", "y")
BF16 = jnp.bfloat16
F32 = jnp.float32
MESH = pl.DeviceIdType.MESH
GATHER_PARTS = 4
SCATTER_PARTS = 4
CORE_PARTS = 4


def dot_nn(a, b):
    return lax.dot_general(a, b, (((1,), (0,)), ((), ())), preferred_element_type=F32)


def dot_nt(a, b):
    return lax.dot_general(a, b, (((1,), (1,)), ((), ())), preferred_element_type=F32)


def dot_tn(a, b):
    return lax.dot_general(a, b, (((0,), (0,)), ((), ())), preferred_element_type=F32)


def rotate(values, cosine, sine):
    half = values.shape[-1] // 2
    a, b = values[:, :half], values[:, half:]
    return jnp.concatenate([a * cosine - b * sine, b * cosine + a * sine], -1)


QUERY_ROWS = 256


def query_blocks(seq_len):
    out = []
    for first in range(0, seq_len, QUERY_ROWS):
        low = max(0, first - WINDOW + 1) // 128 * 128
        out.append((first, low, min(seq_len, first + QUERY_ROWS)))
    return out


def masked_prob(q, k, first, low, qseg, kseg):
    scores = dot_nt(q, k) * SCALE
    qpos = first + lax.broadcasted_iota(jnp.int32, scores.shape, 0)
    kpos = low + lax.broadcasted_iota(jnp.int32, scores.shape, 1)
    allowed = (kpos <= qpos) & (qpos - kpos < WINDOW) & (qseg == kseg)
    masked = jnp.where(allowed, scores, NEG_LARGE)
    e = jnp.exp(masked - jnp.max(masked, -1, keepdims=True))
    return e / jnp.sum(e, -1, keepdims=True)


def attn_fwd_kernel(q_ref, k_ref, v_ref, qseg_ref, kseg_ref, o_ref):
    for first, low, end in query_blocks(q_ref.shape[0]):
        rows, keys = pl.ds(first, QUERY_ROWS), pl.ds(low, end - low)
        prob = masked_prob(q_ref[rows, :], k_ref[keys, :], first, low, qseg_ref[rows, :], kseg_ref[:, keys])
        o_ref[rows, :] = dot_nn(prob.astype(BF16), v_ref[keys, :]).astype(BF16)


def attn_bwd_kernel(q_ref, k_ref, v_ref, do_ref, qseg_ref, kseg_ref, *refs):
    dq_ref, dkv_ref, dk_sum, dv_sum = refs[-4:]
    dk_sum[...] = jnp.zeros_like(dk_sum)
    dv_sum[...] = jnp.zeros_like(dv_sum)
    for first, low, end in query_blocks(q_ref.shape[0]):
        rows, keys = pl.ds(first, QUERY_ROWS), pl.ds(low, end - low)
        q, k, v, do = q_ref[rows, :], k_ref[keys, :], v_ref[keys, :], do_ref[rows, :]
        prob = masked_prob(q, k, first, low, qseg_ref[rows, :], kseg_ref[:, keys])
        dprob = dot_nt(do, v)
        ds = prob * (dprob - jnp.sum(prob * dprob, -1, keepdims=True))
        dsb = ds.astype(BF16)
        dq_ref[rows, :] = dot_nn(dsb, k) * SCALE
        dk_sum[keys, :] += dot_tn(dsb, q)
        dv_sum[keys, :] += dot_tn(prob.astype(BF16), do)
    dkv_ref[0] = (dk_sum[...] * SCALE).astype(BF16)
    dkv_ref[1] = dv_sum[...].astype(BF16)


def attention_specs(seq_len):
    qspec = pl.BlockSpec((None, seq_len, HEAD_DIM), lambda s: (s, 0, 0))
    kspec = pl.BlockSpec((None, None, seq_len, HEAD_DIM), lambda s: (0, s, 0, 0))
    vspec = pl.BlockSpec((None, None, seq_len, HEAD_DIM), lambda s: (1, s, 0, 0))
    qseg = pl.BlockSpec((None, seq_len, 1), lambda s: (s, 0, 0))
    kseg = pl.BlockSpec((None, 1, seq_len), lambda s: (s, 0, 0))
    return qspec, kspec, vspec, qseg, kseg


def attn_forward(q, kv, qseg, kseg):
    seqs, seq_len, _ = q.shape
    qspec, kspec, vspec, qi, ks = attention_specs(seq_len)
    return pl.pallas_call(
        attn_fwd_kernel,
        grid=(seqs,),
        in_specs=[qspec, kspec, vspec, qi, ks],
        out_specs=qspec,
        out_shape=jax.ShapeDtypeStruct(q.shape, BF16),
        compiler_params=pltpu.CompilerParams(vmem_limit_bytes=48 << 20),
        cost_estimate=light(),
        name="attention_forward",
    )(q, kv, kv, qseg, kseg)


def attn_backward(q, kv, do, qseg, kseg, *earlier):
    seqs, seq_len, _ = q.shape
    qspec, kspec, vspec, qi, ks = attention_specs(seq_len)
    return pl.pallas_call(
        attn_bwd_kernel,
        grid=(seqs,),
        in_specs=[qspec, kspec, vspec, qspec, qi, ks] + [ANY] * len(earlier),
        out_specs=[qspec, pl.BlockSpec((2, None, seq_len, HEAD_DIM), lambda s: (0, s, 0, 0))],
        out_shape=[
            jax.ShapeDtypeStruct(q.shape, F32),
            jax.ShapeDtypeStruct((2, *q.shape), BF16),
        ],
        scratch_shapes=[pltpu.VMEM((seq_len, HEAD_DIM), F32)] * 2,
        compiler_params=pltpu.CompilerParams(vmem_limit_bytes=48 << 20),
        cost_estimate=light(),
        name="attention_backward",
    )(q, kv, kv, do, qseg, kseg, *earlier)


NUMBERS = [0]


def fresh():
    NUMBERS[0] += 1
    return NUMBERS[0] - 1


def flips():
    x, c, y = (lax.axis_index(a) for a in PLANE)
    return x, c, y, {"x": 1 - x}, {"y": 1 - y}, {"core": 1 - c}


def greet(*targets):
    barrier = pltpu.get_barrier_semaphore()
    for target in targets:
        pl.semaphore_signal(barrier, 1, device_id=target, device_id_type=MESH)
    pl.semaphore_wait(barrier, len(targets))


def pieces_at(ref, split, px, pc, py):
    return ref.at[pc, :, px, py] if split == 2 else ref.at[:, pc, px, py]


def plane_shape(split, slots, *rest):
    return (2, slots, 2, 2, *rest) if split == 2 else (slots, 2, 2, 2, *rest)


def gather_kernel(split, a_ref, *refs):
    o_ref, own_sem, send_sem, recv_sem = refs[-4:]
    x, c, y, to_x, to_y, to_c = flips()
    slots, piece, _ = a_ref.shape
    per_slot = GATHER_PARTS // slots
    step = piece // per_slot
    greet(to_x, to_y, to_c)

    def rows_of(i):
        return i // per_slot, pl.ds(i % per_slot * step, step)

    def part(px, pc, py, i):
        return pieces_at(o_ref, split, px, pc, py).at[rows_of(i)]

    def send(kind, i, src, dst, target):
        copy = pltpu.make_async_remote_copy(
            src_ref=src, dst_ref=dst, send_sem=send_sem.at[kind, i], recv_sem=recv_sem.at[kind, i],
            device_id=target, device_id_type=MESH,
        )
        copy.start()
        return copy

    own_copy = pltpu.make_async_copy(a_ref, pieces_at(o_ref, split, x, c, y), own_sem)
    own_copy.start()
    copies = {}
    for i in range(GATHER_PARTS):
        own = a_ref.at[rows_of(i)]
        for kind, target in enumerate((to_x, to_y, to_c)):
            copies[kind, i] = send(kind, i, own, part(x, c, y, i), target)
    src_x, src_y = jnp.where(c == 0, x, 1 - x), jnp.where(c == 0, 1 - y, y)
    dst_x, dst_y = jnp.where(c == 0, 1 - x, x), jnp.where(c == 0, y, 1 - y)
    for i in range(GATHER_PARTS):
        for kind, (px, py) in enumerate(((1 - x, y), (x, 1 - y))):
            copies[kind, i].wait_recv()
            block = part(px, c, py, i)
            copies[3 + kind, i] = send(3 + kind, i, block, block, to_c)
        block = part(src_x, c, src_y, i)
        copies[5, i] = send(5, i, block, block, {"x": dst_x, "y": dst_y})
    for i in range(GATHER_PARTS):
        copies[5, i].wait_recv()
        block = part(1 - x, c, 1 - y, i)
        copies[6, i] = send(6, i, block, block, to_c)
    for i in range(GATHER_PARTS):
        for kind in (2, 3, 4, 6):
            copies[kind, i].wait_recv()
    own_copy.wait()
    for i in range(GATHER_PARTS):
        for kind in range(7):
            copies[kind, i].wait_send()


ANY = pl.BlockSpec(memory_space=pl.ANY)
WHOLE = pl.BlockSpec(memory_space=pltpu.VMEM)


def light(bytes_accessed=1024):
    return pl.CostEstimate(flops=0, bytes_accessed=bytes_accessed, transcendentals=0)


def plane_gather(a, split, *earlier):
    slots, piece, width = a.shape
    out = pl.pallas_call(
        functools.partial(gather_kernel, split),
        out_shape=jax.ShapeDtypeStruct(plane_shape(split, slots, piece, width), a.dtype),
        in_specs=[WHOLE] + [ANY] * len(earlier),
        out_specs=ANY,
        scratch_shapes=[
            pltpu.SemaphoreType.DMA,
            pltpu.SemaphoreType.DMA((7, GATHER_PARTS)),
            pltpu.SemaphoreType.DMA((7, GATHER_PARTS)),
        ],
        compiler_params=pltpu.CompilerParams(collective_id=fresh(), has_side_effects=True),
        cost_estimate=light(),
        name="plane_gather",
    )(a, *earlier)
    return out.reshape(-1, width)


def scatter_kernel(split, p_ref, *refs):
    o_ref, own, got_c, put_x, put_y, got_x, got_y, fin_x, fin_y, end_x, end_y, own_sem, send_sem, recv_sem = refs[-14:]
    x, c, y, to_x, to_y, to_c = flips()
    parts, _, _, step, width = own.shape
    slots, piece, _ = o_ref.shape
    per_slot = parts // slots
    half = width // 2
    left, right = pl.ds(0, half), pl.ds(half, half)
    greet(to_x, to_y, to_c)

    def send(kind, i, src, dst, target):
        copy = pltpu.make_async_remote_copy(
            src_ref=src.at[i] if kind else src, dst_ref=dst.at[i],
            send_sem=send_sem.at[kind, i], recv_sem=recv_sem.at[kind, i],
            device_id=target, device_id_type=MESH,
        )
        copy.start()
        return copy

    loads, first, second, third = [], [], [], []
    def rows_of(i):
        return i // per_slot, pl.ds(i % per_slot * step, step)

    def blocks(pc, i):
        slot, rows = rows_of(i)
        return p_ref.at[pc, slot, :, :, rows, :] if split == 2 else p_ref.at[slot, pc, :, :, rows, :]

    for i in range(parts):
        first.append(send(0, i, blocks(1 - c, i), got_c, to_c))
        load = pltpu.make_async_copy(blocks(c, i), own.at[i], own_sem.at[i])
        load.start()
        loads.append(load)

    def f32(ref, *index):
        return ref[index].astype(F32)

    for i in range(parts):
        loads[i].wait()
        first[i].wait_recv()
        for j in range(2):
            put_x[i, j] = (f32(own, i, 1 - x, j, slice(None), left) + f32(got_c, i, 1 - x, j, slice(None), left)).astype(BF16)
            put_y[i, j] = (f32(own, i, j, 1 - y, slice(None), right) + f32(got_c, i, j, 1 - y, slice(None), right)).astype(BF16)
        second.append((send(1, i, put_x, got_x, to_x), send(2, i, put_y, got_y, to_y)))
    for i in range(parts):
        for copy in second[i]:
            copy.wait_recv()
        fin_y[i] = (
            f32(own, i, x, 1 - y, slice(None), left) + f32(got_c, i, x, 1 - y, slice(None), left) + f32(got_x, i, 1 - y)
        ).astype(BF16)
        fin_x[i] = (
            f32(own, i, 1 - x, y, slice(None), right) + f32(got_c, i, 1 - x, y, slice(None), right) + f32(got_y, i, 1 - x)
        ).astype(BF16)
        third.append((send(3, i, fin_y, end_y, to_y), send(4, i, fin_x, end_x, to_x)))
    for i in range(parts):
        for copy in third[i]:
            copy.wait_recv()
        slot, rows = rows_of(i)
        o_ref[slot, rows, left] = (
            f32(own, i, x, y, slice(None), left) + f32(got_c, i, x, y, slice(None), left)
            + f32(got_x, i, y) + f32(end_y, i)
        )
        o_ref[slot, rows, right] = (
            f32(own, i, x, y, slice(None), right) + f32(got_c, i, x, y, slice(None), right)
            + f32(got_y, i, x) + f32(end_x, i)
        )
    for i in range(parts):
        for copy in (first[i], *second[i], *third[i]):
            copy.wait_send()


def plane_scatter(a, split, slots, *earlier):
    rows, width = a.shape[0] // 8, a.shape[1]
    piece = rows // slots
    n = SCATTER_PARTS
    step, half = rows // n, width // 2
    return pl.pallas_call(
        functools.partial(scatter_kernel, split),
        out_shape=jax.ShapeDtypeStruct((slots, piece, width), F32),
        in_specs=[ANY] * (1 + len(earlier)),
        out_specs=WHOLE,
        scratch_shapes=[
            pltpu.VMEM((n, 2, 2, step, width), BF16),
            pltpu.VMEM((n, 2, 2, step, width), BF16),
            pltpu.VMEM((n, 2, step, half), BF16),
            pltpu.VMEM((n, 2, step, half), BF16),
            pltpu.VMEM((n, 2, step, half), BF16),
            pltpu.VMEM((n, 2, step, half), BF16),
            pltpu.VMEM((n, step, half), BF16),
            pltpu.VMEM((n, step, half), BF16),
            pltpu.VMEM((n, step, half), BF16),
            pltpu.VMEM((n, step, half), BF16),
            pltpu.SemaphoreType.DMA((n,)),
            pltpu.SemaphoreType.DMA((5, n)),
            pltpu.SemaphoreType.DMA((5, n)),
        ],
        compiler_params=pltpu.CompilerParams(
            collective_id=fresh(), has_side_effects=True, vmem_limit_bytes=32 << 20
        ),
        cost_estimate=light(),
        name="plane_scatter",
    )(a.reshape(plane_shape(split, slots, piece, width)), *earlier)


def pair_kernel(a_ref, *refs):
    o_ref, own_sem, send_sem, recv_sem = refs[-4:]
    c = lax.axis_index("core")
    greet({"core": 1 - c})
    keep = pltpu.make_async_copy(a_ref, o_ref.at[c], own_sem)
    keep.start()
    copy = pltpu.make_async_remote_copy(
        src_ref=a_ref, dst_ref=o_ref.at[c], send_sem=send_sem, recv_sem=recv_sem,
        device_id={"core": 1 - c}, device_id_type=MESH,
    )
    copy.start()
    keep.wait()
    copy.wait()


def core_gather(a, *earlier):
    return pl.pallas_call(
        pair_kernel,
        out_shape=jax.ShapeDtypeStruct((2, *a.shape), a.dtype),
        in_specs=[WHOLE] + [ANY] * len(earlier),
        out_specs=ANY,
        scratch_shapes=[pltpu.SemaphoreType.DMA] * 3,
        compiler_params=pltpu.CompilerParams(
            collective_id=fresh(), has_side_effects=True, vmem_limit_bytes=32 << 20
        ),
        cost_estimate=light(),
        name="core_gather",
    )(a, *earlier)


def pair_sum_kernel(a_ref, *refs):
    o_ref, own, got, out, own_sem, out_sem, send_sem, recv_sem = refs[-8:]
    c = lax.axis_index("core")
    parts, step, _ = own.shape
    greet({"core": 1 - c})
    copies, loads, stores = [], [], []
    for i in range(parts):
        rows = pl.ds(i * step, step)
        copy = pltpu.make_async_remote_copy(
            src_ref=a_ref.at[1 - c, rows, :], dst_ref=got.at[i], send_sem=send_sem.at[i], recv_sem=recv_sem.at[i],
            device_id={"core": 1 - c}, device_id_type=MESH,
        )
        copy.start()
        copies.append(copy)
        load = pltpu.make_async_copy(a_ref.at[c, rows, :], own.at[i], own_sem.at[i])
        load.start()
        loads.append(load)
    for i in range(parts):
        loads[i].wait()
        copies[i].wait_recv()
        out[i] = own[i].astype(F32) + got[i].astype(F32)
        store = pltpu.make_async_copy(out.at[i], o_ref.at[pl.ds(i * step, step), :], out_sem.at[i])
        store.start()
        stores.append(store)
    for i in range(parts):
        stores[i].wait()
        copies[i].wait_send()


def core_scatter(a, *earlier):
    _, rows, width = a.shape
    n = CORE_PARTS
    return pl.pallas_call(
        pair_sum_kernel,
        out_shape=jax.ShapeDtypeStruct((rows, width), F32),
        in_specs=[ANY] * (1 + len(earlier)),
        out_specs=ANY,
        scratch_shapes=[pltpu.VMEM((n, rows // n, width), BF16)] * 2
        + [pltpu.VMEM((n, rows // n, width), F32)]
        + [pltpu.SemaphoreType.DMA((n,))] * 4,
        compiler_params=pltpu.CompilerParams(
            collective_id=fresh(), has_side_effects=True, vmem_limit_bytes=32 << 20
        ),
        cost_estimate=light(),
        name="core_scatter",
    )(a, *earlier)


def others():
    x, c, y, *_ = flips()
    out = []
    for dx, dc, dy in ((1, 0, 1), (1, 1, 1), (1, 0, 0), (0, 0, 1), (1, 1, 0), (0, 1, 1), (0, 1, 0)):
        px, pc, py = (1 - x if dx else x), (1 - c if dc else c), (1 - y if dy else y)
        out.append(((px * 2 + pc) * 2 + py, {"x": px, "core": pc, "y": py}))
    return (x * 2 + c) * 2 + y, out


def token_moves(split, ms):
    x, c, y, *_ = flips()
    z = lax.axis_index("z")
    if split == 2:
        slot, group = z // 2, z // 2
        to = [(z % 2, c, 2 * j + x) for j in range(ms)]
        of = [(z % 2, c, 2 * k + x) for k in range(ms)]
    else:
        slot, group = z // 4, z // 4
        to = [(z % 2, z // 2 % 2, (2 * j + x) * 2 + c) for j in range(ms)]
        of = [(z // 2 % 2, z % 2, 4 * k + 2 * c + x) for k in range(ms)]
    me = (x * 2 + c) * 64 + z
    places = [[{"x": px, "core": pc, "z": pz}, (px * 2 + pc) * 64 + pz != me] for px, pc, pz in to]
    sources = [[{"x": px, "core": pc, "z": pz}, (px * 2 + pc) * 64 + pz != me] for px, pc, pz in of]
    return slot, group, places, sources


def token_kernel(split, t_ref, *refs):
    o_ref, send_sem, recv_sem = refs[-3:]
    finish = start_tokens(split, t_ref, o_ref, send_sem, recv_sem, [])
    finish()


def start_tokens(split, t_ref, o_ref, send_sem, recv_sem, targets):
    ms = t_ref.shape[0]
    slot, group, places, sources = token_moves(split, ms)
    barrier = pltpu.get_barrier_semaphore()
    for target, remote in sources:
        @pl.when(remote)
        def _(target=target):
            pl.semaphore_signal(barrier, 1, device_id=target, device_id_type=MESH)
    for target in targets:
        pl.semaphore_signal(barrier, 1, device_id=target, device_id_type=MESH)
    count = len(targets)
    for _, remote in places:
        count = count + remote.astype(jnp.int32)
    pl.semaphore_wait(barrier, count)

    def local(j):
        return pltpu.make_async_copy(t_ref.at[j], o_ref.at[slot], recv_sem.at[slot])

    def away(j):
        return pltpu.make_async_remote_copy(
            src_ref=t_ref.at[j], dst_ref=o_ref.at[slot], send_sem=send_sem.at[j], recv_sem=recv_sem.at[slot],
            device_id=places[j][0], device_id_type=MESH,
        )

    for j in range(ms):
        pl.when(places[j][1])(lambda j=j: away(j).start())
        pl.when(jnp.logical_not(places[j][1]))(lambda j=j: local(j).start())

    def finish():
        for k in range(ms):
            pltpu.make_async_copy(t_ref.at[0], o_ref.at[k], recv_sem.at[k]).wait()
        for j in range(ms):
            pl.when(places[j][1])(lambda j=j: away(j).wait_send())

    return finish


def spread_kernel(with_gain, with_seg, w_ref, *refs):
    refs = list(refs)
    g_ref = refs.pop(0) if with_gain else None
    seg_ref, tok_ref = (refs.pop(0), refs.pop(0)) if with_seg else (None, None)
    scaled, own_sem, send_sem, recv_sem, tok_send, tok_recv = refs[-6:]
    o_ref, seg_out, tok_out = refs[-9:-6] if with_seg else (refs[-7], None, None)
    rows, width = w_ref.shape
    cols = width // 8
    me, peers = others()
    if with_seg:
        finish = start_tokens(with_seg, tok_ref, tok_out, tok_send, tok_recv, [target for _, target in peers])
    else:
        greet(*(target for _, target in peers))

    def place(p):
        return o_ref.at[pl.ds(pl.multiple_of(p * rows, rows), rows), :]

    copies = []

    def send(kind, src, dst, target):
        copy = pltpu.make_async_remote_copy(
            src_ref=src, dst_ref=dst, send_sem=send_sem.at[kind], recv_sem=recv_sem.at[kind],
            device_id=target, device_id_type=MESH,
        )
        copy.start()
        copies.append(copy)

    def columns(p):
        return pl.ds(pl.multiple_of(p * cols, cols), cols)

    def piece(p):
        if with_gain:
            scaled[p] = (w_ref[:, columns(p)].astype(F32) * g_ref[...]).astype(BF16)
            return scaled.at[p]
        return w_ref.at[:, columns(p)]

    for kind, (p, target) in enumerate(peers):
        send(kind, piece(p), place(me), target)
        if with_seg:
            send(7 + kind, seg_ref, seg_out.at[me], target)
    keeps = [pltpu.make_async_copy(piece(me), place(me), own_sem.at[0])]
    if with_seg:
        keeps.append(pltpu.make_async_copy(seg_ref, seg_out.at[me], own_sem.at[1]))
    for keep in keeps:
        keep.start()
    for keep in keeps:
        keep.wait()
    for copy in copies:
        copy.wait()
    if with_seg:
        finish()


def to_columns(w, gain, seg, *earlier, split=0, tokens=None):
    rows, width = w.shape
    cols = width // 8
    operands = [w] + ([gain] if gain is not None else []) + ([seg, tokens] if seg is not None else [])
    ms = tokens.shape[0] if seg is not None else 1
    out_shape = [jax.ShapeDtypeStruct((8 * rows, cols), BF16)]
    if seg is not None:
        out_shape.append(jax.ShapeDtypeStruct((8, *seg.shape), seg.dtype))
        out_shape.append(jax.ShapeDtypeStruct(tokens.shape, tokens.dtype))
    return pl.pallas_call(
        functools.partial(spread_kernel, gain is not None, split),
        out_shape=out_shape,
        in_specs=[WHOLE] * len(operands) + [ANY] * len(earlier),
        out_specs=[ANY] * len(out_shape),
        scratch_shapes=[
            pltpu.VMEM((8, rows, cols), BF16),
            pltpu.SemaphoreType.DMA((2,)),
            pltpu.SemaphoreType.DMA((14,)),
            pltpu.SemaphoreType.DMA((14,)),
            pltpu.SemaphoreType.DMA((ms,)),
            pltpu.SemaphoreType.DMA((ms,)),
        ],
        compiler_params=pltpu.CompilerParams(collective_id=fresh(), has_side_effects=True),
        cost_estimate=light(),
        name="weight_columns",
    )(*operands, *earlier)


def return_kernel(with_gain, p_ref, *refs):
    refs = list(refs)
    w_ref, g_ref = (refs.pop(0), refs.pop(0)) if with_gain else (None, None)
    got, own_sem, send_sem, recv_sem = refs[-4:]
    o_ref = refs[-6] if with_gain else refs[-5]
    _, rows, cols = got.shape
    me, peers = others()
    greet(*(target for _, target in peers))

    def block(p):
        return p_ref.at[pl.ds(pl.multiple_of(p * rows, rows), rows), :]

    copies = []
    for kind, (p, target) in enumerate(peers):
        copy = pltpu.make_async_remote_copy(
            src_ref=block(p), dst_ref=got.at[me], send_sem=send_sem.at[kind], recv_sem=recv_sem.at[kind],
            device_id=target, device_id_type=MESH,
        )
        copy.start()
        copies.append(copy)
    keep = pltpu.make_async_copy(block(me), got.at[me], own_sem)
    keep.start()
    total = jnp.zeros((rows, 1), F32)

    def finish(p, total):
        columns = pl.ds(pl.multiple_of(p * cols, cols), cols)
        grad = got[p].astype(F32)
        if with_gain:
            total = total + jnp.sum(w_ref[:, columns].astype(F32) * grad, -1, keepdims=True)
            grad = grad * g_ref[...]
        o_ref[:, columns] = grad
        return total

    keep.wait()
    total = finish(me, total)
    for kind in (6, 2, 3, 4, 5, 0, 1):
        copies[kind].wait_recv()
        total = finish(peers[kind][0], total)
    if with_gain:
        refs[-5][...] = total
    for copy in copies:
        copy.wait_send()


def to_rows(part, w, gain, *earlier):
    cols = part.shape[1]
    rows = part.shape[0] // 8
    operands = [part] + ([w, gain] if gain is not None else [])
    out_shape = [jax.ShapeDtypeStruct((rows, 8 * cols), F32)]
    if gain is not None:
        out_shape.append(jax.ShapeDtypeStruct((rows, 1), F32))
    return pl.pallas_call(
        functools.partial(return_kernel, gain is not None),
        out_shape=out_shape,
        in_specs=[ANY] + [WHOLE] * (len(operands) - 1) + [ANY] * len(earlier),
        out_specs=[WHOLE] * len(out_shape),
        scratch_shapes=[
            pltpu.VMEM((8, rows, cols), BF16),
            pltpu.SemaphoreType.DMA,
            pltpu.SemaphoreType.DMA((7,)),
            pltpu.SemaphoreType.DMA((7,)),
        ],
        compiler_params=pltpu.CompilerParams(
            collective_id=fresh(), has_side_effects=True, vmem_limit_bytes=24 << 20
        ),
        cost_estimate=light(),
        name="weight_rows",
    )(*operands, *earlier)


def tie_kernel(a_ref, *refs):
    pass


def tie(a, *earlier):
    return pl.pallas_call(
        tie_kernel,
        out_shape=jax.ShapeDtypeStruct(a.shape, a.dtype),
        in_specs=[ANY] * (1 + len(earlier)),
        out_specs=ANY,
        input_output_aliases={0: 0},
        cost_estimate=light(),
        name="tie",
    )(a, *earlier)


def along_z(part):
    return lax.all_gather(part, "z", axis=0, tiled=True)


def sum_along_z(g):
    return lax.psum_scatter(g, "z", scatter_dimension=0, tiled=True)


def shards(
    tokens,
    segments,
    attn_gain,
    query_weight,
    key_weight,
    value_weight,
    out_weight,
    ffn_gain,
    gate_weight,
    up_weight,
    down_weight,
    cotangent,
):
    NUMBERS[0] = 0
    micro, seq_local, pl_len, width = tokens.shape
    seq_len = segments.shape[2]
    ms = micro * seq_local
    rows_w = gate_weight.shape[0]
    nx, nc, nz, ny = (lax.axis_size(a) for a in EVERY)
    dp = nx * nc
    n_plane = 8 * ms * pl_len
    col_block = width // (dp * nz)
    z_index = lax.axis_index("z")
    core = lax.axis_index("core")
    split = dp * ms // nz

    def perm(a):
        lead = a.shape[:-1]
        return a.reshape(*lead, dp, nz, col_block).swapaxes(-3, -2).reshape(*lead, width)

    def unperm(a):
        lead = a.shape[:-1]
        return a.reshape(*lead, nz, dp, col_block).swapaxes(-3, -2).reshape(*lead, width)

    def by_head(a):
        return a.reshape(a.shape[0], 2, 2, 2, -1).swapaxes(2, 3).reshape(a.shape[0], 8, -1)

    def from_head(a):
        return a.reshape(a.shape[0], 2, 2, 2, -1).swapaxes(2, 3).reshape(a.shape[0], -1)

    heads_of = [(x * 2 + y) * 2 + c for x in range(2) for c in range(2) for y in range(2)]

    def place(x, c, z, y):
        return ((x * 2 + c) * nz + z) * 2 + y

    to_head, to_owner = [], []
    for x in range(2):
        for c in range(2):
            for y in range(2):
                head = (x * 2 + y) * 2 + c
                for k in range(nz):
                    to_head.append((head * nz + k, place(x, c, k, y)))
                    to_owner.append((place(x, c, k, y), head * nz + k))

    def slot_of(z):
        return z // 2 if split == 2 else z // 4

    def group_of(z):
        return z // 2 if split == 2 else z // 4

    rounds = []
    for k in range(ms):
        moves = []
        for ox in range(2):
            for oc in range(2):
                for oz in range(nz):
                    j = (k + slot_of(oz)) % ms
                    if split == 2:
                        to = (oz % 2, oc, 2 * j + ox)
                    else:
                        to = (oz % 2, oz // 2 % 2, (2 * j + ox) * 2 + oc)
                    moves += [(place(ox, oc, oz, oy), place(*to, oy)) for oy in range(2)]
        rounds.append(moves)

    def pick(a, index):
        return lax.dynamic_index_in_dim(a, index, 0, keepdims=False)

    def to_planes(a):
        got = jnp.stack([
            lax.ppermute(pick(a, (k + slot_of(z_index)) % ms), EVERY, rounds[k]) for k in range(ms)
        ])
        return jnp.stack([pick(got, (group_of(z_index) - slot + ms) % ms) for slot in range(ms)])

    def from_planes(a):
        got = jnp.stack([
            lax.ppermute(
                pick(a, (group_of(z_index) - k + ms) % ms), EVERY, [(to, of) for of, to in rounds[k]]
            )
            for k in range(ms)
        ])
        return jnp.stack([pick(got, (j - slot_of(z_index) + ms) % ms) for j in range(ms)])

    g1 = attn_gain.astype(F32)[:, None]
    g2 = ffn_gain.astype(F32)[:, None]

    wq_own = by_head(query_weight)
    wkv_own = jnp.stack(
        [key_weight.reshape(rows_w, KV_HEADS, HEAD_DIM), value_weight.reshape(rows_w, KV_HEADS, HEAD_DIM)], 2
    ).reshape(rows_w, 8 * HEAD_DIM)
    wkv_own = by_head(wkv_own)
    wqkv_own = jnp.concatenate([wq_own, wkv_own], 2).reshape(rows_w, -1)
    wqkv_part, seg_all, x = to_columns(
        wqkv_own, g1, segments.reshape(ms, seq_len), split=split, tokens=tokens.reshape(ms, pl_len, width)
    )
    (gate_part,) = to_columns(gate_weight, g2, None, wqkv_part)
    w_qkv = along_z(wqkv_part)
    w_out = along_z(lax.ppermute(perm(out_weight), EVERY, to_head))

    seg_all = seg_all.reshape(2, 2, 2, ms, seq_len)[:, :, 0]
    if split == 2:
        seg = pick(pick(seg_all, z_index % 2).swapaxes(0, 1), z_index // 2)
    else:
        seg = pick(pick(pick(seg_all, z_index // 2 % 2), z_index % 2), z_index // 4)[None]
    qseg, kseg = seg[:, :, None], seg[:, None, :]

    x = perm(x).astype(F32)
    r1 = lax.rsqrt(jnp.mean(x * x, -1, keepdims=True) + NORM_EPS)
    xhat = x * r1
    xa = plane_gather(xhat.astype(BF16), split, gate_part)
    (down_part,) = to_columns(down_weight, None, None, xa)

    inv_freq = 1.0 / ROPE_BASE ** (jnp.arange(0, HEAD_DIM, 2, dtype=F32) / HEAD_DIM)
    angles = jnp.arange(seq_len, dtype=jnp.int32).astype(F32)[:, None] * inv_freq[None, :]
    cos_q, sin_q = (jnp.tile(t, (split, 1)) for t in (jnp.cos(angles), jnp.sin(angles)))
    cos_k = jnp.where(core == 0, cos_q, 1.0)
    sin_k = jnp.where(core == 0, sin_q, 0.0)

    qkv = dot_nn(xa, w_qkv)
    qb = rotate(qkv[:, :HEAD_DIM], cos_q, sin_q).astype(BF16).reshape(split, seq_len, HEAD_DIM)
    kvb = rotate(qkv[:, HEAD_DIM:], cos_k, sin_k).astype(BF16)
    kv_all = core_gather(kvb, down_part).reshape(2, split, seq_len, HEAD_DIM)

    w_gate = along_z(gate_part)
    w_down = along_z(down_part)
    ob = attn_forward(qb, kv_all, qseg, kseg).reshape(n_plane, HEAD_DIM)
    cot = perm(to_planes(tie(cotangent.reshape(ms, pl_len, width), ob)))
    h = x + plane_scatter(dot_nn(ob, w_out).astype(BF16), split, ms)

    r2 = lax.rsqrt(jnp.mean(h * h, -1, keepdims=True) + NORM_EPS)
    hhat = h * r2
    ha = plane_gather(hhat.astype(BF16), split)
    (up_part,) = to_columns(up_weight, g2, None, ha)
    w_up = along_z(up_part)
    ca = plane_gather(cot, split, up_part)
    gate = dot_nn(ha, w_gate)
    sig = jax.nn.sigmoid(gate)
    silu = gate * sig
    d_mid = dot_nn(ca, w_down)
    dub = (d_mid * silu).astype(BF16)
    d_up = dot_tn(ha, dub).astype(BF16)
    w_up = tie(w_up, d_up)
    up = dot_nn(ha, w_up)
    dgb = (d_mid * up * sig * (1.0 + gate * (1.0 - sig))).astype(BF16)
    mid = (silu * up).astype(BF16)
    part_hhat = (dot_nt(dgb, w_gate) + dot_nt(dub, w_up)).astype(BF16)
    d_gate = dot_tn(ha, dgb).astype(BF16)
    up_z = sum_along_z(d_up)
    gate_z = sum_along_z(d_gate)
    d_hhat = plane_scatter(part_hhat, split, ms, d_gate)
    dh = cot.astype(F32) + r2 * (d_hhat - hhat * jnp.mean(d_hhat * hhat, -1, keepdims=True))
    da = plane_gather(dh.astype(BF16), split)
    dob = dot_nt(da, w_out).astype(BF16)

    dq, dkv_h = attn_backward(qb, kv_all, dob.reshape(qb.shape), qseg, kseg, up_z)
    dkv = core_scatter(dkv_h.reshape(2, n_plane, HEAD_DIM), gate_z)
    dqb = rotate(dq.reshape(n_plane, HEAD_DIM), cos_q, -sin_q).astype(BF16)
    dkvb = rotate(dkv, cos_k, -sin_k).astype(BF16)
    dqkv = jnp.concatenate([dqb, dkvb], 1)
    d_down = dot_tn(ca, mid).astype(BF16)
    d_qkv = dot_tn(xa, dqkv).astype(BF16)
    d_out = dot_tn(ob, da).astype(BF16)
    down_z = sum_along_z(d_down)
    out_z = sum_along_z(d_out)
    qkv_z = sum_along_z(d_qkv)
    part_xhat = dot_nt(dqkv, w_qkv).astype(BF16)
    d_xhat = plane_scatter(part_xhat, split, ms, d_down, d_qkv)
    input_grad = dh + r1 * (d_xhat - xhat * jnp.mean(d_xhat * xhat, -1, keepdims=True))
    input_grad = from_planes(unperm(input_grad).astype(BF16)).astype(F32).reshape(tokens.shape)

    up_back, up_gain = to_rows(up_z, up_weight, g2, d_xhat)
    part_out = dot_nt(mid, w_down).astype(BF16)
    result = h + plane_scatter(part_out, split, ms, up_back)
    output = from_planes(unperm(result.astype(BF16))).reshape(tokens.shape)
    gate_back, gate_gain = to_rows(gate_z, gate_weight, g2, result)

    (down_back,) = to_rows(down_z, None, None, gate_back)
    out_back = unperm(lax.ppermute(out_z, EVERY, to_owner).astype(F32))
    qkv_back, attn_gain_term = to_rows(qkv_z, wqkv_own, g1, down_back)
    qkv_back = qkv_back.reshape(rows_w, 8, -1)
    q_back = from_head(qkv_back[:, :, :HEAD_DIM])
    kv_back = from_head(qkv_back[:, :, HEAD_DIM:]).reshape(rows_w, KV_HEADS, 2, HEAD_DIM)
    k_back = kv_back[:, :, 0].reshape(rows_w, -1)
    v_back = kv_back[:, :, 1].reshape(rows_w, -1)

    return (
        output,
        input_grad,
        attn_gain_term.reshape(-1),
        q_back,
        k_back,
        v_back,
        out_back,
        (gate_gain + up_gain).reshape(-1),
        gate_back,
        up_back,
        down_back,
    )


def solution(mesh):
    dp, seq = mesh.shape["dp"], mesh.shape["seq"]
    fine = Mesh(mesh.devices.reshape(dp // 2, 2, seq // 2, 2), EVERY)
    dp_axes, seq_axes = ("x", "core"), ("z", "y")
    tok = P(None, dp_axes, seq_axes, None)
    vec, mat = P(EVERY), P(EVERY, None)
    return jax.shard_map(
        shards,
        mesh=fine,
        in_specs=(tok, P(None, dp_axes, None), vec, mat, mat, mat, mat, vec, mat, mat, mat, tok),
        out_specs=(tok, tok, vec, mat, mat, mat, mat, vec, mat, mat, mat),
        check_vma=False,
    )
```

```python
import functools
import itertools

import jax
import jax.numpy as jnp
from jax import lax
from jax.experimental import pallas as pl
from jax.experimental.pallas import tpu as pltpu
from jax.sharding import Mesh
from jax.sharding import PartitionSpec as P

HEADS = 8
KV_HEADS = 4
HEAD_DIM = 256
WINDOW = 1024
NORM_EPS = 1e-06
ROPE_BASE = 1000042.0
NEG_LARGE = -1e30
SCALE = HEAD_DIM**-0.5
PLANE = ("x", "core", "y")
EVERY = ("x", "core", "z", "y")
BF16 = jnp.bfloat16
F32 = jnp.float32
MESH = pl.DeviceIdType.MESH
GATHER_PARTS = 4
SCATTER_PARTS = 4
CORE_PARTS = 4


def dot_nn(a, b):
    return lax.dot_general(a, b, (((1,), (0,)), ((), ())), preferred_element_type=F32)


def dot_nt(a, b):
    return lax.dot_general(a, b, (((1,), (1,)), ((), ())), preferred_element_type=F32)


def dot_tn(a, b):
    return lax.dot_general(a, b, (((0,), (0,)), ((), ())), preferred_element_type=F32)


def rotate(values, cosine, sine):
    half = values.shape[-1] // 2
    a, b = values[:, :half], values[:, half:]
    return jnp.concatenate([a * cosine - b * sine, b * cosine + a * sine], -1)


def reorder(values, outer, inner):
    block = values.shape[-1] // (outer * inner)
    return jnp.concatenate(
        [
            values[..., (o * inner + i) * block : (o * inner + i + 1) * block]
            for i in range(inner)
            for o in range(outer)
        ],
        -1,
    )


QUERY_ROWS = 256


def query_blocks(seq_len):
    out = []
    for first in range(0, seq_len, QUERY_ROWS):
        low = max(0, first - WINDOW + 1) // 128 * 128
        out.append((first, low, min(seq_len, first + QUERY_ROWS)))
    return out


def masked_prob(q, k, first, low, qseg, kseg):
    scores = dot_nt(q, k) * SCALE
    qpos = first + lax.broadcasted_iota(jnp.int32, scores.shape, 0)
    kpos = low + lax.broadcasted_iota(jnp.int32, scores.shape, 1)
    allowed = (kpos <= qpos) & (qpos - kpos < WINDOW) & (qseg == kseg)
    masked = jnp.where(allowed, scores, NEG_LARGE)
    e = jnp.exp(masked - jnp.max(masked, -1, keepdims=True))
    return e / jnp.sum(e, -1, keepdims=True)


def attn_fwd_kernel(q_ref, k_ref, v_ref, qseg_ref, kseg_ref, o_ref):
    for first, low, end in query_blocks(q_ref.shape[0]):
        rows, keys = pl.ds(first, QUERY_ROWS), pl.ds(low, end - low)
        prob = masked_prob(q_ref[rows, :], k_ref[keys, :], first, low, qseg_ref[rows, :], kseg_ref[:, keys])
        o_ref[rows, :] = dot_nn(prob.astype(BF16), v_ref[keys, :]).astype(BF16)


def attn_bwd_kernel(q_ref, k_ref, v_ref, do_ref, qseg_ref, kseg_ref, *refs):
    dq_ref, dkv_ref, dk_sum, dv_sum = refs[-4:]
    dk_sum[...] = jnp.zeros_like(dk_sum)
    dv_sum[...] = jnp.zeros_like(dv_sum)
    for first, low, end in query_blocks(q_ref.shape[0]):
        rows, keys = pl.ds(first, QUERY_ROWS), pl.ds(low, end - low)
        q, k, v, do = q_ref[rows, :], k_ref[keys, :], v_ref[keys, :], do_ref[rows, :]
        prob = masked_prob(q, k, first, low, qseg_ref[rows, :], kseg_ref[:, keys])
        dprob = dot_nt(do, v)
        ds = prob * (dprob - jnp.sum(prob * dprob, -1, keepdims=True))
        dsb = ds.astype(BF16)
        dq_ref[rows, :] = dot_nn(dsb, k) * SCALE
        dk_sum[keys, :] += dot_tn(dsb, q)
        dv_sum[keys, :] += dot_tn(prob.astype(BF16), do)
    dkv_ref[0] = (dk_sum[...] * SCALE).astype(BF16)
    dkv_ref[1] = dv_sum[...].astype(BF16)


def attention_specs(seq_len):
    qspec = pl.BlockSpec((None, seq_len, HEAD_DIM), lambda s: (s, 0, 0))
    kspec = pl.BlockSpec((None, None, seq_len, HEAD_DIM), lambda s: (0, s, 0, 0))
    vspec = pl.BlockSpec((None, None, seq_len, HEAD_DIM), lambda s: (1, s, 0, 0))
    qseg = pl.BlockSpec((None, seq_len, 1), lambda s: (s, 0, 0))
    kseg = pl.BlockSpec((None, 1, seq_len), lambda s: (s, 0, 0))
    return qspec, kspec, vspec, qseg, kseg


def attn_forward(q, kv, qseg, kseg):
    seqs, seq_len, _ = q.shape
    qspec, kspec, vspec, qi, ks = attention_specs(seq_len)
    return pl.pallas_call(
        attn_fwd_kernel,
        grid=(seqs,),
        in_specs=[qspec, kspec, vspec, qi, ks],
        out_specs=qspec,
        out_shape=jax.ShapeDtypeStruct(q.shape, BF16),
        compiler_params=pltpu.CompilerParams(vmem_limit_bytes=48 << 20),
        cost_estimate=light(),
        name="attention_forward",
    )(q, kv, kv, qseg, kseg)


def attn_backward(q, kv, do, qseg, kseg, *earlier):
    seqs, seq_len, _ = q.shape
    qspec, kspec, vspec, qi, ks = attention_specs(seq_len)
    return pl.pallas_call(
        attn_bwd_kernel,
        grid=(seqs,),
        in_specs=[qspec, kspec, vspec, qspec, qi, ks] + [ANY] * len(earlier),
        out_specs=[qspec, pl.BlockSpec((2, None, seq_len, HEAD_DIM), lambda s: (0, s, 0, 0))],
        out_shape=[
            jax.ShapeDtypeStruct(q.shape, F32),
            jax.ShapeDtypeStruct((2, *q.shape), BF16),
        ],
        scratch_shapes=[pltpu.VMEM((seq_len, HEAD_DIM), F32)] * 2,
        compiler_params=pltpu.CompilerParams(vmem_limit_bytes=48 << 20),
        cost_estimate=light(),
        name="attention_backward",
    )(q, kv, kv, do, qseg, kseg, *earlier)


NUMBERS = [0]


def fresh():
    NUMBERS[0] += 1
    return NUMBERS[0] - 1


def flips():
    x, c, y = (lax.axis_index(a) for a in PLANE)
    return x, c, y, {"x": 1 - x}, {"y": 1 - y}, {"core": 1 - c}


def greet(*targets):
    barrier = pltpu.get_barrier_semaphore()
    for target in targets:
        pl.semaphore_signal(barrier, 1, device_id=target, device_id_type=MESH)
    pl.semaphore_wait(barrier, len(targets))


def pieces_at(ref, split, px, pc, py):
    return ref.at[px, :, pc, py] if split == 2 else ref.at[:, pc, px, py]


def plane_shape(split, slots, *rest):
    return (2, slots, 2, 2, *rest) if split == 2 else (slots, 2, 2, 2, *rest)


ANY = pl.BlockSpec(memory_space=pl.ANY)
WHOLE = pl.BlockSpec(memory_space=pltpu.VMEM)


def light(bytes_accessed=1024):
    return pl.CostEstimate(flops=0, bytes_accessed=bytes_accessed, transcendentals=0)


FORMS = {"nn": dot_nn, "nt": dot_nt, "tn": dot_tn}


class Matmul:
    def __init__(self, form, a, b, dtype=BF16):
        self.form, self.operands = form, [a, b]
        rows = a.shape[1] if form == "tn" else a.shape[0]
        cols = b.shape[0] if form == "nt" else b.shape[1]
        self.out = jax.ShapeDtypeStruct((rows, cols), dtype)
        self.parts = max(1, rows // 256)
        self.scratch = [
            pltpu.VMEM(a.shape, a.dtype),
            pltpu.VMEM(b.shape, b.dtype),
            pltpu.VMEM(self.out.shape, dtype),
            pltpu.SemaphoreType.DMA((2,)),
            pltpu.SemaphoreType.DMA((self.parts,)),
        ]

    def steps(self, a_ref, b_ref, o_ref, a, b, out, load_sem, store_sem):
        loads = [
            pltpu.make_async_copy(a_ref, a, load_sem.at[0]),
            pltpu.make_async_copy(b_ref, b, load_sem.at[1]),
        ]
        for load in loads:
            load.start()
        yield
        for load in loads:
            load.wait()
        step = out.shape[0] // self.parts
        stores = []
        for i in range(self.parts):
            rows = pl.ds(i * step, step)
            left = a[:, rows] if self.form == "tn" else a[rows, :]
            out[rows, :] = FORMS[self.form](left, b[...]).astype(out.dtype)
            store = pltpu.make_async_copy(out.at[rows, :], o_ref.at[rows, :], store_sem.at[i])
            store.start()
            stores.append(store)
            yield
        for store in stores:
            store.wait()


def interleave(main, side):
    for matmul in side:
        next(matmul)
    rest = itertools.chain(*side)
    for _ in main:
        next(rest, None)
    for _ in rest:
        pass


def communicate(name, steps, operands, earlier, out, scratch, matmuls, vmem, specs=None, moves=None):
    n_in = len(operands)
    n_scratch = len(scratch)
    split, back, tokens = moves or (0, False, None)
    moved = [] if moves is None else [tokens]
    side_in = [a for m in matmuls for a in m.operands]

    def kernel(*refs):
        refs = list(refs)
        ins, refs = refs[:n_in], refs[n_in:]
        before, refs = refs[: len(moved)], refs[len(moved) :]
        side_ins, refs = refs[: len(side_in)], refs[len(side_in) + len(earlier) :]
        outs, refs = refs[: 1 + len(matmuls)], refs[1 + len(matmuls) :]
        behind, refs = refs[: len(moved)], refs[len(moved) :]
        own, refs = refs[:n_scratch], refs[n_scratch:]
        finish = []

        def meet(*targets):
            if moved:
                finish.append(start_tokens(split, back, before[0], behind[0], refs[-2], refs[-1], targets))
            else:
                greet(*targets)

        side = []
        for i, m in enumerate(matmuls):
            side.append(m.steps(*side_ins[2 * i : 2 * i + 2], outs[1 + i], *refs[5 * i : 5 * i + 5]))
        interleave(steps(meet, *ins, outs[0], *own), side)
        for wait in finish:
            wait()

    shape, spec = out
    result = pl.pallas_call(
        kernel,
        out_shape=[shape] + [m.out for m in matmuls] + [jax.ShapeDtypeStruct(t.shape, t.dtype) for t in moved],
        in_specs=(specs or [ANY] * n_in) + [ANY] * (len(moved) + len(side_in) + len(earlier)),
        out_specs=[spec] + [ANY] * (len(matmuls) + len(moved)),
        scratch_shapes=scratch
        + [t for m in matmuls for t in m.scratch]
        + [pltpu.SemaphoreType.DMA((t.shape[0],)) for t in moved for _ in range(2)],
        compiler_params=pltpu.CompilerParams(
            collective_id=fresh(), has_side_effects=True, vmem_limit_bytes=vmem << 20
        ),
        cost_estimate=light(),
        name=name,
    )(*operands, *moved, *side_in, *earlier)
    return result


def gather_steps(split, prepare, meet, *refs):
    sources, (o_ref, a_ref, own_sem, send_sem, recv_sem) = refs[:-5], refs[-5:]
    x, c, y, to_x, to_y, to_c = flips()
    slots, piece, _ = a_ref.shape
    per_slot = GATHER_PARTS // slots
    step = piece // per_slot
    meet(to_x, to_y, to_c)

    def rows_of(i):
        return i // per_slot, pl.ds(i % per_slot * step, step)

    def part(px, pc, py, i):
        return pieces_at(o_ref, split, px, pc, py).at[rows_of(i)]

    def send(kind, i, src, dst, target):
        copy = pltpu.make_async_remote_copy(
            src_ref=src, dst_ref=dst, send_sem=send_sem.at[kind, i], recv_sem=recv_sem.at[kind, i],
            device_id=target, device_id_type=MESH,
        )
        copy.start()
        return copy

    copies = {}
    for i in range(GATHER_PARTS):
        a_ref[rows_of(i)] = prepare(*(source[rows_of(i)] for source in sources)).astype(BF16)
        own = a_ref.at[rows_of(i)]
        for kind, target in enumerate((to_x, to_y, to_c)):
            copies[kind, i] = send(kind, i, own, part(x, c, y, i), target)
    own_copy = pltpu.make_async_copy(a_ref, pieces_at(o_ref, split, x, c, y), own_sem)
    own_copy.start()
    yield
    src_x, src_y = jnp.where(c == 0, x, 1 - x), jnp.where(c == 0, 1 - y, y)
    dst_x, dst_y = jnp.where(c == 0, 1 - x, x), jnp.where(c == 0, y, 1 - y)
    for i in range(GATHER_PARTS):
        for kind, (px, py) in enumerate(((1 - x, y), (x, 1 - y))):
            copies[kind, i].wait_recv()
            block = part(px, c, py, i)
            copies[3 + kind, i] = send(3 + kind, i, block, block, to_c)
        block = part(src_x, c, src_y, i)
        copies[5, i] = send(5, i, block, block, {"x": dst_x, "y": dst_y})
        yield
        yield
    for i in range(GATHER_PARTS):
        copies[5, i].wait_recv()
        block = part(1 - x, c, 1 - y, i)
        copies[6, i] = send(6, i, block, block, to_c)
        yield
    for i in range(GATHER_PARTS):
        for kind in (2, 3, 4, 6):
            copies[kind, i].wait_recv()
    own_copy.wait()
    for i in range(GATHER_PARTS):
        for kind in range(7):
            copies[kind, i].wait_send()


def plane_gather(sources, prepare, split, *earlier, matmuls=()):
    slots, piece, width = sources[0].shape
    out = jax.ShapeDtypeStruct(plane_shape(split, slots, piece, width), BF16)
    scratch = [
        pltpu.VMEM((slots, piece, width), BF16),
        pltpu.SemaphoreType.DMA,
        pltpu.SemaphoreType.DMA((7, GATHER_PARTS)),
        pltpu.SemaphoreType.DMA((7, GATHER_PARTS)),
    ]
    result = communicate(
        "plane_gather", functools.partial(gather_steps, split, prepare), list(sources), earlier, (out, ANY), scratch,
        matmuls, 40 if matmuls else 16, [WHOLE] * len(sources),
    )
    got = result[0].reshape(-1, width)
    return (got, *result[1:]) if matmuls else got


def scatter_steps(split, forms, finish, n_sources, meet, *refs):
    n = len(forms)
    hbm, refs = refs[: 2 * n], refs[2 * n :]
    sources, refs = refs[:n_sources], refs[n_sources:]
    o_ref, refs = refs[0], refs[1:]
    held, refs = refs[: 2 * n], refs[2 * n :]
    own, put_c, got_c, put_x, put_y, got_x, got_y, fin_x, fin_y, end_x, end_y, load_sem, send_sem, recv_sem = refs
    x, c, y, to_x, to_y, to_c = flips()
    parts, _, _, step, width = own.shape
    slots = o_ref.shape[0]
    per_slot = parts // slots
    half = width // 2
    left, right = pl.ds(0, half), pl.ds(half, half)
    loads = [pltpu.make_async_copy(of, to, load_sem.at[i]) for i, (of, to) in enumerate(zip(hbm, held))]
    for load in loads:
        load.start()
    meet(to_x, to_y, to_c)
    for load in loads:
        load.wait()

    def rows_of(i):
        return i // per_slot, pl.ds(i % per_slot * step, step)

    def partial_sums(pc, i, columns):
        slot, rows = rows_of(i)
        total = None
        for form, a, b in zip(forms, held[::2], held[1::2]):
            if split == 2:
                block = a[:, slot, pc, :, rows, :]
            else:
                block = a[slot, pc, :, :, rows, :]
            block = block.reshape(4 * step, block.shape[-1])
            term = dot_nn(block, b[:, columns]) if form == "nn" else dot_nt(block, b[columns, :])
            total = term if total is None else total + term
        return total.astype(BF16).reshape(2, 2, step, half)

    def send(kind, i, src, dst, target):
        copy = pltpu.make_async_remote_copy(
            src_ref=src.at[i], dst_ref=dst.at[i], send_sem=send_sem.at[kind, i], recv_sem=recv_sem.at[kind, i],
            device_id=target, device_id_type=MESH,
        )
        copy.start()
        return copy

    def f32(ref, *index):
        return ref[index].astype(F32)

    first, second, third = [], [], []

    def along_first_axis(i):
        first[i].wait_recv()
        for j in range(2):
            put_x[i, j] = (f32(own, i, 1 - x, j, slice(None), left) + f32(got_c, i, 1 - x, j, slice(None), left)).astype(BF16)
            put_y[i, j] = (f32(own, i, j, 1 - y, slice(None), right) + f32(got_c, i, j, 1 - y, slice(None), right)).astype(BF16)
        second.append((send(1, i, put_x, got_x, to_x), send(2, i, put_y, got_y, to_y)))

    for i in range(parts):
        for columns in (left, right):
            put_c[i, :, :, :, columns] = partial_sums(1 - c, i, columns)
        first.append(send(0, i, put_c, got_c, to_c))
        for columns in (left, right):
            own[i, :, :, :, columns] = partial_sums(c, i, columns)
        if i:
            along_first_axis(i - 1)
    along_first_axis(parts - 1)
    yield
    yield
    for i in range(parts):
        for copy in second[i]:
            copy.wait_recv()
        fin_y[i] = (
            f32(own, i, x, 1 - y, slice(None), left) + f32(got_c, i, x, 1 - y, slice(None), left) + f32(got_x, i, 1 - y)
        ).astype(BF16)
        fin_x[i] = (
            f32(own, i, 1 - x, y, slice(None), right) + f32(got_c, i, 1 - x, y, slice(None), right) + f32(got_y, i, 1 - x)
        ).astype(BF16)
        third.append((send(3, i, fin_y, end_y, to_y), send(4, i, fin_x, end_x, to_x)))
        yield
        yield
    for i in range(parts):
        for copy in third[i]:
            copy.wait_recv()
        slot, rows = rows_of(i)
        total = jnp.concatenate(
            [
                f32(own, i, x, y, slice(None), left) + f32(got_c, i, x, y, slice(None), left)
                + f32(got_x, i, y) + f32(end_y, i),
                f32(own, i, x, y, slice(None), right) + f32(got_c, i, x, y, slice(None), right)
                + f32(got_y, i, x) + f32(end_x, i),
            ],
            -1,
        )
        o_ref[slot, rows, :] = finish(total, *(source[slot, rows, :] for source in sources)).astype(o_ref.dtype)
        yield
    for i in range(parts):
        for copy in (first[i], *second[i], *third[i]):
            copy.wait_send()


def plane_scatter(products, sources, finish, dtype, split, slots, *earlier, matmuls=(), moves=None):
    forms = [form for form, _, _ in products]
    _, a, b = products[0]
    rows, width = a.shape[0] // 8, (b.shape[1] if forms[0] == "nn" else b.shape[0])
    piece = rows // slots
    n = SCATTER_PARTS
    step, half = rows // n, width // 2
    operands = []
    for _, a, b in products:
        operands += [a.reshape(plane_shape(split, slots, piece, a.shape[1])), b]
    whole, two, one = (
        pltpu.VMEM((n, 2, 2, step, width), BF16),
        pltpu.VMEM((n, 2, step, half), BF16),
        pltpu.VMEM((n, step, half), BF16),
    )
    scratch = [pltpu.VMEM(t.shape, t.dtype) for t in operands]
    scratch += [whole] * 3 + [two] * 4 + [one] * 4
    scratch += [
        pltpu.SemaphoreType.DMA((len(operands),)),
        pltpu.SemaphoreType.DMA((5, n)),
        pltpu.SemaphoreType.DMA((5, n)),
    ]
    out = jax.ShapeDtypeStruct((slots, piece, width), dtype)
    result = communicate(
        "plane_scatter", functools.partial(scatter_steps, split, forms, finish, len(sources)),
        operands + list(sources), earlier, (out, WHOLE), scratch, matmuls, 62,
        [ANY] * len(operands) + [WHOLE] * len(sources), moves,
    )
    return result if matmuls or moves else result[0]


def pair_kernel(a_ref, *refs):
    o_ref, own_sem, send_sem, recv_sem = refs[-4:]
    c = lax.axis_index("core")
    greet({"core": 1 - c})
    keep = pltpu.make_async_copy(a_ref, o_ref.at[c], own_sem)
    keep.start()
    copy = pltpu.make_async_remote_copy(
        src_ref=a_ref, dst_ref=o_ref.at[c], send_sem=send_sem, recv_sem=recv_sem,
        device_id={"core": 1 - c}, device_id_type=MESH,
    )
    copy.start()
    keep.wait()
    copy.wait()


def core_gather(a, *earlier):
    return pl.pallas_call(
        pair_kernel,
        out_shape=jax.ShapeDtypeStruct((2, *a.shape), a.dtype),
        in_specs=[WHOLE] + [ANY] * len(earlier),
        out_specs=ANY,
        scratch_shapes=[pltpu.SemaphoreType.DMA] * 3,
        compiler_params=pltpu.CompilerParams(
            collective_id=fresh(), has_side_effects=True, vmem_limit_bytes=32 << 20
        ),
        cost_estimate=light(),
        name="core_gather",
    )(a, *earlier)


def pair_sum_kernel(a_ref, *refs):
    o_ref, own, got, out, own_sem, out_sem, send_sem, recv_sem = refs[-8:]
    c = lax.axis_index("core")
    parts, step, _ = own.shape
    greet({"core": 1 - c})
    copies, loads, stores = [], [], []
    for i in range(parts):
        rows = pl.ds(i * step, step)
        copy = pltpu.make_async_remote_copy(
            src_ref=a_ref.at[1 - c, rows, :], dst_ref=got.at[i], send_sem=send_sem.at[i], recv_sem=recv_sem.at[i],
            device_id={"core": 1 - c}, device_id_type=MESH,
        )
        copy.start()
        copies.append(copy)
        load = pltpu.make_async_copy(a_ref.at[c, rows, :], own.at[i], own_sem.at[i])
        load.start()
        loads.append(load)
    for i in range(parts):
        loads[i].wait()
        copies[i].wait_recv()
        out[i] = own[i].astype(F32) + got[i].astype(F32)
        store = pltpu.make_async_copy(out.at[i], o_ref.at[pl.ds(i * step, step), :], out_sem.at[i])
        store.start()
        stores.append(store)
    for i in range(parts):
        stores[i].wait()
        copies[i].wait_send()


def core_scatter(a, *earlier):
    _, rows, width = a.shape
    n = CORE_PARTS
    return pl.pallas_call(
        pair_sum_kernel,
        out_shape=jax.ShapeDtypeStruct((rows, width), F32),
        in_specs=[ANY] * (1 + len(earlier)),
        out_specs=ANY,
        scratch_shapes=[pltpu.VMEM((n, rows // n, width), BF16)] * 2
        + [pltpu.VMEM((n, rows // n, width), F32)]
        + [pltpu.SemaphoreType.DMA((n,))] * 4,
        compiler_params=pltpu.CompilerParams(
            collective_id=fresh(), has_side_effects=True, vmem_limit_bytes=32 << 20
        ),
        cost_estimate=light(),
        name="core_scatter",
    )(a, *earlier)


def others():
    x, c, y, *_ = flips()
    out = []
    for dx, dc, dy in ((1, 0, 1), (1, 1, 1), (1, 0, 0), (0, 0, 1), (1, 1, 0), (0, 1, 1), (0, 1, 0)):
        px, pc, py = (1 - x if dx else x), (1 - c if dc else c), (1 - y if dy else y)
        out.append(((px * 2 + pc) * 2 + py, {"x": px, "core": pc, "y": py}))
    return (x * 2 + c) * 2 + y, out


def token_moves(split, ms):
    x, c, y, *_ = flips()
    z = lax.axis_index("z")
    if split == 2:
        slot, group = z // 2, z // 2
        to = [(x, z % 2, 2 * j + c) for j in range(ms)]
        of = [(x, z % 2, 2 * k + c) for k in range(ms)]
    else:
        slot, group = z // 4, z // 4
        to = [(z % 2, z // 2 % 2, (2 * j + x) * 2 + c) for j in range(ms)]
        of = [(z // 2 % 2, z % 2, 4 * k + 2 * c + x) for k in range(ms)]
    me = (x * 2 + c) * 64 + z
    places = [[{"x": px, "core": pc, "z": pz}, (px * 2 + pc) * 64 + pz != me] for px, pc, pz in to]
    sources = [[{"x": px, "core": pc, "z": pz}, (px * 2 + pc) * 64 + pz != me] for px, pc, pz in of]
    return slot, group, places, sources


def start_tokens(split, back, t_ref, o_ref, send_sem, recv_sem, targets):
    ms = t_ref.shape[0]
    slot, group, places, sources = token_moves(split, ms)
    if back:
        slot, places, sources = group, sources, places
    barrier = pltpu.get_barrier_semaphore()
    for target, remote in sources:
        @pl.when(remote)
        def _(target=target):
            pl.semaphore_signal(barrier, 1, device_id=target, device_id_type=MESH)
    for target in targets:
        pl.semaphore_signal(barrier, 1, device_id=target, device_id_type=MESH)
    count = len(targets)
    for _, remote in places:
        count = count + remote.astype(jnp.int32)
    pl.semaphore_wait(barrier, count)

    def local(j):
        return pltpu.make_async_copy(t_ref.at[j], o_ref.at[slot], recv_sem.at[slot])

    def away(j):
        return pltpu.make_async_remote_copy(
            src_ref=t_ref.at[j], dst_ref=o_ref.at[slot], send_sem=send_sem.at[j], recv_sem=recv_sem.at[slot],
            device_id=places[j][0], device_id_type=MESH,
        )

    for j in range(ms):
        pl.when(places[j][1])(lambda j=j: away(j).start())
        pl.when(jnp.logical_not(places[j][1]))(lambda j=j: local(j).start())

    def finish():
        for k in range(ms):
            pltpu.make_async_copy(t_ref.at[0], o_ref.at[k], recv_sem.at[k]).wait()
        for j in range(ms):
            pl.when(places[j][1])(lambda j=j: away(j).wait_send())

    return finish


def head_columns(px, pc, py):
    return tuple(pl.ds(pl.multiple_of(h * HEAD_DIM, HEAD_DIM), HEAD_DIM) for h in (4 * px + 2 * py + pc, 2 * px + py))


def spread_kernel(heads, with_gain, split, *refs):
    refs = list(refs)
    w_refs = [refs.pop(0) for _ in range(3 if heads else 1)]
    g_ref = refs.pop(0) if with_gain else None
    seg_ref, tok_ref = (refs.pop(0), refs.pop(0)) if split else (None, None)
    scaled, own_sem, send_sem, recv_sem, tok_send, tok_recv = refs[-6:]
    o_ref, seg_out, tok_out = refs[-9:-6] if split else (refs[-7], None, None)
    _, rows, cols = scaled.shape
    me, peers = others()
    x, c, y, *_ = flips()
    if split:
        finish = start_tokens(split, False, tok_ref, tok_out, tok_send, tok_recv, [target for _, target in peers])
    else:
        greet(*(target for _, target in peers))

    def place(p):
        return o_ref.at[pl.ds(pl.multiple_of(p * rows, rows), rows), :]

    copies = []

    def send(kind, src, dst, target):
        copy = pltpu.make_async_remote_copy(
            src_ref=src, dst_ref=dst, send_sem=send_sem.at[kind], recv_sem=recv_sem.at[kind],
            device_id=target, device_id_type=MESH,
        )
        copy.start()
        copies.append(copy)

    def columns(p):
        return pl.ds(pl.multiple_of(p * cols, cols), cols)

    def piece(p, px, pc, py):
        if heads:
            q_cols, kv_cols = head_columns(px, pc, py)
            key, value = (w[:, kv_cols].astype(F32) for w in w_refs[1:])
            scaled[p, :, :HEAD_DIM] = (w_refs[0][:, q_cols].astype(F32) * g_ref[...]).astype(BF16)
            scaled[p, :, HEAD_DIM:] = (jnp.where(pc == 0, key, value) * g_ref[...]).astype(BF16)
            return scaled.at[p]
        if with_gain:
            scaled[p] = (w_refs[0][:, columns(p)].astype(F32) * g_ref[...]).astype(BF16)
            return scaled.at[p]
        return w_refs[0].at[:, columns(p)]

    for kind, (p, target) in enumerate(peers):
        send(kind, piece(p, target["x"], target["core"], target["y"]), place(me), target)
        if split:
            send(7 + kind, seg_ref, seg_out.at[me], target)
    keeps = [pltpu.make_async_copy(piece(me, x, c, y), place(me), own_sem.at[0])]
    if split:
        keeps.append(pltpu.make_async_copy(seg_ref, seg_out.at[me], own_sem.at[1]))
    for keep in keeps:
        keep.start()
    for keep in keeps:
        keep.wait()
    for copy in copies:
        copy.wait()
    if split:
        finish()


def to_columns(weights, gain, seg, *earlier, split=0, tokens=None):
    rows = weights[0].shape[0]
    heads = len(weights) == 3
    cols = 2 * HEAD_DIM if heads else weights[0].shape[1] // 8
    operands = list(weights) + ([gain] if gain is not None else []) + ([seg, tokens] if split else [])
    ms = tokens.shape[0] if split else 1
    out_shape = [jax.ShapeDtypeStruct((8 * rows, cols), BF16)]
    if split:
        out_shape.append(jax.ShapeDtypeStruct((8, *seg.shape), seg.dtype))
        out_shape.append(jax.ShapeDtypeStruct(tokens.shape, tokens.dtype))
    return pl.pallas_call(
        functools.partial(spread_kernel, heads, gain is not None, split),
        out_shape=out_shape,
        in_specs=[WHOLE] * len(operands) + [ANY] * len(earlier),
        out_specs=[ANY] * len(out_shape),
        scratch_shapes=[
            pltpu.VMEM((8, rows, cols), BF16),
            pltpu.SemaphoreType.DMA((2,)),
            pltpu.SemaphoreType.DMA((14,)),
            pltpu.SemaphoreType.DMA((14,)),
            pltpu.SemaphoreType.DMA((ms,)),
            pltpu.SemaphoreType.DMA((ms,)),
        ],
        compiler_params=pltpu.CompilerParams(collective_id=fresh(), has_side_effects=True),
        cost_estimate=light(),
        name="weight_columns",
    )(*operands, *earlier)


class Rows:
    def __init__(self, part, weights=(), gain=None):
        self.cols, rows = part.shape[1], part.shape[0] // 8
        self.heads, self.scaled = len(weights) == 3, gain is not None
        self.operands = [part, *weights] + ([gain] if self.scaled else [])
        widths = [w.shape[1] for w in weights] if self.heads else [8 * self.cols]
        self.out = [jax.ShapeDtypeStruct((rows, n), F32) for n in widths + ([1] if self.scaled else [])]
        self.scratch = [
            pltpu.VMEM((8, rows, self.cols), BF16),
            pltpu.SemaphoreType.DMA,
            pltpu.SemaphoreType.DMA((7,)),
            pltpu.SemaphoreType.DMA((7,)),
        ]

    def start(self, me, peers, p_ref, got, own_sem, send_sem, recv_sem):
        rows = got.shape[1]

        def block(p):
            return p_ref.at[pl.ds(pl.multiple_of(p * rows, rows), rows), :]

        copies = []
        for kind, (p, target) in enumerate(peers):
            copy = pltpu.make_async_remote_copy(
                src_ref=block(p), dst_ref=got.at[me], send_sem=send_sem.at[kind], recv_sem=recv_sem.at[kind],
                device_id=target, device_id_type=MESH,
            )
            copy.start()
            copies.append(copy)
        keep = pltpu.make_async_copy(block(me), got.at[me], own_sem)
        keep.start()
        return copies, keep

    def store(self, p, place, got, ins, outs, total):
        grad = got[p].astype(F32)
        if self.heads:
            q_cols, kv_cols = head_columns(*place)
            wq, wk, wv, gain = ins
            q_out, k_out, v_out, _ = outs
            for_q, for_kv = grad[:, :HEAD_DIM], grad[:, HEAD_DIM:]
            is_key = place[1] == 0
            w_kv = jnp.where(is_key, wk[:, kv_cols].astype(F32), wv[:, kv_cols].astype(F32))
            q_out[:, q_cols] = for_q * gain[...]

            @pl.when(is_key)
            def _():
                k_out[:, kv_cols] = for_kv * gain[...]

            @pl.when(jnp.logical_not(is_key))
            def _():
                v_out[:, kv_cols] = for_kv * gain[...]

            terms = wq[:, q_cols].astype(F32) * for_q + w_kv * for_kv
            return total + jnp.sum(terms, -1, keepdims=True)
        columns = pl.ds(pl.multiple_of(p * self.cols, self.cols), self.cols)
        if self.scaled:
            total = total + jnp.sum(ins[0][:, columns].astype(F32) * grad, -1, keepdims=True)
            grad = grad * ins[1][...]
        outs[0][:, columns] = grad
        return total


def to_rows(items, *earlier, moves=None):
    split, tokens = moves or (0, None)
    moved = [tokens] if moves else []
    operands = [a for item in items for a in item.operands]
    specs = [spec for item in items for spec in [ANY] + [WHOLE] * (len(item.operands) - 1)]
    outs = [o for item in items for o in item.out]
    ms = tokens.shape[0] if moves else 1

    def kernel(*refs):
        refs = list(refs)
        ins = [[refs.pop(0) for _ in item.operands] for item in items]
        before = [refs.pop(0) for _ in moved]
        refs = refs[len(earlier) :]
        results = [[refs.pop(0) for _ in item.out] for item in items]
        behind = [refs.pop(0) for _ in moved]
        held = [[refs.pop(0) for _ in item.scratch] for item in items]
        me, peers = others()
        x, c, y, *_ = flips()
        targets = [target for _, target in peers]
        if moved:
            finish = start_tokens(split, True, before[0], behind[0], *refs, targets)
        else:
            greet(*targets)
        started = [item.start(me, peers, i[0], *h) for item, i, h in zip(items, ins, held)]
        for item, i, o, h, (copies, keep) in zip(items, ins, results, held, started):
            total = jnp.zeros((h[0].shape[1], 1), F32)
            keep.wait()
            total = item.store(me, (x, c, y), h[0], i[1:], o, total)
            for kind in (6, 2, 3, 4, 5, 0, 1):
                copies[kind].wait_recv()
                p, target = peers[kind]
                total = item.store(p, (target["x"], target["core"], target["y"]), h[0], i[1:], o, total)
            if item.scaled:
                o[-1][...] = total
        for copies, _ in started:
            for copy in copies:
                copy.wait_send()
        if moved:
            finish()

    return pl.pallas_call(
        kernel,
        out_shape=outs + [jax.ShapeDtypeStruct(t.shape, t.dtype) for t in moved],
        in_specs=specs + [ANY] * (len(moved) + len(earlier)),
        out_specs=[WHOLE] * len(outs) + [ANY] * len(moved),
        scratch_shapes=[t for item in items for t in item.scratch] + [pltpu.SemaphoreType.DMA((ms,))] * 2 * len(moved),
        compiler_params=pltpu.CompilerParams(
            collective_id=fresh(), has_side_effects=True, vmem_limit_bytes=32 << 20
        ),
        cost_estimate=light(),
        name="weight_rows",
    )(*operands, *moved, *earlier)


def tie_kernel(a_ref, *refs):
    pass


def tie(a, *earlier):
    return pl.pallas_call(
        tie_kernel,
        out_shape=jax.ShapeDtypeStruct(a.shape, a.dtype),
        in_specs=[ANY] * (1 + len(earlier)),
        out_specs=ANY,
        input_output_aliases={0: 0},
        cost_estimate=light(),
        name="tie",
    )(a, *earlier)


def along_z(part):
    return lax.all_gather(part, "z", axis=0, tiled=True)


def sum_along_z(g):
    return lax.psum_scatter(g, "z", scatter_dimension=0, tiled=True)


def shards(
    tokens,
    segments,
    attn_gain,
    query_weight,
    key_weight,
    value_weight,
    out_weight,
    ffn_gain,
    gate_weight,
    up_weight,
    down_weight,
    cotangent,
):
    NUMBERS[0] = 0
    micro, seq_local, pl_len, width = tokens.shape
    seq_len = segments.shape[2]
    ms = micro * seq_local
    rows_w = gate_weight.shape[0]
    nx, nc, nz, ny = (lax.axis_size(a) for a in EVERY)
    dp = nx * nc
    n_plane = 8 * ms * pl_len
    col_block = width // (dp * nz)
    z_index = lax.axis_index("z")
    core = lax.axis_index("core")
    split = dp * ms // nz

    def perm(a):
        lead = a.shape[:-1]
        return a.reshape(*lead, dp, nz, col_block).swapaxes(-3, -2).reshape(*lead, width)

    def unperm(a):
        lead = a.shape[:-1]
        return a.reshape(*lead, nz, dp, col_block).swapaxes(-3, -2).reshape(*lead, width)

    whole_lanes = col_block % 128 == 0

    def inward(v):
        return reorder(v, dp, nz) if whole_lanes else v

    def outward(v):
        return reorder(v, nz, dp) if whole_lanes else v

    def inside(a):
        return a if whole_lanes else perm(a)

    def outside(a):
        return a if whole_lanes else unperm(a)

    def scale_of(v):
        return lax.rsqrt(jnp.mean(v * v, -1, keepdims=True) + NORM_EPS)

    def norm_back(v, d_hat):
        scale = scale_of(v)
        hat = v * scale
        return scale * (d_hat - hat * jnp.mean(d_hat * hat, -1, keepdims=True))

    def place(x, c, z, y):
        return ((x * 2 + c) * nz + z) * 2 + y

    to_head, to_owner = [], []
    for x in range(2):
        for c in range(2):
            for y in range(2):
                head = (x * 2 + y) * 2 + c
                for k in range(nz):
                    to_head.append((head * nz + k, place(x, c, k, y)))
                    to_owner.append((place(x, c, k, y), head * nz + k))

    def pick(a, index):
        return lax.dynamic_index_in_dim(a, index, 0, keepdims=False)

    g1 = attn_gain.astype(F32)[:, None]
    g2 = ffn_gain.astype(F32)[:, None]

    wqkv = (query_weight, key_weight, value_weight)
    wqkv_part, seg_all, x = to_columns(
        wqkv, g1, segments.reshape(ms, seq_len), split=split, tokens=tokens.reshape(ms, pl_len, width)
    )
    w_qkv = along_z(wqkv_part)
    w_out = along_z(lax.ppermute(perm(out_weight), EVERY, to_head))

    seg_all = seg_all.reshape(2, 2, 2, ms, seq_len)[:, :, 0]
    if split == 2:
        seg = pick(pick(seg_all.swapaxes(0, 1), z_index % 2).swapaxes(0, 1), z_index // 2)
    else:
        seg = pick(pick(pick(seg_all, z_index // 2 % 2), z_index % 2), z_index // 4)[None]
    qseg, kseg = seg[:, :, None], seg[:, None, :]

    x = inside(x)

    def norm_in(v):
        v = inward(v.astype(F32))
        return v * scale_of(v)

    xa = plane_gather([x], norm_in, split, wqkv_part)
    (gate_part,) = to_columns([gate_weight], g2, None, xa)

    inv_freq = 1.0 / ROPE_BASE ** (jnp.arange(0, HEAD_DIM, 2, dtype=F32) / HEAD_DIM)
    angles = jnp.arange(seq_len, dtype=jnp.int32).astype(F32)[:, None] * inv_freq[None, :]
    cos_q, sin_q = (jnp.tile(t, (split, 1)) for t in (jnp.cos(angles), jnp.sin(angles)))
    cos_k = jnp.where(core == 0, cos_q, 1.0)
    sin_k = jnp.where(core == 0, sin_q, 0.0)

    qkv = dot_nn(xa, w_qkv)
    qb = rotate(qkv[:, :HEAD_DIM], cos_q, sin_q).astype(BF16).reshape(split, seq_len, HEAD_DIM)
    kvb = rotate(qkv[:, HEAD_DIM:], cos_k, sin_k).astype(BF16)
    kv_all = core_gather(kvb, gate_part).reshape(2, split, seq_len, HEAD_DIM)

    w_gate = along_z(gate_part)
    ob = attn_forward(qb, kv_all, qseg, kseg).reshape(n_plane, HEAD_DIM)
    (down_part,) = to_columns([down_weight], None, None, ob)
    w_down = along_z(down_part)
    h, cot = plane_scatter(
        [("nn", ob, w_out)], [x], lambda total, v: inward(v.astype(F32)) + total, F32, split, ms, down_part,
        moves=(split, False, cotangent.reshape(ms, pl_len, width)),
    )
    cot = inside(cot)

    ha = plane_gather([h], lambda v: v * scale_of(v), split)
    (up_part,) = to_columns([up_weight], g2, None, ha)
    w_up = along_z(up_part)
    ca, gate = plane_gather([cot], inward, split, up_part, matmuls=[Matmul("nn", ha, w_gate, F32)])
    sig = jax.nn.sigmoid(gate)
    silu = gate * sig
    d_mid = dot_nn(ca, w_down)
    dub = (d_mid * silu).astype(BF16)
    d_up = dot_tn(ha, dub).astype(BF16)
    w_up = tie(w_up, d_up)
    up = dot_nn(ha, w_up)
    dgb = (d_mid * up * sig * (1.0 + gate * (1.0 - sig))).astype(BF16)
    mid = (silu * up).astype(BF16)
    dh, d_gate = plane_scatter(
        [("nt", dgb, w_gate), ("nt", dub, w_up)],
        [h, cot],
        lambda total, v, dy: inward(dy.astype(F32)) + norm_back(v, total),
        F32, split, ms, matmuls=[Matmul("tn", ha, dgb)],
    )
    up_z = sum_along_z(d_up)
    gate_z = sum_along_z(d_gate)
    da, d_down = plane_gather([dh], lambda v: v, split, matmuls=[Matmul("tn", ca, mid)])
    dob = dot_nt(da, w_out).astype(BF16)

    dq, dkv_h = attn_backward(qb, kv_all, dob.reshape(qb.shape), qseg, kseg, up_z)
    dkv = core_scatter(dkv_h.reshape(2, n_plane, HEAD_DIM), gate_z)
    dqb = rotate(dq.reshape(n_plane, HEAD_DIM), cos_q, -sin_q).astype(BF16)
    dkvb = rotate(dkv, cos_k, -sin_k).astype(BF16)
    dqkv = jnp.concatenate([dqb, dkvb], 1)
    down_z = sum_along_z(d_down)
    input_grad, d_qkv, d_out = plane_scatter(
        [("nt", dqkv, w_qkv)],
        [x, dh],
        lambda total, v, direct: outward(direct + norm_back(inward(v.astype(F32)), total)),
        BF16, split, ms, matmuls=[Matmul("tn", xa, dqkv), Matmul("tn", ob, da)],
    )
    qkv_z = sum_along_z(d_qkv)
    out_z = sum_along_z(d_out)
    up_back, up_gain, gate_back, gate_gain, input_grad = to_rows(
        [Rows(up_z, [up_weight], g2), Rows(gate_z, [gate_weight], g2)], moves=(split, outside(input_grad))
    )
    input_grad = input_grad.astype(F32).reshape(tokens.shape)
    output = plane_scatter(
        [("nt", mid, w_down)], [h], lambda total, v: outward(v + total), BF16, split, ms, up_back, down_z
    )
    out_z = tie(out_z, output)
    down_back, output = to_rows([Rows(down_z)], moves=(split, outside(output)))
    output = output.reshape(tokens.shape)
    out_back = unperm(lax.ppermute(out_z, EVERY, to_owner).astype(F32))
    q_back, k_back, v_back, attn_gain_term = to_rows([Rows(qkv_z, wqkv, g1)], down_back, out_back)

    return (
        output,
        input_grad,
        attn_gain_term.reshape(-1),
        q_back,
        k_back,
        v_back,
        out_back,
        (gate_gain + up_gain).reshape(-1),
        gate_back,
        up_back,
        down_back,
    )


def solution(mesh):
    dp, seq = mesh.shape["dp"], mesh.shape["seq"]
    fine = Mesh(mesh.devices.reshape(dp // 2, 2, seq // 2, 2), EVERY)
    dp_axes, seq_axes = ("x", "core"), ("z", "y")
    tok = P(None, dp_axes, seq_axes, None)
    vec, mat = P(EVERY), P(EVERY, None)
    return jax.shard_map(
        shards,
        mesh=fine,
        in_specs=(tok, P(None, dp_axes, None), vec, mat, mat, mat, mat, vec, mat, mat, mat, tok),
        out_specs=(tok, tok, vec, mat, mat, mat, mat, vec, mat, mat, mat),
        check_vma=False,
    )
```

```python
import functools
import itertools

import jax
import jax.numpy as jnp
from jax import lax
from jax.experimental import pallas as pl
from jax.experimental.pallas import tpu as pltpu
from jax.sharding import Mesh
from jax.sharding import PartitionSpec as P

HEADS = 8
KV_HEADS = 4
HEAD_DIM = 256
WINDOW = 1024
NORM_EPS = 1e-06
ROPE_BASE = 1000042.0
NEG_LARGE = -1e30
SCALE = HEAD_DIM**-0.5
PLANE = ("x", "core", "y")
EVERY = ("x", "core", "z", "y")
BF16 = jnp.bfloat16
F32 = jnp.float32
MESH = pl.DeviceIdType.MESH
GATHER_PARTS = 4
SCATTER_PARTS = 4


def dot_nn(a, b):
    return lax.dot_general(a, b, (((1,), (0,)), ((), ())), preferred_element_type=F32)


def dot_nt(a, b):
    return lax.dot_general(a, b, (((1,), (1,)), ((), ())), preferred_element_type=F32)


def dot_tn(a, b):
    return lax.dot_general(a, b, (((0,), (0,)), ((), ())), preferred_element_type=F32)


def rotate(values, cosine, sine):
    half = values.shape[-1] // 2
    a, b = values[:, :half], values[:, half:]
    return jnp.concatenate([a * cosine - b * sine, b * cosine + a * sine], -1)


def reorder(values, outer, inner):
    block = values.shape[-1] // (outer * inner)
    return jnp.concatenate(
        [
            values[..., (o * inner + i) * block : (o * inner + i + 1) * block]
            for i in range(inner)
            for o in range(outer)
        ],
        -1,
    )


QUERY_ROWS = 256


def query_blocks(seq_len):
    out = []
    for first in range(0, seq_len, QUERY_ROWS):
        low = max(0, first - WINDOW + 1) // 128 * 128
        out.append((first, low, min(seq_len, first + QUERY_ROWS)))
    return out


def masked_prob(q, k, first, low, qseg, kseg):
    scores = dot_nt(q, k) * SCALE
    qpos = first + lax.broadcasted_iota(jnp.int32, scores.shape, 0)
    kpos = low + lax.broadcasted_iota(jnp.int32, scores.shape, 1)
    allowed = (kpos <= qpos) & (qpos - kpos < WINDOW) & (qseg == kseg)
    masked = jnp.where(allowed, scores, NEG_LARGE)
    e = jnp.exp(masked - jnp.max(masked, -1, keepdims=True))
    return e / jnp.sum(e, -1, keepdims=True)


def attn_fwd_kernel(q_ref, k_ref, v_ref, qseg_ref, kseg_ref, o_ref):
    for first, low, end in query_blocks(q_ref.shape[0]):
        rows, keys = pl.ds(first, QUERY_ROWS), pl.ds(low, end - low)
        prob = masked_prob(q_ref[rows, :], k_ref[keys, :], first, low, qseg_ref[rows, :], kseg_ref[:, keys])
        o_ref[rows, :] = dot_nn(prob.astype(BF16), v_ref[keys, :]).astype(BF16)


def attention_specs(seq_len):
    qspec = pl.BlockSpec((None, seq_len, HEAD_DIM), lambda s: (s, 0, 0))
    kspec = pl.BlockSpec((None, None, seq_len, HEAD_DIM), lambda s: (0, s, 0, 0))
    vspec = pl.BlockSpec((None, None, seq_len, HEAD_DIM), lambda s: (1, s, 0, 0))
    qseg = pl.BlockSpec((None, seq_len, 1), lambda s: (s, 0, 0))
    kseg = pl.BlockSpec((None, 1, seq_len), lambda s: (s, 0, 0))
    return qspec, kspec, vspec, qseg, kseg


def attn_forward(q, kv, qseg, kseg):
    seqs, seq_len, _ = q.shape
    qspec, kspec, vspec, qi, ks = attention_specs(seq_len)
    return pl.pallas_call(
        attn_fwd_kernel,
        grid=(seqs,),
        in_specs=[qspec, kspec, vspec, qi, ks],
        out_specs=qspec,
        out_shape=jax.ShapeDtypeStruct(q.shape, BF16),
        compiler_params=pltpu.CompilerParams(vmem_limit_bytes=48 << 20),
        cost_estimate=light(),
        name="attention_forward",
    )(q, kv, kv, qseg, kseg)


NUMBERS = [0]


def fresh():
    NUMBERS[0] += 1
    return NUMBERS[0] - 1


def flips():
    x, c, y = (lax.axis_index(a) for a in PLANE)
    return x, c, y, {"x": 1 - x}, {"y": 1 - y}, {"core": 1 - c}


def greet(*targets):
    join([([(target, None) for target in targets], len(targets))])


def join(parties):
    barrier = pltpu.get_barrier_semaphore()

    def signal(target):
        pl.semaphore_signal(barrier, 1, device_id=target, device_id_type=MESH)

    count = 0
    for signals, number in parties:
        for target, remote in signals:
            if remote is None:
                signal(target)
            else:
                pl.when(remote)(functools.partial(signal, target))
        count = count + number
    pl.semaphore_wait(barrier, count)


def own_place():
    x, c, z, y = (lax.axis_index(a) for a in EVERY)
    return x, c, z, y, ((x * 2 + c) * lax.axis_size("z") + z) * 2 + y


def at_place(x, c, z, y):
    me = own_place()[-1]
    return {"x": x, "core": c, "z": z, "y": y}, ((x * 2 + c) * lax.axis_size("z") + z) * 2 + y != me


def send_or_keep(src, dst, send_sem, recv_sem, target, remote):
    def away():
        return pltpu.make_async_remote_copy(
            src_ref=src, dst_ref=dst, send_sem=send_sem, recv_sem=recv_sem, device_id=target, device_id_type=MESH
        )

    pl.when(remote)(lambda: away().start())
    pl.when(jnp.logical_not(remote))(lambda: pltpu.make_async_copy(src, dst, recv_sem).start())
    return lambda: pl.when(remote)(lambda: away().wait_send())


def remotes(devices):
    return sum(remote.astype(jnp.int32) for _, remote in devices)


def pieces_at(ref, split, px, pc, py):
    return ref.at[px, :, pc, py] if split == 2 else ref.at[:, pc, px, py]


def plane_shape(split, slots, *rest):
    return (2, slots, 2, 2, *rest) if split == 2 else (slots, 2, 2, 2, *rest)


ANY = pl.BlockSpec(memory_space=pl.ANY)
WHOLE = pl.BlockSpec(memory_space=pltpu.VMEM)


def light(bytes_accessed=1024):
    return pl.CostEstimate(flops=0, bytes_accessed=bytes_accessed, transcendentals=0)


FORMS = {"nn": dot_nn, "nt": dot_nt, "tn": dot_tn}


class Matmul:
    def __init__(self, form, a, b, dtype=BF16):
        self.form, self.operands = form, [a, b]
        rows = a.shape[1] if form == "tn" else a.shape[0]
        cols = b.shape[0] if form == "nt" else b.shape[1]
        self.out = jax.ShapeDtypeStruct((rows, cols), dtype)
        self.parts = max(1, rows // 256)
        self.scratch = [
            pltpu.VMEM(a.shape, a.dtype),
            pltpu.VMEM(b.shape, b.dtype),
            pltpu.VMEM(self.out.shape, dtype),
            pltpu.SemaphoreType.DMA((2,)),
            pltpu.SemaphoreType.DMA((self.parts,)),
        ]

    def steps(self, a_ref, b_ref, o_ref, a, b, out, load_sem, store_sem):
        loads = [
            pltpu.make_async_copy(a_ref, a, load_sem.at[0]),
            pltpu.make_async_copy(b_ref, b, load_sem.at[1]),
        ]
        for load in loads:
            load.start()
        yield
        for load in loads:
            load.wait()
        step = out.shape[0] // self.parts
        stores = []
        for i in range(self.parts):
            rows = pl.ds(i * step, step)
            left = a[:, rows] if self.form == "tn" else a[rows, :]
            out[rows, :] = FORMS[self.form](left, b[...]).astype(out.dtype)
            store = pltpu.make_async_copy(out.at[rows, :], o_ref.at[rows, :], store_sem.at[i])
            store.start()
            stores.append(store)
            yield
        for store in stores:
            store.wait()


def interleave(main, side):
    for matmul in side:
        next(matmul)
    rest = itertools.chain(*side)
    for _ in main:
        next(rest, None)
    for _ in rest:
        pass


def communicate(name, steps, operands, earlier, out, scratch, matmuls, vmem, specs=None, movers=()):
    n_in = len(operands)
    n_scratch = len(scratch)
    side_in = [a for m in matmuls for a in m.operands]

    def kernel(*refs):
        refs = list(refs)
        ins, refs = refs[:n_in], refs[n_in:]
        move_ins = [[refs.pop(0) for _ in m.operands] for m in movers]
        side_ins, refs = refs[: len(side_in)], refs[len(side_in) + len(earlier) :]
        outs, refs = refs[: 1 + len(matmuls)], refs[1 + len(matmuls) :]
        move_outs = [[refs.pop(0) for _ in m.out] for m in movers]
        own, refs = refs[:n_scratch], refs[n_scratch:]
        move_held = [[refs.pop(0) for _ in m.scratch] for m in movers]
        moving = [m.begin(i, o, h) for m, i, o, h in zip(movers, move_ins, move_outs, move_held)]

        def meet(*targets):
            for m in moving:
                next(m)
            join([([(t, None) for t in targets], len(targets))] + [m.party() for m in movers])
            for m in moving:
                next(m)

        side = []
        for i, m in enumerate(matmuls):
            side.append(m.steps(*side_ins[2 * i : 2 * i + 2], outs[1 + i], *refs[5 * i : 5 * i + 5]))
        interleave(steps(meet, *ins, outs[0], *own), side)
        for m in moving:
            next(m, None)

    shape, spec = out
    move_out = [o for m in movers for o in m.out]
    return pl.pallas_call(
        kernel,
        out_shape=[shape] + [m.out for m in matmuls] + move_out,
        in_specs=(specs or [ANY] * n_in)
        + [spec for m in movers for spec in m.specs]
        + [ANY] * (len(side_in) + len(earlier)),
        out_specs=[spec] + [ANY] * len(matmuls) + [spec for m in movers for spec in m.out_specs],
        scratch_shapes=scratch + [t for m in movers for t in m.scratch] + [t for m in matmuls for t in m.scratch],
        compiler_params=pltpu.CompilerParams(
            collective_id=fresh(), has_side_effects=True, vmem_limit_bytes=vmem << 20
        ),
        cost_estimate=light(),
        name=name,
    )(*operands, *[a for m in movers for a in m.operands], *side_in, *earlier)


def gather_steps(split, prepare, meet, *refs):
    sources, (o_ref, a_ref, own_sem, send_sem, recv_sem) = refs[:-5], refs[-5:]
    x, c, y, to_x, to_y, to_c = flips()
    slots, piece, _ = a_ref.shape
    per_slot = GATHER_PARTS // slots
    step = piece // per_slot
    meet(to_x, to_y, to_c)

    def rows_of(i):
        return i // per_slot, pl.ds(i % per_slot * step, step)

    def part(px, pc, py, i):
        return pieces_at(o_ref, split, px, pc, py).at[rows_of(i)]

    def send(kind, i, src, dst, target):
        copy = pltpu.make_async_remote_copy(
            src_ref=src, dst_ref=dst, send_sem=send_sem.at[kind, i], recv_sem=recv_sem.at[kind, i],
            device_id=target, device_id_type=MESH,
        )
        copy.start()
        return copy

    copies = {}
    for i in range(GATHER_PARTS):
        a_ref[rows_of(i)] = prepare(*(source[rows_of(i)] for source in sources)).astype(BF16)
        own = a_ref.at[rows_of(i)]
        for kind, target in enumerate((to_x, to_y, to_c)):
            copies[kind, i] = send(kind, i, own, part(x, c, y, i), target)
    own_copy = pltpu.make_async_copy(a_ref, pieces_at(o_ref, split, x, c, y), own_sem)
    own_copy.start()
    yield
    src_x, src_y = jnp.where(c == 0, x, 1 - x), jnp.where(c == 0, 1 - y, y)
    dst_x, dst_y = jnp.where(c == 0, 1 - x, x), jnp.where(c == 0, y, 1 - y)
    for i in range(GATHER_PARTS):
        for kind, (px, py) in enumerate(((1 - x, y), (x, 1 - y))):
            copies[kind, i].wait_recv()
            block = part(px, c, py, i)
            copies[3 + kind, i] = send(3 + kind, i, block, block, to_c)
        block = part(src_x, c, src_y, i)
        copies[5, i] = send(5, i, block, block, {"x": dst_x, "y": dst_y})
        yield
        yield
    for i in range(GATHER_PARTS):
        copies[5, i].wait_recv()
        block = part(1 - x, c, 1 - y, i)
        copies[6, i] = send(6, i, block, block, to_c)
        yield
    for i in range(GATHER_PARTS):
        for kind in (2, 3, 4, 6):
            copies[kind, i].wait_recv()
    own_copy.wait()
    for i in range(GATHER_PARTS):
        for kind in range(7):
            copies[kind, i].wait_send()


def plane_gather(sources, prepare, split, *earlier, matmuls=(), movers=()):
    slots, piece, width = sources[0].shape
    out = jax.ShapeDtypeStruct(plane_shape(split, slots, piece, width), BF16)
    scratch = [
        pltpu.VMEM((slots, piece, width), BF16),
        pltpu.SemaphoreType.DMA,
        pltpu.SemaphoreType.DMA((7, GATHER_PARTS)),
        pltpu.SemaphoreType.DMA((7, GATHER_PARTS)),
    ]
    result = communicate(
        "plane_gather", functools.partial(gather_steps, split, prepare), list(sources), earlier, (out, ANY), scratch,
        matmuls, 40 if matmuls else 16, [WHOLE] * len(sources), movers,
    )
    got = result[0].reshape(-1, width)
    return (got, *result[1:]) if matmuls or movers else got


def scatter_steps(split, forms, finish, n_sources, meet, *refs):
    n = len(forms)
    hbm, refs = refs[: 2 * n], refs[2 * n :]
    sources, refs = refs[:n_sources], refs[n_sources:]
    o_ref, refs = refs[0], refs[1:]
    held, refs = refs[: 2 * n], refs[2 * n :]
    own, put_c, got_c, put_x, put_y, got_x, got_y, fin_x, fin_y, end_x, end_y, load_sem, send_sem, recv_sem = refs
    x, c, y, to_x, to_y, to_c = flips()
    parts, _, _, step, width = own.shape
    slots = o_ref.shape[0]
    per_slot = parts // slots
    half = width // 2
    left, right = pl.ds(0, half), pl.ds(half, half)
    loads = [pltpu.make_async_copy(of, to, load_sem.at[i]) for i, (of, to) in enumerate(zip(hbm, held))]
    for load in loads:
        load.start()
    meet(to_x, to_y, to_c)
    for load in loads:
        load.wait()

    def rows_of(i):
        return i // per_slot, pl.ds(i % per_slot * step, step)

    def partial_sums(pc, i, columns):
        slot, rows = rows_of(i)
        total = None
        for form, a, b in zip(forms, held[::2], held[1::2]):
            if split == 2:
                block = a[:, slot, pc, :, rows, :]
            else:
                block = a[slot, pc, :, :, rows, :]
            block = block.reshape(4 * step, block.shape[-1])
            term = dot_nn(block, b[:, columns]) if form == "nn" else dot_nt(block, b[columns, :])
            total = term if total is None else total + term
        return total.astype(BF16).reshape(2, 2, step, half)

    def send(kind, i, src, dst, target):
        copy = pltpu.make_async_remote_copy(
            src_ref=src.at[i], dst_ref=dst.at[i], send_sem=send_sem.at[kind, i], recv_sem=recv_sem.at[kind, i],
            device_id=target, device_id_type=MESH,
        )
        copy.start()
        return copy

    def f32(ref, *index):
        return ref[index].astype(F32)

    first, second, third = [], [], []

    def along_first_axis(i):
        first[i].wait_recv()
        for j in range(2):
            put_x[i, j] = (f32(own, i, 1 - x, j, slice(None), left) + f32(got_c, i, 1 - x, j, slice(None), left)).astype(BF16)
            put_y[i, j] = (f32(own, i, j, 1 - y, slice(None), right) + f32(got_c, i, j, 1 - y, slice(None), right)).astype(BF16)
        second.append((send(1, i, put_x, got_x, to_x), send(2, i, put_y, got_y, to_y)))

    for i in range(parts):
        for columns in (left, right):
            put_c[i, :, :, :, columns] = partial_sums(1 - c, i, columns)
        first.append(send(0, i, put_c, got_c, to_c))
        for columns in (left, right):
            own[i, :, :, :, columns] = partial_sums(c, i, columns)
        if i:
            along_first_axis(i - 1)
    along_first_axis(parts - 1)
    yield
    yield
    for i in range(parts):
        for copy in second[i]:
            copy.wait_recv()
        fin_y[i] = (
            f32(own, i, x, 1 - y, slice(None), left) + f32(got_c, i, x, 1 - y, slice(None), left) + f32(got_x, i, 1 - y)
        ).astype(BF16)
        fin_x[i] = (
            f32(own, i, 1 - x, y, slice(None), right) + f32(got_c, i, 1 - x, y, slice(None), right) + f32(got_y, i, 1 - x)
        ).astype(BF16)
        third.append((send(3, i, fin_y, end_y, to_y), send(4, i, fin_x, end_x, to_x)))
        yield
        yield
    for i in range(parts):
        for copy in third[i]:
            copy.wait_recv()
        slot, rows = rows_of(i)
        total = jnp.concatenate(
            [
                f32(own, i, x, y, slice(None), left) + f32(got_c, i, x, y, slice(None), left)
                + f32(got_x, i, y) + f32(end_y, i),
                f32(own, i, x, y, slice(None), right) + f32(got_c, i, x, y, slice(None), right)
                + f32(got_y, i, x) + f32(end_x, i),
            ],
            -1,
        )
        o_ref[slot, rows, :] = finish(total, *(source[slot, rows, :] for source in sources)).astype(o_ref.dtype)
        yield
    for i in range(parts):
        for copy in (first[i], *second[i], *third[i]):
            copy.wait_send()


def plane_scatter(products, sources, finish, dtype, split, slots, *earlier, matmuls=(), movers=()):
    forms = [form for form, _, _ in products]
    _, a, b = products[0]
    rows, width = a.shape[0] // 8, (b.shape[1] if forms[0] == "nn" else b.shape[0])
    piece = rows // slots
    n = SCATTER_PARTS
    step, half = rows // n, width // 2
    operands = []
    for _, a, b in products:
        operands += [a.reshape(plane_shape(split, slots, piece, a.shape[1])), b]
    whole, two, one = (
        pltpu.VMEM((n, 2, 2, step, width), BF16),
        pltpu.VMEM((n, 2, step, half), BF16),
        pltpu.VMEM((n, step, half), BF16),
    )
    scratch = [pltpu.VMEM(t.shape, t.dtype) for t in operands]
    scratch += [whole] * 3 + [two] * 4 + [one] * 4
    scratch += [
        pltpu.SemaphoreType.DMA((len(operands),)),
        pltpu.SemaphoreType.DMA((5, n)),
        pltpu.SemaphoreType.DMA((5, n)),
    ]
    out = jax.ShapeDtypeStruct((slots, piece, width), dtype)
    result = communicate(
        "plane_scatter", functools.partial(scatter_steps, split, forms, finish, len(sources)),
        operands + list(sources), earlier, (out, WHOLE), scratch, matmuls, 62,
        [ANY] * len(operands) + [WHOLE] * len(sources), movers,
    )
    return result if matmuls or movers else result[0]


def pair_kernel(a_ref, *refs):
    o_ref, own_sem, send_sem, recv_sem = refs[-4:]
    c = lax.axis_index("core")
    greet({"core": 1 - c})
    keep = pltpu.make_async_copy(a_ref, o_ref.at[c], own_sem)
    keep.start()
    copy = pltpu.make_async_remote_copy(
        src_ref=a_ref, dst_ref=o_ref.at[c], send_sem=send_sem, recv_sem=recv_sem,
        device_id={"core": 1 - c}, device_id_type=MESH,
    )
    copy.start()
    keep.wait()
    copy.wait()


def core_gather(a, *earlier):
    return pl.pallas_call(
        pair_kernel,
        out_shape=jax.ShapeDtypeStruct((2, *a.shape), a.dtype),
        in_specs=[WHOLE] + [ANY] * len(earlier),
        out_specs=ANY,
        scratch_shapes=[pltpu.SemaphoreType.DMA] * 3,
        compiler_params=pltpu.CompilerParams(
            collective_id=fresh(), has_side_effects=True, vmem_limit_bytes=32 << 20
        ),
        cost_estimate=light(),
        name="core_gather",
    )(a, *earlier)


def others():
    x, c, y, *_ = flips()
    out = []
    for dx, dc, dy in ((1, 0, 1), (1, 1, 1), (1, 0, 0), (0, 0, 1), (1, 1, 0), (0, 1, 1), (0, 1, 0)):
        px, pc, py = (1 - x if dx else x), (1 - c if dc else c), (1 - y if dy else y)
        out.append(((px * 2 + pc) * 2 + py, {"x": px, "core": pc, "y": py}))
    return (x * 2 + c) * 2 + y, out


class TokenMoves:
    def __init__(self, tokens, split, back=False):
        self.split, self.back, self.operands = split, back, [tokens]
        self.out = [jax.ShapeDtypeStruct(tokens.shape, tokens.dtype)]
        self.specs = self.out_specs = [ANY]
        self.scratch = [pltpu.SemaphoreType.DMA((tokens.shape[0],))] * 2

    def places(self):
        ms = self.out[0].shape[0]
        x, c, z, y, _ = own_place()
        if self.split == 2:
            slot = group = z // 2
            to = [at_place(x, z % 2, 2 * j + c, y) for j in range(ms)]
            of = [at_place(x, z % 2, 2 * k + c, y) for k in range(ms)]
        else:
            slot = group = z // 4
            to = [at_place(z % 2, z // 2 % 2, (2 * j + x) * 2 + c, y) for j in range(ms)]
            of = [at_place(z // 2 % 2, z % 2, 4 * k + 2 * c + x, y) for k in range(ms)]
        return (group, of, to) if self.back else (slot, to, of)

    def party(self):
        _, to, of = self.places()
        return of, remotes(to)

    def begin(self, ins, outs, held):
        (t_ref,), (o_ref,), (send_sem, recv_sem) = ins, outs, held
        slot, to, _ = self.places()
        yield
        waits = [
            send_or_keep(t_ref.at[j], o_ref.at[slot], send_sem.at[j], recv_sem.at[slot], *place)
            for j, place in enumerate(to)
        ]
        yield
        for k in range(len(to)):
            pltpu.make_async_copy(t_ref.at[0], o_ref.at[k], recv_sem.at[k]).wait()
        for wait in waits:
            wait()


def head_device(h, z):
    return at_place(h // 4, h % 2, z, h // 2 % 2)


def head_owner(h, k):
    nz = lax.axis_size("z")
    rest = h % 2 * nz + k
    return at_place(h // 4, h // 2 % 2, rest // 2, rest % 2)


class HeadRows:
    def __init__(self, w, inward):
        rows, width = w.shape
        self.nz, self.inward, self.operands = lax.axis_size("z"), inward, [w]
        self.out = [jax.ShapeDtypeStruct((self.nz * rows, width), BF16)]
        self.specs, self.out_specs = [WHOLE], [ANY]
        self.scratch = [pltpu.VMEM((rows, width), BF16)] + [pltpu.SemaphoreType.DMA((self.nz,))] * 2

    def places(self):
        x, c, z, y, me = own_place()
        targets = [head_device(me // self.nz, t) for t in range(self.nz)]
        return targets, [head_owner(4 * x + 2 * y + c, k) for k in range(self.nz)], me % self.nz

    def party(self):
        targets, sources, _ = self.places()
        return sources, remotes(targets)

    def begin(self, ins, outs, held):
        (w_ref,), (o_ref,), (turned, send_sem, recv_sem) = ins, outs, held
        rows = turned.shape[0]
        targets, _, k = self.places()
        turned[...] = self.inward(w_ref[...])
        yield
        to = o_ref.at[pl.ds(pl.multiple_of(k * rows, rows), rows), :]
        waits = [send_or_keep(turned, to, send_sem.at[t], recv_sem.at[k], *place) for t, place in enumerate(targets)]
        yield
        for j in range(self.nz):
            pltpu.make_async_copy(turned, o_ref.at[pl.ds(j * rows, rows), :], recv_sem.at[j]).wait()
        for wait in waits:
            wait()


class HeadSums:
    def __init__(self, d):
        self.nz, self.operands = lax.axis_size("z"), [d]
        rows, width = d.shape[0] // self.nz, d.shape[1]
        self.out = [jax.ShapeDtypeStruct((rows, width), F32)]
        self.specs, self.out_specs = [ANY], [WHOLE]
        self.scratch = [pltpu.VMEM((self.nz, rows, width), BF16)] + [pltpu.SemaphoreType.DMA((self.nz,))] * 2

    def places(self):
        x, c, z, y, me = own_place()
        targets = [head_owner(4 * x + 2 * y + c, k) for k in range(self.nz)]
        return targets, [head_device(me // self.nz, t) for t in range(self.nz)], z

    def party(self):
        targets, sources, _ = self.places()
        return sources, remotes(targets)

    def begin(self, ins, outs, held):
        (d_ref,), (o_ref,), (got, send_sem, recv_sem) = ins, outs, held
        rows = got.shape[1]
        targets, _, z = self.places()
        yield
        waits = [
            send_or_keep(d_ref.at[pl.ds(k * rows, rows), :], got.at[z], send_sem.at[k], recv_sem.at[z], *place)
            for k, place in enumerate(targets)
        ]
        yield
        total = None
        for t in range(self.nz):
            pltpu.make_async_copy(d_ref.at[pl.ds(0, rows), :], got.at[t], recv_sem.at[t]).wait()
            total = got[t].astype(F32) if total is None else total + got[t].astype(F32)
        o_ref[...] = total
        for wait in waits:
            wait()


def head_columns(px, pc, py):
    return tuple(pl.ds(pl.multiple_of(h * HEAD_DIM, HEAD_DIM), HEAD_DIM) for h in (4 * px + 2 * py + pc, 2 * px + py))


class Columns:
    def __init__(self, weights, gain=None):
        rows = weights[0].shape[0]
        self.heads, self.scaled = len(weights) == 3, gain is not None
        cols = 2 * HEAD_DIM if self.heads else weights[0].shape[1] // 8
        self.operands = list(weights) + ([gain] if self.scaled else [])
        self.out = [jax.ShapeDtypeStruct((8 * rows, cols), BF16)]
        self.specs, self.out_specs = [ANY] * len(self.operands), [ANY]
        self.scratch = [
            pltpu.VMEM((8, rows, cols), BF16),
            pltpu.SemaphoreType.DMA,
            pltpu.SemaphoreType.DMA((7,)),
            pltpu.SemaphoreType.DMA((7,)),
        ]
        if self.scaled:
            self.scratch += [pltpu.VMEM(t.shape, t.dtype) for t in self.operands]
            self.scratch.append(pltpu.SemaphoreType.DMA((len(self.operands),)))

    def begin(self, ins, outs, held):
        (o_ref,), (scaled, own_sem, send_sem, recv_sem, *loaded) = outs, held
        _, rows, cols = scaled.shape
        me, peers = others()
        x, c, y, *_ = flips()
        to = o_ref.at[pl.ds(pl.multiple_of(me * rows, rows), rows), :]
        loads = [pltpu.make_async_copy(of, to_, loaded[-1].at[i]) for i, (of, to_) in enumerate(zip(ins, loaded[:-1]))]
        for load in loads:
            load.start()

        def piece(p, px, pc, py):
            if self.heads:
                wq, wk, wv, gain = loaded[:-1]
                q_cols, kv_cols = head_columns(px, pc, py)
                scaled[p, :, :HEAD_DIM] = (wq[:, q_cols].astype(F32) * gain[...]).astype(BF16)
                for_kv = jnp.where(pc == 0, wk[:, kv_cols].astype(F32), wv[:, kv_cols].astype(F32))
                scaled[p, :, HEAD_DIM:] = (for_kv * gain[...]).astype(BF16)
                return scaled.at[p]
            columns = pl.ds(pl.multiple_of(p * cols, cols), cols)
            if self.scaled:
                scaled[p] = (loaded[0][:, columns].astype(F32) * loaded[1][...]).astype(BF16)
                return scaled.at[p]
            return ins[0].at[:, columns]

        yield
        for load in loads:
            load.wait()
        copies = []
        for kind, (p, target) in enumerate(peers):
            copy = pltpu.make_async_remote_copy(
                src_ref=piece(p, target["x"], target["core"], target["y"]), dst_ref=to,
                send_sem=send_sem.at[kind], recv_sem=recv_sem.at[kind], device_id=target, device_id_type=MESH,
            )
            copy.start()
            copies.append(copy)
        keep = pltpu.make_async_copy(piece(me, x, c, y), to, own_sem)
        keep.start()
        yield
        keep.wait()
        for copy in copies:
            copy.wait()


class Segments:
    def __init__(self, seg):
        self.operands, self.out = [seg], [jax.ShapeDtypeStruct((8, *seg.shape), seg.dtype)]
        self.specs, self.out_specs = [WHOLE], [ANY]
        self.scratch = [pltpu.SemaphoreType.DMA, pltpu.SemaphoreType.DMA((7,)), pltpu.SemaphoreType.DMA((7,))]

    def begin(self, ins, outs, held):
        (seg_ref,), (o_ref,), (own_sem, send_sem, recv_sem) = ins, outs, held
        me, peers = others()
        yield
        copies = []
        for kind, (_, target) in enumerate(peers):
            copy = pltpu.make_async_remote_copy(
                src_ref=seg_ref, dst_ref=o_ref.at[me], send_sem=send_sem.at[kind], recv_sem=recv_sem.at[kind],
                device_id=target, device_id_type=MESH,
            )
            copy.start()
            copies.append(copy)
        keep = pltpu.make_async_copy(seg_ref, o_ref.at[me], own_sem)
        keep.start()
        yield
        keep.wait()
        for copy in copies:
            copy.wait()


def exchange(name, items, *earlier, movers=()):
    parts = [*movers, *items]

    def kernel(*refs):
        refs = list(refs)
        ins = [[refs.pop(0) for _ in part.operands] for part in parts]
        refs = refs[len(earlier) :]
        outs = [[refs.pop(0) for _ in part.out] for part in parts]
        held = [[refs.pop(0) for _ in part.scratch] for part in parts]
        running = [part.begin(*given) for part, *given in zip(parts, ins, outs, held)]
        for part in running:
            next(part)
        targets = [(target, None) for _, target in others()[1]]
        join([(targets, len(targets))] + [mover.party() for mover in movers])
        for part in running:
            next(part)
        for part in running:
            next(part, None)

    result = pl.pallas_call(
        kernel,
        out_shape=[o for part in parts for o in part.out],
        in_specs=[spec for part in parts for spec in part.specs] + [ANY] * len(earlier),
        out_specs=[spec for part in parts for spec in part.out_specs],
        scratch_shapes=[t for part in parts for t in part.scratch],
        compiler_params=pltpu.CompilerParams(
            collective_id=fresh(), has_side_effects=True, vmem_limit_bytes=62 << 20
        ),
        cost_estimate=light(),
        name=name,
    )(*[a for part in parts for a in part.operands], *earlier)
    return result


class Rows:
    def __init__(self, part):
        self.cols, rows = part.shape[1], part.shape[0] // 8
        self.operands, self.specs = [part], [ANY]
        self.out, self.out_specs = [jax.ShapeDtypeStruct((rows, 8 * self.cols), BF16)], [ANY]
        self.scratch = [pltpu.SemaphoreType.DMA, pltpu.SemaphoreType.DMA((7,)), pltpu.SemaphoreType.DMA((7,))]

    def begin(self, ins, outs, held):
        (p_ref,), (o_ref,), (own_sem, send_sem, recv_sem) = ins, outs, held
        rows = o_ref.shape[0]
        me, peers = others()
        to = o_ref.at[:, pl.ds(pl.multiple_of(me * self.cols, self.cols), self.cols)]

        def block(p):
            return p_ref.at[pl.ds(pl.multiple_of(p * rows, rows), rows), :]

        yield
        copies = []
        for kind, (p, target) in enumerate(peers):
            copy = pltpu.make_async_remote_copy(
                src_ref=block(p), dst_ref=to, send_sem=send_sem.at[kind], recv_sem=recv_sem.at[kind],
                device_id=target, device_id_type=MESH,
            )
            copy.start()
            copies.append(copy)
        keep = pltpu.make_async_copy(block(me), to, own_sem)
        keep.start()
        yield
        keep.wait()
        for copy in copies:
            copy.wait()


class HeadGradients:
    def __init__(self, part, widths):
        rows = part.shape[0] // 8
        self.operands, self.specs = [part], [ANY]
        self.out = [jax.ShapeDtypeStruct((rows, n), BF16) for n in widths]
        self.out_specs = [ANY] * 3
        self.scratch = [pltpu.SemaphoreType.DMA((2,)), pltpu.SemaphoreType.DMA((14,)), pltpu.SemaphoreType.DMA((14,))]

    def begin(self, ins, outs, held):
        (p_ref,), (q_out, k_out, v_out), (own_sem, send_sem, recv_sem) = ins, outs, held
        rows = q_out.shape[0]
        me, peers = others()
        x, c, y, *_ = flips()
        q_cols, kv_cols = head_columns(x, c, y)
        halves = pl.ds(0, HEAD_DIM), pl.ds(HEAD_DIM, HEAD_DIM)

        def block(p, half):
            return p_ref.at[pl.ds(pl.multiple_of(p * rows, rows), rows), halves[half]]

        def away(kind, half, to):
            p, target = peers[kind]
            return pltpu.make_async_remote_copy(
                src_ref=block(p, half), dst_ref=to,
                send_sem=send_sem.at[2 * kind + half], recv_sem=recv_sem.at[2 * kind + half],
                device_id=target, device_id_type=MESH,
            )

        q_to, k_to, v_to = q_out.at[:, q_cols], k_out.at[:, kv_cols], v_out.at[:, kv_cols]
        yield
        for kind in range(7):
            away(kind, 0, q_to).start()
            pl.when(c == 0)(lambda: away(kind, 1, k_to).start())
            pl.when(c == 1)(lambda: away(kind, 1, v_to).start())
        pltpu.make_async_copy(block(me, 0), q_to, own_sem.at[0]).start()
        pl.when(c == 0)(lambda: pltpu.make_async_copy(block(me, 1), k_to, own_sem.at[1]).start())
        pl.when(c == 1)(lambda: pltpu.make_async_copy(block(me, 1), v_to, own_sem.at[1]).start())
        yield
        for half in range(2):
            pltpu.make_async_copy(block(me, half), q_to, own_sem.at[half]).wait()
        for kind in range(7):
            for half in range(2):
                away(kind, half, q_to).wait()


class AttentionBackward:
    def __init__(self, da, w_out, q, kv, qseg, kseg, cosine, sine):
        seqs, seq_len, hd = q.shape
        self.operands = [da.reshape(seqs, seq_len, -1), w_out, q, kv, qseg, kseg, cosine, sine]
        self.specs = [ANY] * 4 + [WHOLE] * 2 + [ANY] * 2
        self.out = [jax.ShapeDtypeStruct((seqs, seq_len, 2 * hd), BF16)]
        self.out_specs = [WHOLE]
        self.loaded = (1, 2, 3, 6, 7)
        self.scratch = [pltpu.VMEM(self.operands[i].shape, self.operands[i].dtype) for i in self.loaded]
        self.scratch += [
            pltpu.SemaphoreType.DMA((len(self.loaded),)),
            pltpu.VMEM(self.operands[0].shape, BF16),
            pltpu.VMEM((seq_len, hd), F32),
            pltpu.VMEM((seq_len, hd), F32),
            pltpu.VMEM((2, seqs, seq_len, hd), BF16),
            pltpu.VMEM((seqs, seq_len, hd), BF16),
            pltpu.SemaphoreType.DMA((seqs,)),
            pltpu.SemaphoreType.DMA((seqs,)),
            pltpu.SemaphoreType.DMA((seqs,)),
        ]

    def begin(self, ins, outs, held):
        n = len(self.loaded)
        w_out, q_ref, kv_ref, cos_ref, sin_ref = copied = held[:n]
        da, dk_sum, dv_sum, dkv, got, da_sem, send_sem, recv_sem = held[n + 1 :]
        qseg_ref, kseg_ref = ins[4:6]
        (o_ref,) = outs
        c = lax.axis_index("core")
        seqs, seq_len, hd = q_ref.shape
        first_loads = [pltpu.make_async_copy(ins[i], copied[j], held[n].at[j]) for j, i in enumerate(self.loaded)]
        loads = [pltpu.make_async_copy(ins[0].at[s], da.at[s], da_sem.at[s]) for s in range(seqs)]
        for load in first_loads + loads:
            load.start()
        yield
        yield
        for load in first_loads:
            load.wait()
        copies = []
        for s, load in enumerate(loads):
            load.wait()
            dk_sum[...] = jnp.zeros_like(dk_sum)
            dv_sum[...] = jnp.zeros_like(dv_sum)
            for first, low, end in query_blocks(seq_len):
                rows, keys = pl.ds(first, QUERY_ROWS), pl.ds(low, end - low)
                q, k, v = q_ref[s, rows, :], kv_ref[0, s, keys, :], kv_ref[1, s, keys, :]
                do = dot_nt(da[s, rows, :], w_out[...]).astype(BF16)
                prob = masked_prob(q, k, first, low, qseg_ref[s, rows, :], kseg_ref[s, :, keys])
                dprob = dot_nt(do, v)
                ds = prob * (dprob - jnp.sum(prob * dprob, -1, keepdims=True))
                dsb = ds.astype(BF16)
                dq = dot_nn(dsb, k) * SCALE
                o_ref[s, rows, :hd] = rotate(dq, cos_ref[rows, :], -sin_ref[rows, :]).astype(BF16)
                dk_sum[keys, :] += dot_tn(dsb, q)
                dv_sum[keys, :] += dot_tn(prob.astype(BF16), do)
            dkv[0, s] = (dk_sum[...] * SCALE).astype(BF16)
            dkv[1, s] = dv_sum[...].astype(BF16)
            copy = pltpu.make_async_remote_copy(
                src_ref=dkv.at[1 - c, s], dst_ref=got.at[s], send_sem=send_sem.at[s], recv_sem=recv_sem.at[s],
                device_id={"core": 1 - c}, device_id_type=MESH,
            )
            copy.start()
            copies.append(copy)
        for s, copy in enumerate(copies):
            copy.wait_recv()
            total = dkv[c, s].astype(F32) + got[s].astype(F32)
            turned = rotate(total, cos_ref[...], -sin_ref[...])
            o_ref[s, :, hd:] = jnp.where(c == 0, turned, total).astype(BF16)
        for copy in copies:
            copy.wait_send()


def tie_kernel(a_ref, *refs):
    pass


def tie(a, *earlier):
    return pl.pallas_call(
        tie_kernel,
        out_shape=jax.ShapeDtypeStruct(a.shape, a.dtype),
        in_specs=[ANY] * (1 + len(earlier)),
        out_specs=ANY,
        input_output_aliases={0: 0},
        cost_estimate=light(),
        name="tie",
    )(a, *earlier)


def along_z(part):
    return lax.all_gather(part, "z", axis=0, tiled=True)


def sum_along_z(g):
    return lax.psum_scatter(g, "z", scatter_dimension=0, tiled=True)


def shards(
    tokens,
    segments,
    attn_gain,
    query_weight,
    key_weight,
    value_weight,
    out_weight,
    ffn_gain,
    gate_weight,
    up_weight,
    down_weight,
    cotangent,
):
    NUMBERS[0] = 0
    micro, seq_local, pl_len, width = tokens.shape
    seq_len = segments.shape[2]
    ms = micro * seq_local
    rows_w = gate_weight.shape[0]
    nx, nc, nz, ny = (lax.axis_size(a) for a in EVERY)
    dp = nx * nc
    n_plane = 8 * ms * pl_len
    col_block = width // (dp * nz)
    z_index = lax.axis_index("z")
    core = lax.axis_index("core")
    split = dp * ms // nz

    def perm(a):
        lead = a.shape[:-1]
        return a.reshape(*lead, dp, nz, col_block).swapaxes(-3, -2).reshape(*lead, width)

    def unperm(a):
        lead = a.shape[:-1]
        return a.reshape(*lead, nz, dp, col_block).swapaxes(-3, -2).reshape(*lead, width)

    whole_lanes = col_block % 128 == 0

    def inward(v):
        return reorder(v, dp, nz) if whole_lanes else v

    def outward(v):
        return reorder(v, nz, dp) if whole_lanes else v

    def inside(a):
        return a if whole_lanes else perm(a)

    def outside(a):
        return a if whole_lanes else unperm(a)

    def scale_of(v):
        return lax.rsqrt(jnp.mean(v * v, -1, keepdims=True) + NORM_EPS)

    def norm_back(v, d_hat):
        scale = scale_of(v)
        hat = v * scale
        return scale * (d_hat - hat * jnp.mean(d_hat * hat, -1, keepdims=True))

    def pick(a, index):
        return lax.dynamic_index_in_dim(a, index, 0, keepdims=False)

    g1 = attn_gain.astype(F32)[:, None]
    g2 = ffn_gain.astype(F32)[:, None]

    wqkv = (query_weight, key_weight, value_weight)
    x, wqkv_part, gate_part, seg_all = exchange(
        "weight_columns",
        [Columns(wqkv, g1), Columns([gate_weight], g2), Segments(segments.reshape(ms, seq_len))],
        movers=[TokenMoves(tokens.reshape(ms, pl_len, width), split)],
    )
    w_qkv = along_z(wqkv_part)

    seg_all = seg_all.reshape(2, 2, 2, ms, seq_len)[:, :, 0]
    if split == 2:
        seg = pick(pick(seg_all.swapaxes(0, 1), z_index % 2).swapaxes(0, 1), z_index // 2)
    else:
        seg = pick(pick(pick(seg_all, z_index // 2 % 2), z_index % 2), z_index // 4)[None]
    qseg, kseg = seg[:, :, None], seg[:, None, :]

    x = inside(x)

    def norm_in(v):
        v = inward(v.astype(F32))
        return v * scale_of(v)

    xa, w_out = plane_gather([x], norm_in, split, wqkv_part, movers=[HeadRows(inside(out_weight), inward)])

    inv_freq = 1.0 / ROPE_BASE ** (jnp.arange(0, HEAD_DIM, 2, dtype=F32) / HEAD_DIM)
    angles = jnp.arange(seq_len, dtype=jnp.int32).astype(F32)[:, None] * inv_freq[None, :]
    cosine, sine = jnp.cos(angles), jnp.sin(angles)
    cos_q, sin_q = (jnp.tile(t, (split, 1)) for t in (cosine, sine))
    cos_k = jnp.where(core == 0, cos_q, 1.0)
    sin_k = jnp.where(core == 0, sin_q, 0.0)

    qkv = dot_nn(xa, w_qkv)
    qb = rotate(qkv[:, :HEAD_DIM], cos_q, sin_q).astype(BF16).reshape(split, seq_len, HEAD_DIM)
    kvb = rotate(qkv[:, HEAD_DIM:], cos_k, sin_k).astype(BF16)
    kv_all = core_gather(kvb).reshape(2, split, seq_len, HEAD_DIM)

    w_gate = along_z(gate_part)
    ob = attn_forward(qb, kv_all, qseg, kseg).reshape(n_plane, HEAD_DIM)
    (down_part,) = exchange("weight_columns", [Columns([down_weight])], ob)
    w_down = along_z(down_part)
    h, cot = plane_scatter(
        [("nn", ob, w_out)], [x], lambda total, v: inward(v.astype(F32)) + total, F32, split, ms, down_part,
        movers=[TokenMoves(cotangent.reshape(ms, pl_len, width), split)],
    )
    cot = inside(cot)

    ha = plane_gather([h], lambda v: v * scale_of(v), split)
    (up_part,) = exchange("weight_columns", [Columns([up_weight], g2)], ha)
    w_up = along_z(up_part)
    ca, gate = plane_gather([cot], inward, split, up_part, matmuls=[Matmul("nn", ha, w_gate, F32)])
    sig = jax.nn.sigmoid(gate)
    silu = gate * sig
    d_mid = dot_nn(ca, w_down)
    dub = (d_mid * silu).astype(BF16)
    d_up = dot_tn(ha, dub).astype(BF16)
    w_up = tie(w_up, d_up)
    up = dot_nn(ha, w_up)
    dgb = (d_mid * up * sig * (1.0 + gate * (1.0 - sig))).astype(BF16)
    mid = (silu * up).astype(BF16)
    dh, d_gate = plane_scatter(
        [("nt", dgb, w_gate), ("nt", dub, w_up)],
        [h, cot],
        lambda total, v, dy: inward(dy.astype(F32)) + norm_back(v, total),
        F32, split, ms, matmuls=[Matmul("tn", ha, dgb)],
    )
    up_z = sum_along_z(d_up)
    gate_z = sum_along_z(d_gate)
    da, d_down = plane_gather([dh], lambda v: v, split, matmuls=[Matmul("tn", ca, mid)])

    down_z = sum_along_z(d_down)
    output = plane_scatter(
        [("nt", mid, w_down)], [h], lambda total, v: outward(v + total), BF16, split, ms, d_down
    )

    up_rows, dqkv = exchange(
        "attention_backward",
        [Rows(up_z), AttentionBackward(da, w_out, qb, kv_all, qseg, kseg, cosine, sine)],
        output,
    )
    dqkv = dqkv.reshape(n_plane, 2 * HEAD_DIM)
    input_grad, d_qkv, d_out, output = plane_scatter(
        [("nt", dqkv, w_qkv)],
        [x, dh],
        lambda total, v, direct: outward(direct + norm_back(inward(v.astype(F32)), total)),
        BF16, split, ms, gate_z, matmuls=[Matmul("tn", xa, dqkv), Matmul("tn", ob, da)],
        movers=[TokenMoves(outside(output), split, True)],
    )
    qkv_z = sum_along_z(d_qkv)
    input_grad, gate_rows, down_rows = exchange(
        "weight_rows", [Rows(gate_z), Rows(down_z)], d_qkv, movers=[TokenMoves(outside(input_grad), split, True)]
    )
    output = output.reshape(tokens.shape)
    input_grad = input_grad.astype(F32).reshape(tokens.shape)
    up_rows, gate_rows, down_back = (t.astype(F32) for t in (up_rows, gate_rows, down_rows))
    ffn_gain_term = jnp.sum(up_rows * up_weight.astype(F32) + gate_rows * gate_weight.astype(F32), -1)
    up_back, gate_back = up_rows * g2, gate_rows * g2
    out_back, *qkv_rows = exchange(
        "weight_rows", [HeadGradients(qkv_z, [w.shape[1] for w in wqkv])],
        up_back, gate_back, down_back, input_grad, ffn_gain_term,
        movers=[HeadSums(d_out)],
    )
    out_back = unperm(out_back)
    qkv_rows = [t.astype(F32) for t in qkv_rows]
    attn_gain_term = sum(jnp.sum(w.astype(F32) * g, -1) for w, g in zip(wqkv, qkv_rows))
    q_back, k_back, v_back = (t * g1 for t in qkv_rows)

    return (
        output,
        input_grad,
        attn_gain_term,
        q_back,
        k_back,
        v_back,
        out_back,
        ffn_gain_term,
        gate_back,
        up_back,
        down_back,
    )


def solution(mesh):
    dp, seq = mesh.shape["dp"], mesh.shape["seq"]
    fine = Mesh(mesh.devices.reshape(dp // 2, 2, seq // 2, 2), EVERY)
    dp_axes, seq_axes = ("x", "core"), ("z", "y")
    tok = P(None, dp_axes, seq_axes, None)
    vec, mat = P(EVERY), P(EVERY, None)
    return jax.shard_map(
        shards,
        mesh=fine,
        in_specs=(tok, P(None, dp_axes, None), vec, mat, mat, mat, mat, vec, mat, mat, mat, tok),
        out_specs=(tok, tok, vec, mat, mat, mat, mat, vec, mat, mat, mat),
        check_vma=False,
    )
```

```python
import functools
import itertools

import jax
import jax.numpy as jnp
from jax import lax
from jax.experimental import pallas as pl
from jax.experimental.pallas import tpu as pltpu
from jax.sharding import Mesh
from jax.sharding import PartitionSpec as P

HEADS = 8
KV_HEADS = 4
HEAD_DIM = 256
WINDOW = 1024
NORM_EPS = 1e-06
ROPE_BASE = 1000042.0
NEG_LARGE = -1e30
SCALE = HEAD_DIM**-0.5
PLANE = ("x", "core", "y")
EVERY = ("x", "core", "z", "y")
BF16 = jnp.bfloat16
F32 = jnp.float32
MESH = pl.DeviceIdType.MESH
GATHER_PARTS = 4
SCATTER_PARTS = 4


def dot_nn(a, b):
    return lax.dot_general(a, b, (((1,), (0,)), ((), ())), preferred_element_type=F32)


def dot_nt(a, b):
    return lax.dot_general(a, b, (((1,), (1,)), ((), ())), preferred_element_type=F32)


def dot_tn(a, b):
    return lax.dot_general(a, b, (((0,), (0,)), ((), ())), preferred_element_type=F32)


def rotate(values, cosine, sine):
    half = values.shape[-1] // 2
    a, b = values[:, :half], values[:, half:]
    return jnp.concatenate([a * cosine - b * sine, b * cosine + a * sine], -1)


def reorder(values, outer, inner):
    block = values.shape[-1] // (outer * inner)
    return jnp.concatenate(
        [
            values[..., (o * inner + i) * block : (o * inner + i + 1) * block]
            for i in range(inner)
            for o in range(outer)
        ],
        -1,
    )


QUERY_ROWS = 256


def query_blocks(seq_len):
    out = []
    for first in range(0, seq_len, QUERY_ROWS):
        low = max(0, first - WINDOW + 1) // 128 * 128
        out.append((first, low, min(seq_len, first + QUERY_ROWS)))
    return out


def masked_prob(q, k, first, low, qseg, kseg):
    scores = dot_nt(q, k) * SCALE
    qpos = first + lax.broadcasted_iota(jnp.int32, scores.shape, 0)
    kpos = low + lax.broadcasted_iota(jnp.int32, scores.shape, 1)
    allowed = (kpos <= qpos) & (qpos - kpos < WINDOW) & (qseg == kseg)
    masked = jnp.where(allowed, scores, NEG_LARGE)
    e = jnp.exp(masked - jnp.max(masked, -1, keepdims=True))
    return e / jnp.sum(e, -1, keepdims=True)


def attn_fwd_kernel(q_ref, k_ref, v_ref, qseg_ref, kseg_ref, o_ref):
    for first, low, end in query_blocks(q_ref.shape[0]):
        rows, keys = pl.ds(first, QUERY_ROWS), pl.ds(low, end - low)
        prob = masked_prob(q_ref[rows, :], k_ref[keys, :], first, low, qseg_ref[rows, :], kseg_ref[:, keys])
        o_ref[rows, :] = dot_nn(prob.astype(BF16), v_ref[keys, :]).astype(BF16)


def attention_specs(seq_len):
    qspec = pl.BlockSpec((None, seq_len, HEAD_DIM), lambda s: (s, 0, 0))
    kspec = pl.BlockSpec((None, None, seq_len, HEAD_DIM), lambda s: (0, s, 0, 0))
    vspec = pl.BlockSpec((None, None, seq_len, HEAD_DIM), lambda s: (1, s, 0, 0))
    qseg = pl.BlockSpec((None, seq_len, 1), lambda s: (s, 0, 0))
    kseg = pl.BlockSpec((None, 1, seq_len), lambda s: (s, 0, 0))
    return qspec, kspec, vspec, qseg, kseg


def attn_forward(q, kv, qseg, kseg):
    seqs, seq_len, _ = q.shape
    qspec, kspec, vspec, qi, ks = attention_specs(seq_len)
    return pl.pallas_call(
        attn_fwd_kernel,
        grid=(seqs,),
        in_specs=[qspec, kspec, vspec, qi, ks],
        out_specs=qspec,
        out_shape=jax.ShapeDtypeStruct(q.shape, BF16),
        compiler_params=pltpu.CompilerParams(vmem_limit_bytes=48 << 20),
        cost_estimate=light(),
        name="attention_forward",
    )(q, kv, kv, qseg, kseg)


NUMBERS = [0]


def fresh():
    NUMBERS[0] += 1
    return NUMBERS[0] - 1


def flips():
    x, c, y = (lax.axis_index(a) for a in PLANE)
    return x, c, y, {"x": 1 - x}, {"y": 1 - y}, {"core": 1 - c}


def greet(*targets):
    join([([(target, None) for target in targets], len(targets))])


def join(parties):
    barrier = pltpu.get_barrier_semaphore()

    def signal(target):
        pl.semaphore_signal(barrier, 1, device_id=target, device_id_type=MESH)

    count = 0
    for signals, number in parties:
        for target, remote in signals:
            if remote is None:
                signal(target)
            else:
                pl.when(remote)(functools.partial(signal, target))
        count = count + number
    pl.semaphore_wait(barrier, count)


def own_place():
    x, c, z, y = (lax.axis_index(a) for a in EVERY)
    return x, c, z, y, ((x * 2 + c) * lax.axis_size("z") + z) * 2 + y


def at_place(x, c, z, y):
    me = own_place()[-1]
    return {"x": x, "core": c, "z": z, "y": y}, ((x * 2 + c) * lax.axis_size("z") + z) * 2 + y != me


def send_or_keep(src, dst, send_sem, recv_sem, target, remote):
    def away():
        return pltpu.make_async_remote_copy(
            src_ref=src, dst_ref=dst, send_sem=send_sem, recv_sem=recv_sem, device_id=target, device_id_type=MESH
        )

    pl.when(remote)(lambda: away().start())
    pl.when(jnp.logical_not(remote))(lambda: pltpu.make_async_copy(src, dst, recv_sem).start())
    return lambda: pl.when(remote)(lambda: away().wait_send())


def remotes(devices):
    return sum(remote.astype(jnp.int32) for _, remote in devices)


def pieces_at(ref, split, px, pc, py):
    return ref.at[px, :, pc, py] if split == 2 else ref.at[:, pc, px, py]


def plane_shape(split, slots, *rest):
    return (2, slots, 2, 2, *rest) if split == 2 else (slots, 2, 2, 2, *rest)


ANY = pl.BlockSpec(memory_space=pl.ANY)
WHOLE = pl.BlockSpec(memory_space=pltpu.VMEM)


def light(bytes_accessed=1024):
    return pl.CostEstimate(flops=0, bytes_accessed=bytes_accessed, transcendentals=0)


FORMS = {"nn": dot_nn, "nt": dot_nt, "tn": dot_tn}


class Matmul:
    def __init__(self, form, a, b, dtype=BF16):
        self.form, self.operands = form, [a, b]
        rows = a.shape[1] if form == "tn" else a.shape[0]
        cols = b.shape[0] if form == "nt" else b.shape[1]
        self.out = jax.ShapeDtypeStruct((rows, cols), dtype)
        self.parts = max(1, rows // 256)
        self.scratch = [
            pltpu.VMEM(a.shape, a.dtype),
            pltpu.VMEM(b.shape, b.dtype),
            pltpu.VMEM(self.out.shape, dtype),
            pltpu.SemaphoreType.DMA((2,)),
            pltpu.SemaphoreType.DMA((self.parts,)),
        ]

    def steps(self, a_ref, b_ref, o_ref, a, b, out, load_sem, store_sem):
        loads = [
            pltpu.make_async_copy(a_ref, a, load_sem.at[0]),
            pltpu.make_async_copy(b_ref, b, load_sem.at[1]),
        ]
        for load in loads:
            load.start()
        yield
        for load in loads:
            load.wait()
        step = out.shape[0] // self.parts
        stores = []
        for i in range(self.parts):
            rows = pl.ds(i * step, step)
            left = a[:, rows] if self.form == "tn" else a[rows, :]
            out[rows, :] = FORMS[self.form](left, b[...]).astype(out.dtype)
            store = pltpu.make_async_copy(out.at[rows, :], o_ref.at[rows, :], store_sem.at[i])
            store.start()
            stores.append(store)
            yield
        for store in stores:
            store.wait()


def interleave(main, side):
    for matmul in side:
        next(matmul)
    rest = itertools.chain(*side)
    for _ in main:
        next(rest, None)
    for _ in rest:
        pass


def communicate(name, steps, operands, earlier, out, scratch, matmuls, vmem, specs=None, movers=()):
    n_in = len(operands)
    n_scratch = len(scratch)
    side_in = [a for m in matmuls for a in m.operands]

    def kernel(*refs):
        refs = list(refs)
        ins, refs = refs[:n_in], refs[n_in:]
        move_ins = [[refs.pop(0) for _ in m.operands] for m in movers]
        side_ins, refs = refs[: len(side_in)], refs[len(side_in) + len(earlier) :]
        outs, refs = refs[: 1 + len(matmuls)], refs[1 + len(matmuls) :]
        move_outs = [[refs.pop(0) for _ in m.out] for m in movers]
        own, refs = refs[:n_scratch], refs[n_scratch:]
        move_held = [[refs.pop(0) for _ in m.scratch] for m in movers]
        moving = [m.begin(i, o, h) for m, i, o, h in zip(movers, move_ins, move_outs, move_held)]

        def meet(*targets):
            for m in moving:
                next(m)
            join([([(t, None) for t in targets], len(targets))] + [m.party() for m in movers])
            for m in moving:
                next(m)

        side = []
        for i, m in enumerate(matmuls):
            side.append(m.steps(*side_ins[2 * i : 2 * i + 2], outs[1 + i], *refs[5 * i : 5 * i + 5]))
        interleave(steps(meet, *ins, outs[0], *own), side)
        for m in moving:
            next(m, None)

    shape, spec = out
    move_out = [o for m in movers for o in m.out]
    return pl.pallas_call(
        kernel,
        out_shape=[shape] + [m.out for m in matmuls] + move_out,
        in_specs=(specs or [ANY] * n_in)
        + [spec for m in movers for spec in m.specs]
        + [ANY] * (len(side_in) + len(earlier)),
        out_specs=[spec] + [ANY] * len(matmuls) + [spec for m in movers for spec in m.out_specs],
        scratch_shapes=scratch + [t for m in movers for t in m.scratch] + [t for m in matmuls for t in m.scratch],
        compiler_params=pltpu.CompilerParams(
            collective_id=fresh(), has_side_effects=True, vmem_limit_bytes=vmem << 20
        ),
        cost_estimate=light(),
        name=name,
    )(*operands, *[a for m in movers for a in m.operands], *side_in, *earlier)


def gather_steps(split, prepare, meet, *refs):
    sources, (o_ref, a_ref, own_sem, send_sem, recv_sem) = refs[:-5], refs[-5:]
    x, c, y, to_x, to_y, to_c = flips()
    slots, piece, _ = a_ref.shape
    per_slot = GATHER_PARTS // slots
    step = piece // per_slot
    meet(to_x, to_y, to_c)

    def rows_of(i):
        return i // per_slot, pl.ds(i % per_slot * step, step)

    def part(px, pc, py, i):
        return pieces_at(o_ref, split, px, pc, py).at[rows_of(i)]

    def send(kind, i, src, dst, target):
        copy = pltpu.make_async_remote_copy(
            src_ref=src, dst_ref=dst, send_sem=send_sem.at[kind, i], recv_sem=recv_sem.at[kind, i],
            device_id=target, device_id_type=MESH,
        )
        copy.start()
        return copy

    copies = {}
    for i in range(GATHER_PARTS):
        a_ref[rows_of(i)] = prepare(*(source[rows_of(i)] for source in sources)).astype(BF16)
        own = a_ref.at[rows_of(i)]
        for kind, target in enumerate((to_x, to_y, to_c)):
            copies[kind, i] = send(kind, i, own, part(x, c, y, i), target)
    own_copy = pltpu.make_async_copy(a_ref, pieces_at(o_ref, split, x, c, y), own_sem)
    own_copy.start()
    yield
    src_x, src_y = jnp.where(c == 0, x, 1 - x), jnp.where(c == 0, 1 - y, y)
    dst_x, dst_y = jnp.where(c == 0, 1 - x, x), jnp.where(c == 0, y, 1 - y)
    for i in range(GATHER_PARTS):
        for kind, (px, py) in enumerate(((1 - x, y), (x, 1 - y))):
            copies[kind, i].wait_recv()
            block = part(px, c, py, i)
            copies[3 + kind, i] = send(3 + kind, i, block, block, to_c)
        block = part(src_x, c, src_y, i)
        copies[5, i] = send(5, i, block, block, {"x": dst_x, "y": dst_y})
        yield
        yield
    for i in range(GATHER_PARTS):
        copies[5, i].wait_recv()
        block = part(1 - x, c, 1 - y, i)
        copies[6, i] = send(6, i, block, block, to_c)
        yield
    for i in range(GATHER_PARTS):
        for kind in (2, 3, 4, 6):
            copies[kind, i].wait_recv()
    own_copy.wait()
    for i in range(GATHER_PARTS):
        for kind in range(7):
            copies[kind, i].wait_send()


def plane_gather(sources, prepare, split, *earlier, matmuls=(), movers=()):
    slots, piece, width = sources[0].shape
    out = jax.ShapeDtypeStruct(plane_shape(split, slots, piece, width), BF16)
    scratch = [
        pltpu.VMEM((slots, piece, width), BF16),
        pltpu.SemaphoreType.DMA,
        pltpu.SemaphoreType.DMA((7, GATHER_PARTS)),
        pltpu.SemaphoreType.DMA((7, GATHER_PARTS)),
    ]
    result = communicate(
        "plane_gather", functools.partial(gather_steps, split, prepare), list(sources), earlier, (out, ANY), scratch,
        matmuls, 40 if matmuls else 16, [WHOLE] * len(sources), movers,
    )
    got = result[0].reshape(-1, width)
    return (got, *result[1:]) if matmuls or movers else got


def scatter_steps(split, forms, finish, n_sources, meet, *refs):
    n = len(forms)
    hbm, refs = refs[: 2 * n], refs[2 * n :]
    sources, refs = refs[:n_sources], refs[n_sources:]
    o_ref, refs = refs[0], refs[1:]
    held, refs = refs[: 2 * n], refs[2 * n :]
    own, put_c, got_c, put_x, put_y, got_x, got_y, fin_x, fin_y, end_x, end_y, load_sem, send_sem, recv_sem = refs
    x, c, y, to_x, to_y, to_c = flips()
    parts, _, _, step, width = own.shape
    slots = o_ref.shape[0]
    per_slot = parts // slots
    half = width // 2
    left, right = pl.ds(0, half), pl.ds(half, half)
    loads = [pltpu.make_async_copy(of, to, load_sem.at[i]) for i, (of, to) in enumerate(zip(hbm, held))]
    for load in loads:
        load.start()
    meet(to_x, to_y, to_c)
    for load in loads:
        load.wait()

    def rows_of(i):
        return i // per_slot, pl.ds(i % per_slot * step, step)

    def partial_sums(pc, i, columns):
        slot, rows = rows_of(i)
        total = None
        for form, a, b in zip(forms, held[::2], held[1::2]):
            if split == 2:
                block = a[:, slot, pc, :, rows, :]
            else:
                block = a[slot, pc, :, :, rows, :]
            block = block.reshape(4 * step, block.shape[-1])
            term = dot_nn(block, b[:, columns]) if form == "nn" else dot_nt(block, b[columns, :])
            total = term if total is None else total + term
        return total.astype(BF16).reshape(2, 2, step, half)

    def send(kind, i, src, dst, target):
        copy = pltpu.make_async_remote_copy(
            src_ref=src.at[i], dst_ref=dst.at[i], send_sem=send_sem.at[kind, i], recv_sem=recv_sem.at[kind, i],
            device_id=target, device_id_type=MESH,
        )
        copy.start()
        return copy

    def f32(ref, *index):
        return ref[index].astype(F32)

    first, second, third = [], [], []

    def along_first_axis(i):
        first[i].wait_recv()
        for j in range(2):
            put_x[i, j] = (f32(own, i, 1 - x, j, slice(None), left) + f32(got_c, i, 1 - x, j, slice(None), left)).astype(BF16)
            put_y[i, j] = (f32(own, i, j, 1 - y, slice(None), right) + f32(got_c, i, j, 1 - y, slice(None), right)).astype(BF16)
        second.append((send(1, i, put_x, got_x, to_x), send(2, i, put_y, got_y, to_y)))

    for i in range(parts):
        for columns in (left, right):
            put_c[i, :, :, :, columns] = partial_sums(1 - c, i, columns)
        first.append(send(0, i, put_c, got_c, to_c))
        for columns in (left, right):
            own[i, :, :, :, columns] = partial_sums(c, i, columns)
        if i:
            along_first_axis(i - 1)
    along_first_axis(parts - 1)
    yield
    yield
    for i in range(parts):
        for copy in second[i]:
            copy.wait_recv()
        fin_y[i] = (
            f32(own, i, x, 1 - y, slice(None), left) + f32(got_c, i, x, 1 - y, slice(None), left) + f32(got_x, i, 1 - y)
        ).astype(BF16)
        fin_x[i] = (
            f32(own, i, 1 - x, y, slice(None), right) + f32(got_c, i, 1 - x, y, slice(None), right) + f32(got_y, i, 1 - x)
        ).astype(BF16)
        third.append((send(3, i, fin_y, end_y, to_y), send(4, i, fin_x, end_x, to_x)))
        yield
        yield
    for i in range(parts):
        for copy in third[i]:
            copy.wait_recv()
        slot, rows = rows_of(i)
        total = jnp.concatenate(
            [
                f32(own, i, x, y, slice(None), left) + f32(got_c, i, x, y, slice(None), left)
                + f32(got_x, i, y) + f32(end_y, i),
                f32(own, i, x, y, slice(None), right) + f32(got_c, i, x, y, slice(None), right)
                + f32(got_y, i, x) + f32(end_x, i),
            ],
            -1,
        )
        o_ref[slot, rows, :] = finish(total, *(source[slot, rows, :] for source in sources)).astype(o_ref.dtype)
        yield
    for i in range(parts):
        for copy in (first[i], *second[i], *third[i]):
            copy.wait_send()


def plane_scatter(products, sources, finish, dtype, split, slots, *earlier, matmuls=(), movers=()):
    forms = [form for form, _, _ in products]
    _, a, b = products[0]
    rows, width = a.shape[0] // 8, (b.shape[1] if forms[0] == "nn" else b.shape[0])
    piece = rows // slots
    n = SCATTER_PARTS
    step, half = rows // n, width // 2
    operands = []
    for _, a, b in products:
        operands += [a.reshape(plane_shape(split, slots, piece, a.shape[1])), b]
    whole, two, one = (
        pltpu.VMEM((n, 2, 2, step, width), BF16),
        pltpu.VMEM((n, 2, step, half), BF16),
        pltpu.VMEM((n, step, half), BF16),
    )
    scratch = [pltpu.VMEM(t.shape, t.dtype) for t in operands]
    scratch += [whole] * 3 + [two] * 4 + [one] * 4
    scratch += [
        pltpu.SemaphoreType.DMA((len(operands),)),
        pltpu.SemaphoreType.DMA((5, n)),
        pltpu.SemaphoreType.DMA((5, n)),
    ]
    out = jax.ShapeDtypeStruct((slots, piece, width), dtype)
    result = communicate(
        "plane_scatter", functools.partial(scatter_steps, split, forms, finish, len(sources)),
        operands + list(sources), earlier, (out, WHOLE), scratch, matmuls, 62,
        [ANY] * len(operands) + [WHOLE] * len(sources), movers,
    )
    return result if matmuls or movers else result[0]


def pair_kernel(a_ref, *refs):
    o_ref, own_sem, send_sem, recv_sem = refs[-4:]
    c = lax.axis_index("core")
    greet({"core": 1 - c})
    keep = pltpu.make_async_copy(a_ref, o_ref.at[c], own_sem)
    keep.start()
    copy = pltpu.make_async_remote_copy(
        src_ref=a_ref, dst_ref=o_ref.at[c], send_sem=send_sem, recv_sem=recv_sem,
        device_id={"core": 1 - c}, device_id_type=MESH,
    )
    copy.start()
    keep.wait()
    copy.wait()


def core_gather(a, *earlier):
    return pl.pallas_call(
        pair_kernel,
        out_shape=jax.ShapeDtypeStruct((2, *a.shape), a.dtype),
        in_specs=[WHOLE] + [ANY] * len(earlier),
        out_specs=ANY,
        scratch_shapes=[pltpu.SemaphoreType.DMA] * 3,
        compiler_params=pltpu.CompilerParams(
            collective_id=fresh(), has_side_effects=True, vmem_limit_bytes=32 << 20
        ),
        cost_estimate=light(),
        name="core_gather",
    )(a, *earlier)


def others():
    x, c, y, *_ = flips()
    out = []
    for dx, dc, dy in ((1, 0, 1), (1, 1, 1), (1, 0, 0), (0, 0, 1), (1, 1, 0), (0, 1, 1), (0, 1, 0)):
        px, pc, py = (1 - x if dx else x), (1 - c if dc else c), (1 - y if dy else y)
        out.append(((px * 2 + pc) * 2 + py, {"x": px, "core": pc, "y": py}))
    return (x * 2 + c) * 2 + y, out


class TokenMoves:
    def __init__(self, tokens, split, back=False):
        self.split, self.back, self.operands = split, back, [tokens]
        self.out = [jax.ShapeDtypeStruct(tokens.shape, tokens.dtype)]
        self.specs = self.out_specs = [ANY]
        self.scratch = [pltpu.SemaphoreType.DMA((tokens.shape[0],))] * 2

    def places(self):
        ms = self.out[0].shape[0]
        x, c, z, y, _ = own_place()
        if self.split == 2:
            slot = group = z // 2
            to = [at_place(x, z % 2, 2 * j + c, y) for j in range(ms)]
            of = [at_place(x, z % 2, 2 * k + c, y) for k in range(ms)]
        else:
            slot = group = z // 4
            to = [at_place(z % 2, z // 2 % 2, (2 * j + x) * 2 + c, y) for j in range(ms)]
            of = [at_place(z // 2 % 2, z % 2, 4 * k + 2 * c + x, y) for k in range(ms)]
        return (group, of, to) if self.back else (slot, to, of)

    def party(self):
        _, to, of = self.places()
        return of, remotes(to)

    def begin(self, ins, outs, held):
        (t_ref,), (o_ref,), (send_sem, recv_sem) = ins, outs, held
        slot, to, _ = self.places()
        yield
        waits = [
            send_or_keep(t_ref.at[j], o_ref.at[slot], send_sem.at[j], recv_sem.at[slot], *place)
            for j, place in enumerate(to)
        ]
        yield
        for k in range(len(to)):
            pltpu.make_async_copy(t_ref.at[0], o_ref.at[k], recv_sem.at[k]).wait()
        for wait in waits:
            wait()


def head_device(h, z):
    return at_place(h // 4, h % 2, z, h // 2 % 2)


def head_owner(h, k):
    nz = lax.axis_size("z")
    rest = h % 2 * nz + k
    return at_place(h // 4, h // 2 % 2, rest // 2, rest % 2)


class HeadRows:
    def __init__(self, w, inward):
        rows, width = w.shape
        self.nz, self.inward, self.operands = lax.axis_size("z"), inward, [w]
        self.out = [jax.ShapeDtypeStruct((self.nz * rows, width), BF16)]
        self.specs, self.out_specs = [WHOLE], [ANY]
        self.scratch = [pltpu.VMEM((rows, width), BF16)] + [pltpu.SemaphoreType.DMA((self.nz,))] * 2

    def places(self):
        x, c, z, y, me = own_place()
        targets = [head_device(me // self.nz, t) for t in range(self.nz)]
        return targets, [head_owner(4 * x + 2 * y + c, k) for k in range(self.nz)], me % self.nz

    def party(self):
        targets, sources, _ = self.places()
        return sources, remotes(targets)

    def begin(self, ins, outs, held):
        (w_ref,), (o_ref,), (turned, send_sem, recv_sem) = ins, outs, held
        rows = turned.shape[0]
        targets, _, k = self.places()
        turned[...] = self.inward(w_ref[...])
        yield
        to = o_ref.at[pl.ds(pl.multiple_of(k * rows, rows), rows), :]
        waits = [send_or_keep(turned, to, send_sem.at[t], recv_sem.at[k], *place) for t, place in enumerate(targets)]
        yield
        for j in range(self.nz):
            pltpu.make_async_copy(turned, o_ref.at[pl.ds(j * rows, rows), :], recv_sem.at[j]).wait()
        for wait in waits:
            wait()


class HeadSums:
    def __init__(self, d):
        self.nz, self.operands = lax.axis_size("z"), [d]
        rows, width = d.shape[0] // self.nz, d.shape[1]
        self.out = [jax.ShapeDtypeStruct((rows, width), F32)]
        self.specs, self.out_specs = [ANY], [WHOLE]
        self.scratch = [pltpu.VMEM((self.nz, rows, width), BF16)] + [pltpu.SemaphoreType.DMA((self.nz,))] * 2

    def places(self):
        x, c, z, y, me = own_place()
        targets = [head_owner(4 * x + 2 * y + c, k) for k in range(self.nz)]
        return targets, [head_device(me // self.nz, t) for t in range(self.nz)], z

    def party(self):
        targets, sources, _ = self.places()
        return sources, remotes(targets)

    def begin(self, ins, outs, held):
        (d_ref,), (o_ref,), (got, send_sem, recv_sem) = ins, outs, held
        rows = got.shape[1]
        targets, _, z = self.places()
        yield
        waits = [
            send_or_keep(d_ref.at[pl.ds(k * rows, rows), :], got.at[z], send_sem.at[k], recv_sem.at[z], *place)
            for k, place in enumerate(targets)
        ]
        yield
        total = None
        for t in range(self.nz):
            pltpu.make_async_copy(d_ref.at[pl.ds(0, rows), :], got.at[t], recv_sem.at[t]).wait()
            total = got[t].astype(F32) if total is None else total + got[t].astype(F32)
        o_ref[...] = total
        for wait in waits:
            wait()


def head_columns(px, pc, py):
    return tuple(pl.ds(pl.multiple_of(h * HEAD_DIM, HEAD_DIM), HEAD_DIM) for h in (4 * px + 2 * py + pc, 2 * px + py))


class Columns:
    def __init__(self, weights, gain=None):
        rows = weights[0].shape[0]
        self.heads, self.scaled = len(weights) == 3, gain is not None
        cols = 2 * HEAD_DIM if self.heads else weights[0].shape[1] // 8
        self.operands = list(weights) + ([gain] if self.scaled else [])
        self.out = [jax.ShapeDtypeStruct((8 * rows, cols), BF16)]
        self.specs, self.out_specs = [ANY] * len(self.operands), [ANY]
        self.scratch = [
            pltpu.VMEM((8, rows, cols), BF16),
            pltpu.SemaphoreType.DMA,
            pltpu.SemaphoreType.DMA((7,)),
            pltpu.SemaphoreType.DMA((7,)),
        ]
        if self.scaled:
            self.scratch += [pltpu.VMEM(t.shape, t.dtype) for t in self.operands]
            self.scratch.append(pltpu.SemaphoreType.DMA((len(self.operands),)))

    def begin(self, ins, outs, held):
        (o_ref,), (scaled, own_sem, send_sem, recv_sem, *loaded) = outs, held
        _, rows, cols = scaled.shape
        me, peers = others()
        x, c, y, *_ = flips()
        to = o_ref.at[pl.ds(pl.multiple_of(me * rows, rows), rows), :]
        loads = [pltpu.make_async_copy(of, to_, loaded[-1].at[i]) for i, (of, to_) in enumerate(zip(ins, loaded[:-1]))]
        for load in loads:
            load.start()

        def piece(p, px, pc, py):
            if self.heads:
                wq, wk, wv, gain = loaded[:-1]
                q_cols, kv_cols = head_columns(px, pc, py)
                scaled[p, :, :HEAD_DIM] = (wq[:, q_cols].astype(F32) * gain[...]).astype(BF16)
                for_kv = jnp.where(pc == 0, wk[:, kv_cols].astype(F32), wv[:, kv_cols].astype(F32))
                scaled[p, :, HEAD_DIM:] = (for_kv * gain[...]).astype(BF16)
                return scaled.at[p]
            columns = pl.ds(pl.multiple_of(p * cols, cols), cols)
            if self.scaled:
                scaled[p] = (loaded[0][:, columns].astype(F32) * loaded[1][...]).astype(BF16)
                return scaled.at[p]
            return ins[0].at[:, columns]

        yield
        for load in loads:
            load.wait()
        copies = []
        for kind, (p, target) in enumerate(peers):
            copy = pltpu.make_async_remote_copy(
                src_ref=piece(p, target["x"], target["core"], target["y"]), dst_ref=to,
                send_sem=send_sem.at[kind], recv_sem=recv_sem.at[kind], device_id=target, device_id_type=MESH,
            )
            copy.start()
            copies.append(copy)
        keep = pltpu.make_async_copy(piece(me, x, c, y), to, own_sem)
        keep.start()
        yield
        keep.wait()
        for copy in copies:
            copy.wait()


class Segments:
    def __init__(self, seg):
        self.operands, self.out = [seg], [jax.ShapeDtypeStruct((8, *seg.shape), seg.dtype)]
        self.specs, self.out_specs = [WHOLE], [ANY]
        self.scratch = [pltpu.SemaphoreType.DMA, pltpu.SemaphoreType.DMA((7,)), pltpu.SemaphoreType.DMA((7,))]

    def begin(self, ins, outs, held):
        (seg_ref,), (o_ref,), (own_sem, send_sem, recv_sem) = ins, outs, held
        me, peers = others()
        yield
        copies = []
        for kind, (_, target) in enumerate(peers):
            copy = pltpu.make_async_remote_copy(
                src_ref=seg_ref, dst_ref=o_ref.at[me], send_sem=send_sem.at[kind], recv_sem=recv_sem.at[kind],
                device_id=target, device_id_type=MESH,
            )
            copy.start()
            copies.append(copy)
        keep = pltpu.make_async_copy(seg_ref, o_ref.at[me], own_sem)
        keep.start()
        yield
        keep.wait()
        for copy in copies:
            copy.wait()


def exchange(name, items, *earlier, movers=()):
    parts = [*movers, *items]

    def kernel(*refs):
        refs = list(refs)
        ins = [[refs.pop(0) for _ in part.operands] for part in parts]
        refs = refs[len(earlier) :]
        outs = [[refs.pop(0) for _ in part.out] for part in parts]
        held = [[refs.pop(0) for _ in part.scratch] for part in parts]
        running = [part.begin(*given) for part, *given in zip(parts, ins, outs, held)]
        for part in running:
            next(part)
        targets = [(target, None) for _, target in others()[1]]
        join([(targets, len(targets))] + [mover.party() for mover in movers])
        for part in running:
            next(part)
        for part in running:
            next(part, None)

    result = pl.pallas_call(
        kernel,
        out_shape=[o for part in parts for o in part.out],
        in_specs=[spec for part in parts for spec in part.specs] + [ANY] * len(earlier),
        out_specs=[spec for part in parts for spec in part.out_specs],
        scratch_shapes=[t for part in parts for t in part.scratch],
        compiler_params=pltpu.CompilerParams(
            collective_id=fresh(), has_side_effects=True, vmem_limit_bytes=62 << 20
        ),
        cost_estimate=light(),
        name=name,
    )(*[a for part in parts for a in part.operands], *earlier)
    return result


class Rows:
    def __init__(self, part):
        self.cols, rows = part.shape[1], part.shape[0] // 8
        self.operands, self.specs = [part], [ANY]
        self.out, self.out_specs = [jax.ShapeDtypeStruct((rows, 8 * self.cols), BF16)], [ANY]
        self.scratch = [pltpu.SemaphoreType.DMA, pltpu.SemaphoreType.DMA((7,)), pltpu.SemaphoreType.DMA((7,))]

    def begin(self, ins, outs, held):
        (p_ref,), (o_ref,), (own_sem, send_sem, recv_sem) = ins, outs, held
        rows = o_ref.shape[0]
        me, peers = others()
        to = o_ref.at[:, pl.ds(pl.multiple_of(me * self.cols, self.cols), self.cols)]

        def block(p):
            return p_ref.at[pl.ds(pl.multiple_of(p * rows, rows), rows), :]

        yield
        copies = []
        for kind, (p, target) in enumerate(peers):
            copy = pltpu.make_async_remote_copy(
                src_ref=block(p), dst_ref=to, send_sem=send_sem.at[kind], recv_sem=recv_sem.at[kind],
                device_id=target, device_id_type=MESH,
            )
            copy.start()
            copies.append(copy)
        keep = pltpu.make_async_copy(block(me), to, own_sem)
        keep.start()
        yield
        keep.wait()
        for copy in copies:
            copy.wait()


class HeadGradients:
    def __init__(self, part, widths):
        rows = part.shape[0] // 8
        self.operands, self.specs = [part], [ANY]
        self.out = [jax.ShapeDtypeStruct((rows, n), BF16) for n in widths]
        self.out_specs = [ANY] * 3
        self.scratch = [pltpu.SemaphoreType.DMA((2,)), pltpu.SemaphoreType.DMA((14,)), pltpu.SemaphoreType.DMA((14,))]

    def begin(self, ins, outs, held):
        (p_ref,), (q_out, k_out, v_out), (own_sem, send_sem, recv_sem) = ins, outs, held
        rows = q_out.shape[0]
        me, peers = others()
        x, c, y, *_ = flips()
        q_cols, kv_cols = head_columns(x, c, y)
        halves = pl.ds(0, HEAD_DIM), pl.ds(HEAD_DIM, HEAD_DIM)

        def block(p, half):
            return p_ref.at[pl.ds(pl.multiple_of(p * rows, rows), rows), halves[half]]

        def away(kind, half, to):
            p, target = peers[kind]
            return pltpu.make_async_remote_copy(
                src_ref=block(p, half), dst_ref=to,
                send_sem=send_sem.at[2 * kind + half], recv_sem=recv_sem.at[2 * kind + half],
                device_id=target, device_id_type=MESH,
            )

        q_to, k_to, v_to = q_out.at[:, q_cols], k_out.at[:, kv_cols], v_out.at[:, kv_cols]
        yield
        for kind in range(7):
            away(kind, 0, q_to).start()
            pl.when(c == 0)(lambda: away(kind, 1, k_to).start())
            pl.when(c == 1)(lambda: away(kind, 1, v_to).start())
        pltpu.make_async_copy(block(me, 0), q_to, own_sem.at[0]).start()
        pl.when(c == 0)(lambda: pltpu.make_async_copy(block(me, 1), k_to, own_sem.at[1]).start())
        pl.when(c == 1)(lambda: pltpu.make_async_copy(block(me, 1), v_to, own_sem.at[1]).start())
        yield
        for half in range(2):
            pltpu.make_async_copy(block(me, half), q_to, own_sem.at[half]).wait()
        for kind in range(7):
            for half in range(2):
                away(kind, half, q_to).wait()


class AttentionBackward:
    def __init__(self, da, w_out, q, kv, qseg, kseg, cosine, sine):
        seqs, seq_len, hd = q.shape
        self.operands = [da.reshape(seqs, seq_len, -1), w_out, q, kv, qseg, kseg, cosine, sine]
        self.specs = [ANY] * 4 + [WHOLE] * 2 + [ANY] * 2
        self.out = [jax.ShapeDtypeStruct((seqs, seq_len, 2 * hd), BF16)]
        self.out_specs = [WHOLE]
        self.loaded = (1, 2, 3, 6, 7)
        self.scratch = [pltpu.VMEM(self.operands[i].shape, self.operands[i].dtype) for i in self.loaded]
        self.scratch += [
            pltpu.SemaphoreType.DMA((len(self.loaded),)),
            pltpu.VMEM(self.operands[0].shape, BF16),
            pltpu.VMEM((seq_len, hd), F32),
            pltpu.VMEM((seq_len, hd), F32),
            pltpu.VMEM((2, seqs, seq_len, hd), BF16),
            pltpu.VMEM((seqs, seq_len, hd), BF16),
            pltpu.SemaphoreType.DMA((seqs,)),
            pltpu.SemaphoreType.DMA((seqs,)),
            pltpu.SemaphoreType.DMA((seqs,)),
        ]

    def begin(self, ins, outs, held):
        n = len(self.loaded)
        w_out, q_ref, kv_ref, cos_ref, sin_ref = copied = held[:n]
        da, dk_sum, dv_sum, dkv, got, da_sem, send_sem, recv_sem = held[n + 1 :]
        qseg_ref, kseg_ref = ins[4:6]
        (o_ref,) = outs
        c = lax.axis_index("core")
        seqs, seq_len, hd = q_ref.shape
        first_loads = [pltpu.make_async_copy(ins[i], copied[j], held[n].at[j]) for j, i in enumerate(self.loaded)]
        loads = [pltpu.make_async_copy(ins[0].at[s], da.at[s], da_sem.at[s]) for s in range(seqs)]
        for load in first_loads + loads:
            load.start()
        yield
        yield
        for load in first_loads:
            load.wait()
        copies = []
        for s, load in enumerate(loads):
            load.wait()
            dk_sum[...] = jnp.zeros_like(dk_sum)
            dv_sum[...] = jnp.zeros_like(dv_sum)
            for first, low, end in query_blocks(seq_len):
                rows, keys = pl.ds(first, QUERY_ROWS), pl.ds(low, end - low)
                q, k, v = q_ref[s, rows, :], kv_ref[0, s, keys, :], kv_ref[1, s, keys, :]
                do = dot_nt(da[s, rows, :], w_out[...]).astype(BF16)
                prob = masked_prob(q, k, first, low, qseg_ref[s, rows, :], kseg_ref[s, :, keys])
                dprob = dot_nt(do, v)
                ds = prob * (dprob - jnp.sum(prob * dprob, -1, keepdims=True))
                dsb = ds.astype(BF16)
                dq = dot_nn(dsb, k) * SCALE
                o_ref[s, rows, :hd] = rotate(dq, cos_ref[rows, :], -sin_ref[rows, :]).astype(BF16)
                dk_sum[keys, :] += dot_tn(dsb, q)
                dv_sum[keys, :] += dot_tn(prob.astype(BF16), do)
            dkv[0, s] = (dk_sum[...] * SCALE).astype(BF16)
            dkv[1, s] = dv_sum[...].astype(BF16)
            copy = pltpu.make_async_remote_copy(
                src_ref=dkv.at[1 - c, s], dst_ref=got.at[s], send_sem=send_sem.at[s], recv_sem=recv_sem.at[s],
                device_id={"core": 1 - c}, device_id_type=MESH,
            )
            copy.start()
            copies.append(copy)
        for s, copy in enumerate(copies):
            copy.wait_recv()
            total = dkv[c, s].astype(F32) + got[s].astype(F32)
            turned = rotate(total, cos_ref[...], -sin_ref[...])
            o_ref[s, :, hd:] = jnp.where(c == 0, turned, total).astype(BF16)
        for copy in copies:
            copy.wait_send()


def tie_kernel(a_ref, *refs):
    pass


def tie(a, *earlier):
    return pl.pallas_call(
        tie_kernel,
        out_shape=jax.ShapeDtypeStruct(a.shape, a.dtype),
        in_specs=[ANY] * (1 + len(earlier)),
        out_specs=ANY,
        input_output_aliases={0: 0},
        cost_estimate=light(),
        name="tie",
    )(a, *earlier)


def along_z(part):
    return lax.all_gather(part, "z", axis=0, tiled=True)


def sum_along_z(g):
    return lax.psum_scatter(g, "z", scatter_dimension=0, tiled=True)


def shards(
    tokens,
    segments,
    attn_gain,
    query_weight,
    key_weight,
    value_weight,
    out_weight,
    ffn_gain,
    gate_weight,
    up_weight,
    down_weight,
    cotangent,
):
    NUMBERS[0] = 0
    micro, seq_local, pl_len, width = tokens.shape
    seq_len = segments.shape[2]
    ms = micro * seq_local
    rows_w = gate_weight.shape[0]
    nx, nc, nz, ny = (lax.axis_size(a) for a in EVERY)
    dp = nx * nc
    n_plane = 8 * ms * pl_len
    col_block = width // (dp * nz)
    z_index = lax.axis_index("z")
    core = lax.axis_index("core")
    split = dp * ms // nz

    def perm(a):
        lead = a.shape[:-1]
        return a.reshape(*lead, dp, nz, col_block).swapaxes(-3, -2).reshape(*lead, width)

    def unperm(a):
        lead = a.shape[:-1]
        return a.reshape(*lead, nz, dp, col_block).swapaxes(-3, -2).reshape(*lead, width)

    whole_lanes = col_block % 128 == 0

    def inward(v):
        return reorder(v, dp, nz) if whole_lanes else v

    def outward(v):
        return reorder(v, nz, dp) if whole_lanes else v

    def inside(a):
        return a if whole_lanes else perm(a)

    def outside(a):
        return a if whole_lanes else unperm(a)

    def scale_of(v):
        return lax.rsqrt(jnp.mean(v * v, -1, keepdims=True) + NORM_EPS)

    def norm_back(v, d_hat):
        scale = scale_of(v)
        hat = v * scale
        return scale * (d_hat - hat * jnp.mean(d_hat * hat, -1, keepdims=True))

    def pick(a, index):
        return lax.dynamic_index_in_dim(a, index, 0, keepdims=False)

    g1 = attn_gain.astype(F32)[:, None]
    g2 = ffn_gain.astype(F32)[:, None]

    wqkv = (query_weight, key_weight, value_weight)
    (wqkv_part,) = exchange("weight_columns", [Columns(wqkv, g1)])
    x, gate_part, seg_all = exchange(
        "weight_columns", [Columns([gate_weight], g2), Segments(segments.reshape(ms, seq_len))], wqkv_part,
        movers=[TokenMoves(tokens.reshape(ms, pl_len, width), split)],
    )
    w_qkv = along_z(wqkv_part)

    seg_all = seg_all.reshape(2, 2, 2, ms, seq_len)[:, :, 0]
    if split == 2:
        seg = pick(pick(seg_all.swapaxes(0, 1), z_index % 2).swapaxes(0, 1), z_index // 2)
    else:
        seg = pick(pick(pick(seg_all, z_index // 2 % 2), z_index % 2), z_index // 4)[None]
    qseg, kseg = seg[:, :, None], seg[:, None, :]

    x = inside(x)

    def norm_in(v):
        v = inward(v.astype(F32))
        return v * scale_of(v)

    xa, w_out = plane_gather([x], norm_in, split, wqkv_part, movers=[HeadRows(inside(out_weight), inward)])

    inv_freq = 1.0 / ROPE_BASE ** (jnp.arange(0, HEAD_DIM, 2, dtype=F32) / HEAD_DIM)
    angles = jnp.arange(seq_len, dtype=jnp.int32).astype(F32)[:, None] * inv_freq[None, :]
    cosine, sine = jnp.cos(angles), jnp.sin(angles)
    cos_q, sin_q = (jnp.tile(t, (split, 1)) for t in (cosine, sine))
    cos_k = jnp.where(core == 0, cos_q, 1.0)
    sin_k = jnp.where(core == 0, sin_q, 0.0)

    qkv = dot_nn(xa, w_qkv)
    qb = rotate(qkv[:, :HEAD_DIM], cos_q, sin_q).astype(BF16).reshape(split, seq_len, HEAD_DIM)
    kvb = rotate(qkv[:, HEAD_DIM:], cos_k, sin_k).astype(BF16)
    kv_all = core_gather(kvb).reshape(2, split, seq_len, HEAD_DIM)

    w_gate = along_z(gate_part)
    ob = attn_forward(qb, kv_all, qseg, kseg).reshape(n_plane, HEAD_DIM)
    (down_part,) = exchange("weight_columns", [Columns([down_weight])], ob)
    w_down = along_z(down_part)
    h, cot = plane_scatter(
        [("nn", ob, w_out)], [x], lambda total, v: inward(v.astype(F32)) + total, F32, split, ms, down_part,
        movers=[TokenMoves(cotangent.reshape(ms, pl_len, width), split)],
    )
    cot = inside(cot)

    ha = plane_gather([h], lambda v: v * scale_of(v), split)
    (up_part,) = exchange("weight_columns", [Columns([up_weight], g2)], ha)
    w_up = along_z(up_part)
    ca, gate = plane_gather([cot], inward, split, up_part, matmuls=[Matmul("nn", ha, w_gate, F32)])
    sig = jax.nn.sigmoid(gate)
    silu = gate * sig
    d_mid = dot_nn(ca, w_down)
    dub = (d_mid * silu).astype(BF16)
    d_up = dot_tn(ha, dub).astype(BF16)
    w_up = tie(w_up, d_up)
    up = dot_nn(ha, w_up)
    dgb = (d_mid * up * sig * (1.0 + gate * (1.0 - sig))).astype(BF16)
    mid = (silu * up).astype(BF16)
    dh, d_gate = plane_scatter(
        [("nt", dgb, w_gate), ("nt", dub, w_up)],
        [h, cot],
        lambda total, v, dy: inward(dy.astype(F32)) + norm_back(v, total),
        F32, split, ms, matmuls=[Matmul("tn", ha, dgb)],
    )
    up_z = sum_along_z(d_up)
    gate_z = sum_along_z(d_gate)
    da, d_down = plane_gather([dh], lambda v: v, split, matmuls=[Matmul("tn", ca, mid)])

    down_z = sum_along_z(d_down)
    output = plane_scatter(
        [("nt", mid, w_down)], [h], lambda total, v: outward(v + total), BF16, split, ms, d_down
    )

    up_rows, dqkv = exchange(
        "attention_backward",
        [Rows(up_z), AttentionBackward(da, w_out, qb, kv_all, qseg, kseg, cosine, sine)],
        output,
    )
    dqkv = dqkv.reshape(n_plane, 2 * HEAD_DIM)
    input_grad, d_qkv, d_out, output = plane_scatter(
        [("nt", dqkv, w_qkv)],
        [x, dh],
        lambda total, v, direct: outward(direct + norm_back(inward(v.astype(F32)), total)),
        BF16, split, ms, gate_z, matmuls=[Matmul("tn", xa, dqkv), Matmul("tn", ob, da)],
        movers=[TokenMoves(outside(output), split, True)],
    )
    qkv_z = sum_along_z(d_qkv)
    input_grad, gate_rows, down_rows = exchange(
        "weight_rows", [Rows(gate_z), Rows(down_z)], d_qkv, movers=[TokenMoves(outside(input_grad), split, True)]
    )
    output = output.reshape(tokens.shape)
    input_grad = input_grad.astype(F32).reshape(tokens.shape)
    up_rows, gate_rows, down_back = (t.astype(F32) for t in (up_rows, gate_rows, down_rows))
    ffn_gain_term = jnp.sum(up_rows * up_weight.astype(F32) + gate_rows * gate_weight.astype(F32), -1)
    up_back, gate_back = up_rows * g2, gate_rows * g2
    out_back, *qkv_rows = exchange(
        "weight_rows", [HeadGradients(qkv_z, [w.shape[1] for w in wqkv])],
        up_back, gate_back, down_back, input_grad, ffn_gain_term,
        movers=[HeadSums(d_out)],
    )
    out_back = unperm(out_back)
    qkv_rows = [t.astype(F32) for t in qkv_rows]
    attn_gain_term = sum(jnp.sum(w.astype(F32) * g, -1) for w, g in zip(wqkv, qkv_rows))
    q_back, k_back, v_back = (t * g1 for t in qkv_rows)

    return (
        output,
        input_grad,
        attn_gain_term,
        q_back,
        k_back,
        v_back,
        out_back,
        ffn_gain_term,
        gate_back,
        up_back,
        down_back,
    )


def solution(mesh):
    dp, seq = mesh.shape["dp"], mesh.shape["seq"]
    fine = Mesh(mesh.devices.reshape(dp // 2, 2, seq // 2, 2), EVERY)
    dp_axes, seq_axes = ("x", "core"), ("z", "y")
    tok = P(None, dp_axes, seq_axes, None)
    vec, mat = P(EVERY), P(EVERY, None)
    return jax.shard_map(
        shards,
        mesh=fine,
        in_specs=(tok, P(None, dp_axes, None), vec, mat, mat, mat, mat, vec, mat, mat, mat, tok),
        out_specs=(tok, tok, vec, mat, mat, mat, mat, vec, mat, mat, mat),
        check_vma=False,
    )
```

```python
import functools
import itertools

import jax
import jax.numpy as jnp
from jax import lax
from jax.experimental import pallas as pl
from jax.experimental.pallas import tpu as pltpu
from jax.sharding import Mesh
from jax.sharding import PartitionSpec as P

HEADS = 8
KV_HEADS = 4
HEAD_DIM = 256
WINDOW = 1024
NORM_EPS = 1e-06
ROPE_BASE = 1000042.0
NEG_LARGE = -1e30
SCALE = HEAD_DIM**-0.5
PLANE = ("x", "core", "y")
EVERY = ("x", "core", "z", "y")
BF16 = jnp.bfloat16
F32 = jnp.float32
MESH = pl.DeviceIdType.MESH
GATHER_PARTS = 4
SCATTER_PARTS = 4


def dot_nn(a, b):
    return lax.dot_general(a, b, (((1,), (0,)), ((), ())), preferred_element_type=F32)


def dot_nt(a, b):
    return lax.dot_general(a, b, (((1,), (1,)), ((), ())), preferred_element_type=F32)


def dot_tn(a, b):
    return lax.dot_general(a, b, (((0,), (0,)), ((), ())), preferred_element_type=F32)


def rotate(values, cosine, sine):
    half = values.shape[-1] // 2
    a, b = values[:, :half], values[:, half:]
    return jnp.concatenate([a * cosine - b * sine, b * cosine + a * sine], -1)


def reorder(values, outer, inner):
    block = values.shape[-1] // (outer * inner)
    return jnp.concatenate(
        [
            values[..., (o * inner + i) * block : (o * inner + i + 1) * block]
            for i in range(inner)
            for o in range(outer)
        ],
        -1,
    )


QUERY_ROWS = 256


def query_blocks(seq_len):
    out = []
    for first in range(0, seq_len, QUERY_ROWS):
        low = max(0, first - WINDOW + 1) // 128 * 128
        out.append((first, low, min(seq_len, first + QUERY_ROWS)))
    return out


def masked_prob(q, k, first, low, qseg, kseg):
    scores = dot_nt(q, k) * SCALE
    qpos = first + lax.broadcasted_iota(jnp.int32, scores.shape, 0)
    kpos = low + lax.broadcasted_iota(jnp.int32, scores.shape, 1)
    allowed = (kpos <= qpos) & (qpos - kpos < WINDOW) & (qseg == kseg)
    masked = jnp.where(allowed, scores, NEG_LARGE)
    e = jnp.exp(masked - jnp.max(masked, -1, keepdims=True))
    return e / jnp.sum(e, -1, keepdims=True)


def attn_fwd_kernel(q_ref, k_ref, v_ref, qseg_ref, kseg_ref, o_ref):
    for first, low, end in query_blocks(q_ref.shape[0]):
        rows, keys = pl.ds(first, QUERY_ROWS), pl.ds(low, end - low)
        prob = masked_prob(q_ref[rows, :], k_ref[keys, :], first, low, qseg_ref[rows, :], kseg_ref[:, keys])
        o_ref[rows, :] = dot_nn(prob.astype(BF16), v_ref[keys, :]).astype(BF16)


def attention_specs(seq_len):
    qspec = pl.BlockSpec((None, seq_len, HEAD_DIM), lambda s: (s, 0, 0))
    kspec = pl.BlockSpec((None, None, seq_len, HEAD_DIM), lambda s: (0, s, 0, 0))
    vspec = pl.BlockSpec((None, None, seq_len, HEAD_DIM), lambda s: (1, s, 0, 0))
    qseg = pl.BlockSpec((None, seq_len, 1), lambda s: (s, 0, 0))
    kseg = pl.BlockSpec((None, 1, seq_len), lambda s: (s, 0, 0))
    return qspec, kspec, vspec, qseg, kseg


def attn_forward(q, kv, qseg, kseg):
    seqs, seq_len, _ = q.shape
    qspec, kspec, vspec, qi, ks = attention_specs(seq_len)
    return pl.pallas_call(
        attn_fwd_kernel,
        grid=(seqs,),
        in_specs=[qspec, kspec, vspec, qi, ks],
        out_specs=qspec,
        out_shape=jax.ShapeDtypeStruct(q.shape, BF16),
        compiler_params=pltpu.CompilerParams(vmem_limit_bytes=48 << 20),
        cost_estimate=light(),
        name="attention_forward",
    )(q, kv, kv, qseg, kseg)


NUMBERS = [0]


def fresh():
    NUMBERS[0] += 1
    return NUMBERS[0] - 1


def flips():
    x, c, y = (lax.axis_index(a) for a in PLANE)
    return x, c, y, {"x": 1 - x}, {"y": 1 - y}, {"core": 1 - c}


def greet(*targets):
    join([([(target, None) for target in targets], len(targets))])


def join(parties):
    barrier = pltpu.get_barrier_semaphore()

    def signal(target):
        pl.semaphore_signal(barrier, 1, device_id=target, device_id_type=MESH)

    count = 0
    for signals, number in parties:
        for target, remote in signals:
            if remote is None:
                signal(target)
            else:
                pl.when(remote)(functools.partial(signal, target))
        count = count + number
    pl.semaphore_wait(barrier, count)


def own_place():
    x, c, z, y = (lax.axis_index(a) for a in EVERY)
    return x, c, z, y, ((x * 2 + c) * lax.axis_size("z") + z) * 2 + y


def at_place(x, c, z, y):
    me = own_place()[-1]
    return {"x": x, "core": c, "z": z, "y": y}, ((x * 2 + c) * lax.axis_size("z") + z) * 2 + y != me


def send_or_keep(src, dst, send_sem, recv_sem, target, remote):
    def away():
        return pltpu.make_async_remote_copy(
            src_ref=src, dst_ref=dst, send_sem=send_sem, recv_sem=recv_sem, device_id=target, device_id_type=MESH
        )

    pl.when(remote)(lambda: away().start())
    pl.when(jnp.logical_not(remote))(lambda: pltpu.make_async_copy(src, dst, recv_sem).start())
    return lambda: pl.when(remote)(lambda: away().wait_send())


def remotes(devices):
    return sum(remote.astype(jnp.int32) for _, remote in devices)


def pieces_at(ref, split, px, pc, py):
    return ref.at[px, :, pc, py] if split == 2 else ref.at[:, pc, px, py]


def plane_shape(split, slots, *rest):
    return (2, slots, 2, 2, *rest) if split == 2 else (slots, 2, 2, 2, *rest)


ANY = pl.BlockSpec(memory_space=pl.ANY)
WHOLE = pl.BlockSpec(memory_space=pltpu.VMEM)


def light(bytes_accessed=1024):
    return pl.CostEstimate(flops=0, bytes_accessed=bytes_accessed, transcendentals=0)


FORMS = {"nn": dot_nn, "nt": dot_nt, "tn": dot_tn}


class Matmul:
    def __init__(self, form, a, b, dtype=BF16):
        self.form, self.operands = form, [a, b]
        rows = a.shape[1] if form == "tn" else a.shape[0]
        cols = b.shape[0] if form == "nt" else b.shape[1]
        self.out = jax.ShapeDtypeStruct((rows, cols), dtype)
        self.parts = max(1, rows // 256)
        self.scratch = [
            pltpu.VMEM(a.shape, a.dtype),
            pltpu.VMEM(b.shape, b.dtype),
            pltpu.VMEM(self.out.shape, dtype),
            pltpu.SemaphoreType.DMA((2,)),
            pltpu.SemaphoreType.DMA((self.parts,)),
        ]

    def steps(self, a_ref, b_ref, o_ref, a, b, out, load_sem, store_sem):
        loads = [
            pltpu.make_async_copy(a_ref, a, load_sem.at[0]),
            pltpu.make_async_copy(b_ref, b, load_sem.at[1]),
        ]
        for load in loads:
            load.start()
        yield
        for load in loads:
            load.wait()
        step = out.shape[0] // self.parts
        stores = []
        for i in range(self.parts):
            rows = pl.ds(i * step, step)
            left = a[:, rows] if self.form == "tn" else a[rows, :]
            out[rows, :] = FORMS[self.form](left, b[...]).astype(out.dtype)
            store = pltpu.make_async_copy(out.at[rows, :], o_ref.at[rows, :], store_sem.at[i])
            store.start()
            stores.append(store)
            yield
        for store in stores:
            store.wait()


def interleave(main, side):
    for matmul in side:
        next(matmul)
    rest = itertools.chain(*side)
    for _ in main:
        next(rest, None)
    for _ in rest:
        pass


def communicate(name, steps, operands, earlier, out, scratch, matmuls, vmem, specs=None, movers=()):
    n_in = len(operands)
    n_scratch = len(scratch)
    side_in = [a for m in matmuls for a in m.operands]

    def kernel(*refs):
        refs = list(refs)
        ins, refs = refs[:n_in], refs[n_in:]
        move_ins = [[refs.pop(0) for _ in m.operands] for m in movers]
        side_ins, refs = refs[: len(side_in)], refs[len(side_in) + len(earlier) :]
        outs, refs = refs[: 1 + len(matmuls)], refs[1 + len(matmuls) :]
        move_outs = [[refs.pop(0) for _ in m.out] for m in movers]
        own, refs = refs[:n_scratch], refs[n_scratch:]
        move_held = [[refs.pop(0) for _ in m.scratch] for m in movers]
        moving = [m.begin(i, o, h) for m, i, o, h in zip(movers, move_ins, move_outs, move_held)]

        def meet(*targets):
            for m in moving:
                next(m)
            join([([(t, None) for t in targets], len(targets))] + [m.party() for m in movers])
            for m in moving:
                next(m)

        side = []
        for i, m in enumerate(matmuls):
            side.append(m.steps(*side_ins[2 * i : 2 * i + 2], outs[1 + i], *refs[5 * i : 5 * i + 5]))
        interleave(steps(meet, *ins, outs[0], *own), side)
        for m in moving:
            next(m, None)

    shape, spec = out
    move_out = [o for m in movers for o in m.out]
    return pl.pallas_call(
        kernel,
        out_shape=[shape] + [m.out for m in matmuls] + move_out,
        in_specs=(specs or [ANY] * n_in)
        + [spec for m in movers for spec in m.specs]
        + [ANY] * (len(side_in) + len(earlier)),
        out_specs=[spec] + [ANY] * len(matmuls) + [spec for m in movers for spec in m.out_specs],
        scratch_shapes=scratch + [t for m in movers for t in m.scratch] + [t for m in matmuls for t in m.scratch],
        compiler_params=pltpu.CompilerParams(
            collective_id=fresh(), has_side_effects=True, vmem_limit_bytes=vmem << 20
        ),
        cost_estimate=light(),
        name=name,
    )(*operands, *[a for m in movers for a in m.operands], *side_in, *earlier)


def gather_steps(split, prepare, meet, *refs):
    sources, (o_ref, a_ref, own_sem, send_sem, recv_sem) = refs[:-5], refs[-5:]
    x, c, y, to_x, to_y, to_c = flips()
    slots, piece, _ = a_ref.shape
    per_slot = GATHER_PARTS // slots
    step = piece // per_slot
    meet(to_x, to_y, to_c)

    def rows_of(i):
        return i // per_slot, pl.ds(i % per_slot * step, step)

    def part(px, pc, py, i):
        return pieces_at(o_ref, split, px, pc, py).at[rows_of(i)]

    def send(kind, i, src, dst, target):
        copy = pltpu.make_async_remote_copy(
            src_ref=src, dst_ref=dst, send_sem=send_sem.at[kind, i], recv_sem=recv_sem.at[kind, i],
            device_id=target, device_id_type=MESH,
        )
        copy.start()
        return copy

    copies = {}
    for i in range(GATHER_PARTS):
        a_ref[rows_of(i)] = prepare(*(source[rows_of(i)] for source in sources)).astype(BF16)
        own = a_ref.at[rows_of(i)]
        for kind, target in enumerate((to_x, to_y, to_c)):
            copies[kind, i] = send(kind, i, own, part(x, c, y, i), target)
    own_copy = pltpu.make_async_copy(a_ref, pieces_at(o_ref, split, x, c, y), own_sem)
    own_copy.start()
    yield
    src_x, src_y = jnp.where(c == 0, x, 1 - x), jnp.where(c == 0, 1 - y, y)
    dst_x, dst_y = jnp.where(c == 0, 1 - x, x), jnp.where(c == 0, y, 1 - y)
    for i in range(GATHER_PARTS):
        for kind, (px, py) in enumerate(((1 - x, y), (x, 1 - y))):
            copies[kind, i].wait_recv()
            block = part(px, c, py, i)
            copies[3 + kind, i] = send(3 + kind, i, block, block, to_c)
        block = part(src_x, c, src_y, i)
        copies[5, i] = send(5, i, block, block, {"x": dst_x, "y": dst_y})
        yield
        yield
    for i in range(GATHER_PARTS):
        copies[5, i].wait_recv()
        block = part(1 - x, c, 1 - y, i)
        copies[6, i] = send(6, i, block, block, to_c)
        yield
    for i in range(GATHER_PARTS):
        for kind in (2, 3, 4, 6):
            copies[kind, i].wait_recv()
    own_copy.wait()
    for i in range(GATHER_PARTS):
        for kind in range(7):
            copies[kind, i].wait_send()


def plane_gather(sources, prepare, split, *earlier, matmuls=(), movers=()):
    slots, piece, width = sources[0].shape
    out = jax.ShapeDtypeStruct(plane_shape(split, slots, piece, width), BF16)
    scratch = [
        pltpu.VMEM((slots, piece, width), BF16),
        pltpu.SemaphoreType.DMA,
        pltpu.SemaphoreType.DMA((7, GATHER_PARTS)),
        pltpu.SemaphoreType.DMA((7, GATHER_PARTS)),
    ]
    result = communicate(
        "plane_gather", functools.partial(gather_steps, split, prepare), list(sources), earlier, (out, ANY), scratch,
        matmuls, 40 if matmuls else 16, [WHOLE] * len(sources), movers,
    )
    got = result[0].reshape(-1, width)
    return (got, *result[1:]) if matmuls or movers else got


def scatter_steps(split, forms, finish, n_sources, meet, *refs):
    n = len(forms)
    hbm, refs = refs[: 2 * n], refs[2 * n :]
    sources, refs = refs[:n_sources], refs[n_sources:]
    o_ref, refs = refs[0], refs[1:]
    held, refs = refs[: 2 * n], refs[2 * n :]
    own, put_c, got_c, put_x, put_y, got_x, got_y, fin_x, fin_y, end_x, end_y, load_sem, send_sem, recv_sem = refs
    x, c, y, to_x, to_y, to_c = flips()
    parts, _, _, step, width = own.shape
    slots = o_ref.shape[0]
    per_slot = parts // slots
    half = width // 2
    left, right = pl.ds(0, half), pl.ds(half, half)
    loads = [pltpu.make_async_copy(of, to, load_sem.at[i]) for i, (of, to) in enumerate(zip(hbm, held))]
    for load in loads:
        load.start()
    meet(to_x, to_y, to_c)
    for load in loads:
        load.wait()

    def rows_of(i):
        return i // per_slot, pl.ds(i % per_slot * step, step)

    def partial_sums(pc, i, columns):
        slot, rows = rows_of(i)
        total = None
        for form, a, b in zip(forms, held[::2], held[1::2]):
            if split == 2:
                block = a[:, slot, pc, :, rows, :]
            else:
                block = a[slot, pc, :, :, rows, :]
            block = block.reshape(4 * step, block.shape[-1])
            term = dot_nn(block, b[:, columns]) if form == "nn" else dot_nt(block, b[columns, :])
            total = term if total is None else total + term
        return total.astype(BF16).reshape(2, 2, step, half)

    def send(kind, i, src, dst, target):
        copy = pltpu.make_async_remote_copy(
            src_ref=src.at[i], dst_ref=dst.at[i], send_sem=send_sem.at[kind, i], recv_sem=recv_sem.at[kind, i],
            device_id=target, device_id_type=MESH,
        )
        copy.start()
        return copy

    def f32(ref, *index):
        return ref[index].astype(F32)

    first, second, third = [], [], []

    def along_first_axis(i):
        first[i].wait_recv()
        for j in range(2):
            put_x[i, j] = (f32(own, i, 1 - x, j, slice(None), left) + f32(got_c, i, 1 - x, j, slice(None), left)).astype(BF16)
            put_y[i, j] = (f32(own, i, j, 1 - y, slice(None), right) + f32(got_c, i, j, 1 - y, slice(None), right)).astype(BF16)
        second.append((send(1, i, put_x, got_x, to_x), send(2, i, put_y, got_y, to_y)))

    for i in range(parts):
        for columns in (left, right):
            put_c[i, :, :, :, columns] = partial_sums(1 - c, i, columns)
        first.append(send(0, i, put_c, got_c, to_c))
        for columns in (left, right):
            own[i, :, :, :, columns] = partial_sums(c, i, columns)
        if i:
            along_first_axis(i - 1)
    along_first_axis(parts - 1)
    yield
    yield
    for i in range(parts):
        for copy in second[i]:
            copy.wait_recv()
        fin_y[i] = (
            f32(own, i, x, 1 - y, slice(None), left) + f32(got_c, i, x, 1 - y, slice(None), left) + f32(got_x, i, 1 - y)
        ).astype(BF16)
        fin_x[i] = (
            f32(own, i, 1 - x, y, slice(None), right) + f32(got_c, i, 1 - x, y, slice(None), right) + f32(got_y, i, 1 - x)
        ).astype(BF16)
        third.append((send(3, i, fin_y, end_y, to_y), send(4, i, fin_x, end_x, to_x)))
        yield
        yield
    for i in range(parts):
        for copy in third[i]:
            copy.wait_recv()
        slot, rows = rows_of(i)
        total = jnp.concatenate(
            [
                f32(own, i, x, y, slice(None), left) + f32(got_c, i, x, y, slice(None), left)
                + f32(got_x, i, y) + f32(end_y, i),
                f32(own, i, x, y, slice(None), right) + f32(got_c, i, x, y, slice(None), right)
                + f32(got_y, i, x) + f32(end_x, i),
            ],
            -1,
        )
        o_ref[slot, rows, :] = finish(total, *(source[slot, rows, :] for source in sources)).astype(o_ref.dtype)
        yield
    for i in range(parts):
        for copy in (first[i], *second[i], *third[i]):
            copy.wait_send()


def plane_scatter(products, sources, finish, dtype, split, slots, *earlier, matmuls=(), movers=()):
    forms = [form for form, _, _ in products]
    _, a, b = products[0]
    rows, width = a.shape[0] // 8, (b.shape[1] if forms[0] == "nn" else b.shape[0])
    piece = rows // slots
    n = SCATTER_PARTS
    step, half = rows // n, width // 2
    operands = []
    for _, a, b in products:
        operands += [a.reshape(plane_shape(split, slots, piece, a.shape[1])), b]
    whole, two, one = (
        pltpu.VMEM((n, 2, 2, step, width), BF16),
        pltpu.VMEM((n, 2, step, half), BF16),
        pltpu.VMEM((n, step, half), BF16),
    )
    scratch = [pltpu.VMEM(t.shape, t.dtype) for t in operands]
    scratch += [whole] * 3 + [two] * 4 + [one] * 4
    scratch += [
        pltpu.SemaphoreType.DMA((len(operands),)),
        pltpu.SemaphoreType.DMA((5, n)),
        pltpu.SemaphoreType.DMA((5, n)),
    ]
    out = jax.ShapeDtypeStruct((slots, piece, width), dtype)
    result = communicate(
        "plane_scatter", functools.partial(scatter_steps, split, forms, finish, len(sources)),
        operands + list(sources), earlier, (out, WHOLE), scratch, matmuls, 62,
        [ANY] * len(operands) + [WHOLE] * len(sources), movers,
    )
    return result if matmuls or movers else result[0]


def pair_kernel(a_ref, *refs):
    o_ref, own_sem, send_sem, recv_sem = refs[-4:]
    c = lax.axis_index("core")
    greet({"core": 1 - c})
    keep = pltpu.make_async_copy(a_ref, o_ref.at[c], own_sem)
    keep.start()
    copy = pltpu.make_async_remote_copy(
        src_ref=a_ref, dst_ref=o_ref.at[c], send_sem=send_sem, recv_sem=recv_sem,
        device_id={"core": 1 - c}, device_id_type=MESH,
    )
    copy.start()
    keep.wait()
    copy.wait()


def core_gather(a, *earlier):
    return pl.pallas_call(
        pair_kernel,
        out_shape=jax.ShapeDtypeStruct((2, *a.shape), a.dtype),
        in_specs=[WHOLE] + [ANY] * len(earlier),
        out_specs=ANY,
        scratch_shapes=[pltpu.SemaphoreType.DMA] * 3,
        compiler_params=pltpu.CompilerParams(
            collective_id=fresh(), has_side_effects=True, vmem_limit_bytes=32 << 20
        ),
        cost_estimate=light(),
        name="core_gather",
    )(a, *earlier)


def others():
    x, c, y, *_ = flips()
    out = []
    for dx, dc, dy in ((1, 0, 1), (1, 1, 1), (1, 0, 0), (0, 0, 1), (1, 1, 0), (0, 1, 1), (0, 1, 0)):
        px, pc, py = (1 - x if dx else x), (1 - c if dc else c), (1 - y if dy else y)
        out.append(((px * 2 + pc) * 2 + py, {"x": px, "core": pc, "y": py}))
    return (x * 2 + c) * 2 + y, out


class TokenMoves:
    def __init__(self, tokens, split, back=False):
        self.split, self.back, self.operands = split, back, [tokens]
        self.out = [jax.ShapeDtypeStruct(tokens.shape, tokens.dtype)]
        self.specs = self.out_specs = [ANY]
        self.scratch = [pltpu.SemaphoreType.DMA((tokens.shape[0],))] * 2

    def places(self):
        ms = self.out[0].shape[0]
        x, c, z, y, _ = own_place()
        if self.split == 2:
            slot = group = z // 2
            to = [at_place(x, z % 2, 2 * j + c, y) for j in range(ms)]
            of = [at_place(x, z % 2, 2 * k + c, y) for k in range(ms)]
        else:
            slot = group = z // 4
            to = [at_place(z % 2, z // 2 % 2, (2 * j + x) * 2 + c, y) for j in range(ms)]
            of = [at_place(z // 2 % 2, z % 2, 4 * k + 2 * c + x, y) for k in range(ms)]
        return (group, of, to) if self.back else (slot, to, of)

    def party(self):
        _, to, of = self.places()
        return of, remotes(to)

    def begin(self, ins, outs, held):
        (t_ref,), (o_ref,), (send_sem, recv_sem) = ins, outs, held
        slot, to, _ = self.places()
        yield
        waits = [
            send_or_keep(t_ref.at[j], o_ref.at[slot], send_sem.at[j], recv_sem.at[slot], *place)
            for j, place in enumerate(to)
        ]
        yield
        for k in range(len(to)):
            pltpu.make_async_copy(t_ref.at[0], o_ref.at[k], recv_sem.at[k]).wait()
        for wait in waits:
            wait()


class TokenRounds(TokenMoves):
    def __init__(self, tokens, split, rounds):
        super().__init__(tokens, split)
        self.rounds = rounds
        self.out = [jax.ShapeDtypeStruct((len(rounds), *tokens.shape[1:]), tokens.dtype)]
        self.scratch = [pltpu.SemaphoreType.DMA((len(rounds),))] * 2

    def places(self):
        ms = self.operands[0].shape[0]
        x, c, z, y, _ = own_place()
        slot = group = z // 2 if self.split == 2 else z // 4
        js = [(r + slot) % ms for r in self.rounds]
        ks = [(group - r + ms) % ms for r in self.rounds]
        if self.split == 2:
            to = [at_place(x, z % 2, 2 * j + c, y) for j in js]
            of = [at_place(x, z % 2, 2 * k + c, y) for k in ks]
        else:
            to = [at_place(z % 2, z // 2 % 2, (2 * j + x) * 2 + c, y) for j in js]
            of = [at_place(z // 2 % 2, z % 2, 4 * k + 2 * c + x, y) for k in ks]
        return js, to, of

    def begin(self, ins, outs, held):
        (t_ref,), (o_ref,), (send_sem, recv_sem) = ins, outs, held
        js, to, _ = self.places()
        yield
        waits = [
            send_or_keep(t_ref.at[j], o_ref.at[i], send_sem.at[i], recv_sem.at[i], *place)
            for i, (j, place) in enumerate(zip(js, to))
        ]
        yield
        for i in range(len(to)):
            pltpu.make_async_copy(t_ref.at[0], o_ref.at[i], recv_sem.at[i]).wait()
        for wait in waits:
            wait()


def head_device(h, z):
    return at_place(h // 4, h % 2, z, h // 2 % 2)


def head_owner(h, k):
    nz = lax.axis_size("z")
    rest = h % 2 * nz + k
    return at_place(h // 4, h // 2 % 2, rest // 2, rest % 2)


class HeadRows:
    def __init__(self, w, inward):
        rows, width = w.shape
        self.nz, self.inward, self.operands = lax.axis_size("z"), inward, [w]
        self.out = [jax.ShapeDtypeStruct((self.nz * rows, width), BF16)]
        self.specs, self.out_specs = [WHOLE], [ANY]
        self.scratch = [pltpu.VMEM((rows, width), BF16)] + [pltpu.SemaphoreType.DMA((self.nz,))] * 2

    def places(self):
        x, c, z, y, me = own_place()
        targets = [head_device(me // self.nz, t) for t in range(self.nz)]
        return targets, [head_owner(4 * x + 2 * y + c, k) for k in range(self.nz)], me % self.nz

    def party(self):
        targets, sources, _ = self.places()
        return sources, remotes(targets)

    def begin(self, ins, outs, held):
        (w_ref,), (o_ref,), (turned, send_sem, recv_sem) = ins, outs, held
        rows = turned.shape[0]
        targets, _, k = self.places()
        turned[...] = self.inward(w_ref[...])
        yield
        to = o_ref.at[pl.ds(pl.multiple_of(k * rows, rows), rows), :]
        waits = [send_or_keep(turned, to, send_sem.at[t], recv_sem.at[k], *place) for t, place in enumerate(targets)]
        yield
        for j in range(self.nz):
            pltpu.make_async_copy(turned, o_ref.at[pl.ds(j * rows, rows), :], recv_sem.at[j]).wait()
        for wait in waits:
            wait()


class HeadSums:
    def __init__(self, d):
        self.nz, self.operands = lax.axis_size("z"), [d]
        rows, width = d.shape[0] // self.nz, d.shape[1]
        self.out = [jax.ShapeDtypeStruct((rows, width), F32)]
        self.specs, self.out_specs = [ANY], [WHOLE]
        self.scratch = [pltpu.VMEM((self.nz, rows, width), BF16)] + [pltpu.SemaphoreType.DMA((self.nz,))] * 2

    def places(self):
        x, c, z, y, me = own_place()
        targets = [head_owner(4 * x + 2 * y + c, k) for k in range(self.nz)]
        return targets, [head_device(me // self.nz, t) for t in range(self.nz)], z

    def party(self):
        targets, sources, _ = self.places()
        return sources, remotes(targets)

    def begin(self, ins, outs, held):
        (d_ref,), (o_ref,), (got, send_sem, recv_sem) = ins, outs, held
        rows = got.shape[1]
        targets, _, z = self.places()
        yield
        waits = [
            send_or_keep(d_ref.at[pl.ds(k * rows, rows), :], got.at[z], send_sem.at[k], recv_sem.at[z], *place)
            for k, place in enumerate(targets)
        ]
        yield
        total = None
        for t in range(self.nz):
            pltpu.make_async_copy(d_ref.at[pl.ds(0, rows), :], got.at[t], recv_sem.at[t]).wait()
            total = got[t].astype(F32) if total is None else total + got[t].astype(F32)
        o_ref[...] = total
        for wait in waits:
            wait()


def head_columns(px, pc, py):
    return tuple(pl.ds(pl.multiple_of(h * HEAD_DIM, HEAD_DIM), HEAD_DIM) for h in (4 * px + 2 * py + pc, 2 * px + py))


class Columns:
    def __init__(self, weights, gain=None):
        rows = weights[0].shape[0]
        self.heads, self.scaled = len(weights) == 3, gain is not None
        cols = 2 * HEAD_DIM if self.heads else weights[0].shape[1] // 8
        self.operands = list(weights) + ([gain] if self.scaled else [])
        self.out = [jax.ShapeDtypeStruct((8 * rows, cols), BF16)]
        self.specs, self.out_specs = [ANY] * len(self.operands), [ANY]
        self.scratch = [
            pltpu.VMEM((8, rows, cols), BF16),
            pltpu.SemaphoreType.DMA,
            pltpu.SemaphoreType.DMA((7,)),
            pltpu.SemaphoreType.DMA((7,)),
        ]
        if self.scaled:
            self.scratch += [pltpu.VMEM(t.shape, t.dtype) for t in self.operands]
            self.scratch.append(pltpu.SemaphoreType.DMA((len(self.operands),)))

    def begin(self, ins, outs, held):
        (o_ref,), (scaled, own_sem, send_sem, recv_sem, *loaded) = outs, held
        _, rows, cols = scaled.shape
        me, peers = others()
        x, c, y, *_ = flips()
        to = o_ref.at[pl.ds(pl.multiple_of(me * rows, rows), rows), :]
        loads = [pltpu.make_async_copy(of, to_, loaded[-1].at[i]) for i, (of, to_) in enumerate(zip(ins, loaded[:-1]))]
        for load in loads:
            load.start()

        def piece(p, px, pc, py):
            if self.heads:
                wq, wk, wv, gain = loaded[:-1]
                q_cols, kv_cols = head_columns(px, pc, py)
                scaled[p, :, :HEAD_DIM] = (wq[:, q_cols].astype(F32) * gain[...]).astype(BF16)
                for_kv = jnp.where(pc == 0, wk[:, kv_cols].astype(F32), wv[:, kv_cols].astype(F32))
                scaled[p, :, HEAD_DIM:] = (for_kv * gain[...]).astype(BF16)
                return scaled.at[p]
            columns = pl.ds(pl.multiple_of(p * cols, cols), cols)
            if self.scaled:
                scaled[p] = (loaded[0][:, columns].astype(F32) * loaded[1][...]).astype(BF16)
                return scaled.at[p]
            return ins[0].at[:, columns]

        yield
        for load in loads:
            load.wait()
        copies = []
        for kind, (p, target) in enumerate(peers):
            copy = pltpu.make_async_remote_copy(
                src_ref=piece(p, target["x"], target["core"], target["y"]), dst_ref=to,
                send_sem=send_sem.at[kind], recv_sem=recv_sem.at[kind], device_id=target, device_id_type=MESH,
            )
            copy.start()
            copies.append(copy)
        keep = pltpu.make_async_copy(piece(me, x, c, y), to, own_sem)
        keep.start()
        yield
        keep.wait()
        for copy in copies:
            copy.wait()


class Segments:
    def __init__(self, seg):
        self.operands, self.out = [seg], [jax.ShapeDtypeStruct((8, *seg.shape), seg.dtype)]
        self.specs, self.out_specs = [WHOLE], [ANY]
        self.scratch = [pltpu.SemaphoreType.DMA, pltpu.SemaphoreType.DMA((7,)), pltpu.SemaphoreType.DMA((7,))]

    def begin(self, ins, outs, held):
        (seg_ref,), (o_ref,), (own_sem, send_sem, recv_sem) = ins, outs, held
        me, peers = others()
        yield
        copies = []
        for kind, (_, target) in enumerate(peers):
            copy = pltpu.make_async_remote_copy(
                src_ref=seg_ref, dst_ref=o_ref.at[me], send_sem=send_sem.at[kind], recv_sem=recv_sem.at[kind],
                device_id=target, device_id_type=MESH,
            )
            copy.start()
            copies.append(copy)
        keep = pltpu.make_async_copy(seg_ref, o_ref.at[me], own_sem)
        keep.start()
        yield
        keep.wait()
        for copy in copies:
            copy.wait()


def exchange(name, items, *earlier, movers=()):
    parts = [*movers, *items]

    def kernel(*refs):
        refs = list(refs)
        ins = [[refs.pop(0) for _ in part.operands] for part in parts]
        refs = refs[len(earlier) :]
        outs = [[refs.pop(0) for _ in part.out] for part in parts]
        held = [[refs.pop(0) for _ in part.scratch] for part in parts]
        running = [part.begin(*given) for part, *given in zip(parts, ins, outs, held)]
        for part in running:
            next(part)
        targets = [(target, None) for _, target in others()[1]]
        join([(targets, len(targets))] + [mover.party() for mover in movers])
        for part in running:
            next(part)
        for part in running:
            next(part, None)

    result = pl.pallas_call(
        kernel,
        out_shape=[o for part in parts for o in part.out],
        in_specs=[spec for part in parts for spec in part.specs] + [ANY] * len(earlier),
        out_specs=[spec for part in parts for spec in part.out_specs],
        scratch_shapes=[t for part in parts for t in part.scratch],
        compiler_params=pltpu.CompilerParams(
            collective_id=fresh(), has_side_effects=True, vmem_limit_bytes=62 << 20
        ),
        cost_estimate=light(),
        name=name,
    )(*[a for part in parts for a in part.operands], *earlier)
    return result


class Rows:
    def __init__(self, part):
        self.cols, rows = part.shape[1], part.shape[0] // 8
        self.operands, self.specs = [part], [ANY]
        self.out, self.out_specs = [jax.ShapeDtypeStruct((rows, 8 * self.cols), BF16)], [ANY]
        self.scratch = [pltpu.SemaphoreType.DMA, pltpu.SemaphoreType.DMA((7,)), pltpu.SemaphoreType.DMA((7,))]

    def begin(self, ins, outs, held):
        (p_ref,), (o_ref,), (own_sem, send_sem, recv_sem) = ins, outs, held
        rows = o_ref.shape[0]
        me, peers = others()
        to = o_ref.at[:, pl.ds(pl.multiple_of(me * self.cols, self.cols), self.cols)]

        def block(p):
            return p_ref.at[pl.ds(pl.multiple_of(p * rows, rows), rows), :]

        yield
        copies = []
        for kind, (p, target) in enumerate(peers):
            copy = pltpu.make_async_remote_copy(
                src_ref=block(p), dst_ref=to, send_sem=send_sem.at[kind], recv_sem=recv_sem.at[kind],
                device_id=target, device_id_type=MESH,
            )
            copy.start()
            copies.append(copy)
        keep = pltpu.make_async_copy(block(me), to, own_sem)
        keep.start()
        yield
        keep.wait()
        for copy in copies:
            copy.wait()


class HeadGradients:
    def __init__(self, part, widths):
        rows = part.shape[0] // 8
        self.operands, self.specs = [part], [ANY]
        self.out = [jax.ShapeDtypeStruct((rows, n), BF16) for n in widths]
        self.out_specs = [ANY] * 3
        self.scratch = [pltpu.SemaphoreType.DMA((2,)), pltpu.SemaphoreType.DMA((14,)), pltpu.SemaphoreType.DMA((14,))]

    def begin(self, ins, outs, held):
        (p_ref,), (q_out, k_out, v_out), (own_sem, send_sem, recv_sem) = ins, outs, held
        rows = q_out.shape[0]
        me, peers = others()
        x, c, y, *_ = flips()
        q_cols, kv_cols = head_columns(x, c, y)
        halves = pl.ds(0, HEAD_DIM), pl.ds(HEAD_DIM, HEAD_DIM)

        def block(p, half):
            return p_ref.at[pl.ds(pl.multiple_of(p * rows, rows), rows), halves[half]]

        def away(kind, half, to):
            p, target = peers[kind]
            return pltpu.make_async_remote_copy(
                src_ref=block(p, half), dst_ref=to,
                send_sem=send_sem.at[2 * kind + half], recv_sem=recv_sem.at[2 * kind + half],
                device_id=target, device_id_type=MESH,
            )

        q_to, k_to, v_to = q_out.at[:, q_cols], k_out.at[:, kv_cols], v_out.at[:, kv_cols]
        yield
        for kind in range(7):
            away(kind, 0, q_to).start()
            pl.when(c == 0)(lambda: away(kind, 1, k_to).start())
            pl.when(c == 1)(lambda: away(kind, 1, v_to).start())
        pltpu.make_async_copy(block(me, 0), q_to, own_sem.at[0]).start()
        pl.when(c == 0)(lambda: pltpu.make_async_copy(block(me, 1), k_to, own_sem.at[1]).start())
        pl.when(c == 1)(lambda: pltpu.make_async_copy(block(me, 1), v_to, own_sem.at[1]).start())
        yield
        for half in range(2):
            pltpu.make_async_copy(block(me, half), q_to, own_sem.at[half]).wait()
        for kind in range(7):
            for half in range(2):
                away(kind, half, q_to).wait()


class AttentionBackward:
    def __init__(self, da, w_out, q, kv, qseg, kseg, cosine, sine):
        seqs, seq_len, hd = q.shape
        self.operands = [da.reshape(seqs, seq_len, -1), w_out, q, kv, qseg, kseg, cosine, sine]
        self.specs = [ANY] * 4 + [WHOLE] * 2 + [ANY] * 2
        self.out = [jax.ShapeDtypeStruct((seqs, seq_len, 2 * hd), BF16)]
        self.out_specs = [WHOLE]
        self.loaded = (1, 2, 3, 6, 7)
        self.scratch = [pltpu.VMEM(self.operands[i].shape, self.operands[i].dtype) for i in self.loaded]
        self.scratch += [
            pltpu.SemaphoreType.DMA((len(self.loaded),)),
            pltpu.VMEM(self.operands[0].shape, BF16),
            pltpu.VMEM((seq_len, hd), F32),
            pltpu.VMEM((seq_len, hd), F32),
            pltpu.VMEM((2, seqs, seq_len, hd), BF16),
            pltpu.VMEM((seqs, seq_len, hd), BF16),
            pltpu.SemaphoreType.DMA((seqs,)),
            pltpu.SemaphoreType.DMA((seqs,)),
            pltpu.SemaphoreType.DMA((seqs,)),
        ]

    def begin(self, ins, outs, held):
        n = len(self.loaded)
        w_out, q_ref, kv_ref, cos_ref, sin_ref = copied = held[:n]
        da, dk_sum, dv_sum, dkv, got, da_sem, send_sem, recv_sem = held[n + 1 :]
        qseg_ref, kseg_ref = ins[4:6]
        (o_ref,) = outs
        c = lax.axis_index("core")
        seqs, seq_len, hd = q_ref.shape
        first_loads = [pltpu.make_async_copy(ins[i], copied[j], held[n].at[j]) for j, i in enumerate(self.loaded)]
        loads = [pltpu.make_async_copy(ins[0].at[s], da.at[s], da_sem.at[s]) for s in range(seqs)]
        for load in first_loads + loads:
            load.start()
        yield
        yield
        for load in first_loads:
            load.wait()
        copies = []
        for s, load in enumerate(loads):
            load.wait()
            dk_sum[...] = jnp.zeros_like(dk_sum)
            dv_sum[...] = jnp.zeros_like(dv_sum)
            for first, low, end in query_blocks(seq_len):
                rows, keys = pl.ds(first, QUERY_ROWS), pl.ds(low, end - low)
                q, k, v = q_ref[s, rows, :], kv_ref[0, s, keys, :], kv_ref[1, s, keys, :]
                do = dot_nt(da[s, rows, :], w_out[...]).astype(BF16)
                prob = masked_prob(q, k, first, low, qseg_ref[s, rows, :], kseg_ref[s, :, keys])
                dprob = dot_nt(do, v)
                ds = prob * (dprob - jnp.sum(prob * dprob, -1, keepdims=True))
                dsb = ds.astype(BF16)
                dq = dot_nn(dsb, k) * SCALE
                o_ref[s, rows, :hd] = rotate(dq, cos_ref[rows, :], -sin_ref[rows, :]).astype(BF16)
                dk_sum[keys, :] += dot_tn(dsb, q)
                dv_sum[keys, :] += dot_tn(prob.astype(BF16), do)
            dkv[0, s] = (dk_sum[...] * SCALE).astype(BF16)
            dkv[1, s] = dv_sum[...].astype(BF16)
            copy = pltpu.make_async_remote_copy(
                src_ref=dkv.at[1 - c, s], dst_ref=got.at[s], send_sem=send_sem.at[s], recv_sem=recv_sem.at[s],
                device_id={"core": 1 - c}, device_id_type=MESH,
            )
            copy.start()
            copies.append(copy)
        for s, copy in enumerate(copies):
            copy.wait_recv()
            total = dkv[c, s].astype(F32) + got[s].astype(F32)
            turned = rotate(total, cos_ref[...], -sin_ref[...])
            o_ref[s, :, hd:] = jnp.where(c == 0, turned, total).astype(BF16)
        for copy in copies:
            copy.wait_send()


def tie_kernel(a_ref, *refs):
    pass


def tie(a, *earlier):
    return pl.pallas_call(
        tie_kernel,
        out_shape=jax.ShapeDtypeStruct(a.shape, a.dtype),
        in_specs=[ANY] * (1 + len(earlier)),
        out_specs=ANY,
        input_output_aliases={0: 0},
        cost_estimate=light(),
        name="tie",
    )(a, *earlier)


def along_z(part):
    return lax.all_gather(part, "z", axis=0, tiled=True)


def sum_along_z(g):
    return lax.psum_scatter(g, "z", scatter_dimension=0, tiled=True)


def shards(
    tokens,
    segments,
    attn_gain,
    query_weight,
    key_weight,
    value_weight,
    out_weight,
    ffn_gain,
    gate_weight,
    up_weight,
    down_weight,
    cotangent,
):
    NUMBERS[0] = 0
    micro, seq_local, pl_len, width = tokens.shape
    seq_len = segments.shape[2]
    ms = micro * seq_local
    rows_w = gate_weight.shape[0]
    nx, nc, nz, ny = (lax.axis_size(a) for a in EVERY)
    dp = nx * nc
    n_plane = 8 * ms * pl_len
    col_block = width // (dp * nz)
    z_index = lax.axis_index("z")
    core = lax.axis_index("core")
    split = dp * ms // nz

    def perm(a):
        lead = a.shape[:-1]
        return a.reshape(*lead, dp, nz, col_block).swapaxes(-3, -2).reshape(*lead, width)

    def unperm(a):
        lead = a.shape[:-1]
        return a.reshape(*lead, nz, dp, col_block).swapaxes(-3, -2).reshape(*lead, width)

    whole_lanes = col_block % 128 == 0

    def inward(v):
        return reorder(v, dp, nz) if whole_lanes else v

    def outward(v):
        return reorder(v, nz, dp) if whole_lanes else v

    def inside(a):
        return a if whole_lanes else perm(a)

    def outside(a):
        return a if whole_lanes else unperm(a)

    def scale_of(v):
        return lax.rsqrt(jnp.mean(v * v, -1, keepdims=True) + NORM_EPS)

    def norm_back(v, d_hat):
        scale = scale_of(v)
        hat = v * scale
        return scale * (d_hat - hat * jnp.mean(d_hat * hat, -1, keepdims=True))

    def pick(a, index):
        return lax.dynamic_index_in_dim(a, index, 0, keepdims=False)

    g1 = attn_gain.astype(F32)[:, None]
    g2 = ffn_gain.astype(F32)[:, None]

    wqkv = (query_weight, key_weight, value_weight)
    pieces = tokens.reshape(ms, pl_len, width)
    x_first, wqkv_part = exchange(
        "weight_columns", [Columns(wqkv, g1)], movers=[TokenRounds(pieces, split, range(ms // 2))]
    )
    x_last, gate_part, seg_all = exchange(
        "weight_columns", [Columns([gate_weight], g2), Segments(segments.reshape(ms, seq_len))], wqkv_part,
        movers=[TokenRounds(pieces, split, range(ms // 2, ms))],
    )
    group = z_index // 2 if split == 2 else z_index // 4
    came_in = (group - jnp.arange(ms, dtype=jnp.int32)[:, None, None] + ms) % ms
    x = x_first[0][None]
    for r in range(1, ms):
        x = jnp.where(came_in == r, x_first[r] if r < ms // 2 else x_last[r - ms // 2], x)
    w_qkv = along_z(wqkv_part)

    seg_all = seg_all.reshape(2, 2, 2, ms, seq_len)[:, :, 0]
    if split == 2:
        seg = pick(pick(seg_all.swapaxes(0, 1), z_index % 2).swapaxes(0, 1), z_index // 2)
    else:
        seg = pick(pick(pick(seg_all, z_index // 2 % 2), z_index % 2), z_index // 4)[None]
    qseg, kseg = seg[:, :, None], seg[:, None, :]

    x = inside(x)

    def norm_in(v):
        v = inward(v.astype(F32))
        return v * scale_of(v)

    xa, w_out = plane_gather([x], norm_in, split, wqkv_part, movers=[HeadRows(inside(out_weight), inward)])

    inv_freq = 1.0 / ROPE_BASE ** (jnp.arange(0, HEAD_DIM, 2, dtype=F32) / HEAD_DIM)
    angles = jnp.arange(seq_len, dtype=jnp.int32).astype(F32)[:, None] * inv_freq[None, :]
    cosine, sine = jnp.cos(angles), jnp.sin(angles)
    cos_q, sin_q = (jnp.tile(t, (split, 1)) for t in (cosine, sine))
    cos_k = jnp.where(core == 0, cos_q, 1.0)
    sin_k = jnp.where(core == 0, sin_q, 0.0)

    qkv = dot_nn(xa, w_qkv)
    qb = rotate(qkv[:, :HEAD_DIM], cos_q, sin_q).astype(BF16).reshape(split, seq_len, HEAD_DIM)
    kvb = rotate(qkv[:, HEAD_DIM:], cos_k, sin_k).astype(BF16)
    kv_all = core_gather(kvb).reshape(2, split, seq_len, HEAD_DIM)

    w_gate = along_z(gate_part)
    ob = attn_forward(qb, kv_all, qseg, kseg).reshape(n_plane, HEAD_DIM)
    (down_part,) = exchange("weight_columns", [Columns([down_weight])], ob)
    w_down = along_z(down_part)
    h, cot = plane_scatter(
        [("nn", ob, w_out)], [x], lambda total, v: inward(v.astype(F32)) + total, F32, split, ms, down_part,
        movers=[TokenMoves(cotangent.reshape(ms, pl_len, width), split)],
    )
    cot = inside(cot)

    ha = plane_gather([h], lambda v: v * scale_of(v), split)
    (up_part,) = exchange("weight_columns", [Columns([up_weight], g2)], ha)
    w_up = along_z(up_part)
    ca, gate = plane_gather([cot], inward, split, up_part, matmuls=[Matmul("nn", ha, w_gate, F32)])
    sig = jax.nn.sigmoid(gate)
    silu = gate * sig
    d_mid = dot_nn(ca, w_down)
    dub = (d_mid * silu).astype(BF16)
    d_up = dot_tn(ha, dub).astype(BF16)
    w_up = tie(w_up, d_up)
    up = dot_nn(ha, w_up)
    dgb = (d_mid * up * sig * (1.0 + gate * (1.0 - sig))).astype(BF16)
    mid = (silu * up).astype(BF16)
    dh, d_gate = plane_scatter(
        [("nt", dgb, w_gate), ("nt", dub, w_up)],
        [h, cot],
        lambda total, v, dy: inward(dy.astype(F32)) + norm_back(v, total),
        F32, split, ms, matmuls=[Matmul("tn", ha, dgb)],
    )
    up_z = sum_along_z(d_up)
    gate_z = sum_along_z(d_gate)
    da, d_down = plane_gather([dh], lambda v: v, split, matmuls=[Matmul("tn", ca, mid)])

    down_z = sum_along_z(d_down)
    output = plane_scatter(
        [("nt", mid, w_down)], [h], lambda total, v: outward(v + total), BF16, split, ms, d_down
    )

    up_rows, dqkv = exchange(
        "attention_backward",
        [Rows(up_z), AttentionBackward(da, w_out, qb, kv_all, qseg, kseg, cosine, sine)],
        output,
    )
    dqkv = dqkv.reshape(n_plane, 2 * HEAD_DIM)
    input_grad, d_qkv, d_out, output = plane_scatter(
        [("nt", dqkv, w_qkv)],
        [x, dh],
        lambda total, v, direct: outward(direct + norm_back(inward(v.astype(F32)), total)),
        BF16, split, ms, gate_z, matmuls=[Matmul("tn", xa, dqkv), Matmul("tn", ob, da)],
        movers=[TokenMoves(outside(output), split, True)],
    )
    qkv_z = sum_along_z(d_qkv)
    input_grad, gate_rows, down_rows = exchange(
        "weight_rows", [Rows(gate_z), Rows(down_z)], d_qkv, movers=[TokenMoves(outside(input_grad), split, True)]
    )
    output = output.reshape(tokens.shape)
    input_grad = input_grad.astype(F32).reshape(tokens.shape)
    up_rows, gate_rows, down_back = (t.astype(F32) for t in (up_rows, gate_rows, down_rows))
    ffn_gain_term = jnp.sum(up_rows * up_weight.astype(F32) + gate_rows * gate_weight.astype(F32), -1)
    up_back, gate_back = up_rows * g2, gate_rows * g2
    out_back, *qkv_rows = exchange(
        "weight_rows", [HeadGradients(qkv_z, [w.shape[1] for w in wqkv])],
        up_back, gate_back, down_back, input_grad, ffn_gain_term,
        movers=[HeadSums(d_out)],
    )
    out_back = unperm(out_back)
    qkv_rows = [t.astype(F32) for t in qkv_rows]
    attn_gain_term = sum(jnp.sum(w.astype(F32) * g, -1) for w, g in zip(wqkv, qkv_rows))
    q_back, k_back, v_back = (t * g1 for t in qkv_rows)

    return (
        output,
        input_grad,
        attn_gain_term,
        q_back,
        k_back,
        v_back,
        out_back,
        ffn_gain_term,
        gate_back,
        up_back,
        down_back,
    )


def solution(mesh):
    dp, seq = mesh.shape["dp"], mesh.shape["seq"]
    fine = Mesh(mesh.devices.reshape(dp // 2, 2, seq // 2, 2), EVERY)
    dp_axes, seq_axes = ("x", "core"), ("z", "y")
    tok = P(None, dp_axes, seq_axes, None)
    vec, mat = P(EVERY), P(EVERY, None)
    return jax.shard_map(
        shards,
        mesh=fine,
        in_specs=(tok, P(None, dp_axes, None), vec, mat, mat, mat, mat, vec, mat, mat, mat, tok),
        out_specs=(tok, tok, vec, mat, mat, mat, mat, vec, mat, mat, mat),
        check_vma=False,
    )
```
